128 devices in a mesh: dp: 8 (over x, z_hi), seq: 16 (over z_lo, y, core).
Axes of the slice: x: 4, y: 4, z: 4 (z_hi: 2, z_lo: 2; z = z_hi * 2 + z_lo), core: 2. Of those that a mesh axis runs over, the one named last changes fastest.
Arguments:
- tokens: bfloat16 [16384, 1024], P(('dp', 'seq')), may hold values from -6 to 6
- w_qkv: bfloat16 [1024, 2048], P('dp'), may hold values from -0.625 to 0.625
- w_out: bfloat16 [1024, 1024], P('dp'), may hold values from -0.375 to 0.375
- w_router: bfloat16 [1024, 16], P('dp'), may hold values from -0.09375 to 0.09375
- gain_attn: bfloat16 [1024], P('dp'), may hold values from 0.5 to 1.5
- gain_moe: bfloat16 [1024], P('dp'), may hold values from 0.5 to 1.5
- experts: bfloat16 [16, 1024, 1536], P('dp'), may hold values from -1.06066017 to 1.06066017
- routes: int32 [16384, 8], P(('dp', 'seq')), may hold values from 0 to 15, all different within a row
- cotangent: bfloat16 [16384, 1024], P(('dp', 'seq')), may hold values from -6 to 6
Outputs:
- layer_out: bfloat16 [16384, 1024], P(('dp', 'seq'))
- grad_tokens: float32 [16384, 1024], P(('dp', 'seq'))
- grad_qkv: float32 [1024, 2048], P('dp')
- grad_out: float32 [1024, 1024], P('dp')
- grad_router: float32 [1024, 16], P('dp')
- grad_gain_attn: float32 [1024], P('dp')
- grad_gain_moe: float32 [1024], P('dp')
- grad_experts: float32 [16, 1024, 1536], P('dp')
The draws below stay inside these ranges and needn't reach their ends.
Inputs may be any that keep to these rules, and one draw needn't show every extreme that they name: `routes`: each token names 8 different experts, and every expert is named by some token.
All inputs are finite; a program needn't handle non-finite values.
Results may differ from the reference program's by a relative error of at most 0.028.
Values may be sent and summed in bfloat16 or wider, within the bound.
A program may use at most 128 MiB of HBM per device.

```python
import jax
import jax.numpy as jnp
from jax import lax

D = 1024
QH = 16
KVH = 8
HD = 64
EXP_FF = 512
TOP = 8
EXPERTS = 16
TOK_DEV = 128
QD = 1024
KVD = 512
TOKENS = 16384
N_SEQ = 16


def draw_experts(key, part):
    key = jax.random.fold_in(key, 7)
    normal = jnp.clip(jax.random.normal(key, (EXPERTS, D, 3 * EXP_FF), jnp.float32), -6.0, 6.0)
    column = jnp.arange(3 * EXP_FF)
    scale = jnp.where(column < 2 * EXP_FF, D ** (-0.5), 4.0 * EXP_FF ** (-0.5)).astype(jnp.float32)
    return (normal * scale[None, None, :]).astype(jnp.bfloat16)


def shard_levels(own_key, extent, shards, smallest, top_value):
    level = 1.0
    for dim, blocks in shards:
        heights = jax.random.uniform(jax.random.fold_in(jax.random.fold_in(own_key, 6), dim), (blocks,), jnp.float32, smallest / len(shards), top_value / len(shards))
        level = level * jnp.repeat(jnp.exp(heights), extent[dim] // blocks).reshape((-1,) + (1,) * (len(extent) - 1 - dim))
    return level


def choose_distinct(stream_key, rows, amount, top, lift):
    ranking = jax.random.permutation(jax.random.fold_in(stream_key, 1), amount)
    favour = ranking
    for power in range(3):
        favour = favour * favour // amount
    favour = favour * lift // amount
    tickets = jax.random.randint(jax.random.fold_in(stream_key, 2), (rows, amount), 0, 4096) + favour
    holders = jax.random.permutation(jax.random.fold_in(stream_key, 3), rows)[jnp.arange(amount) % rows]
    tickets = jnp.where(jnp.arange(rows)[:, None] == holders[None, :], 1 << 14, tickets)
    priority = tickets * amount + jnp.arange(amount)
    return lax.top_k(priority.astype(jnp.int32), top)[1].astype(jnp.int32)


def gaussian(own_key, shape, spread, reach, split=(), kind=jnp.bfloat16):
    values = spread * jax.random.normal(own_key, shape, jnp.float32)
    if split:
        values = values * shard_levels(own_key, shape, split, -0.22, 0.18)
    return jnp.clip(values, -reach, reach).astype(kind)


def setup_inputs(seed: int = 0) -> dict:
    arg_keys = jax.random.split(jax.random.key(seed), 10)
    return {
        "tokens": gaussian(arg_keys[0], (TOKENS, D), 1.0, 6.0, ((0, 128),)),
        "w_qkv": gaussian(arg_keys[1], (D, QD + 2 * KVD), (D // 12) ** -0.5, 0.625, ((0, 8),)),
        "w_out": gaussian(arg_keys[2], (QD, D), (QD // 4) ** -0.5, 0.375, ((0, 8),)),
        "w_router": gaussian(arg_keys[3], (D, EXPERTS), (4 * D) ** -0.5, 0.09375, ((0, 8),)),
        "gain_attn": jnp.clip(1.0 + 0.1 * jax.random.normal(arg_keys[4], (D,), jnp.float32), 0.5, 1.5).astype(jnp.bfloat16),
        "gain_moe": jnp.clip(1.0 + 0.1 * jax.random.normal(arg_keys[5], (D,), jnp.float32), 0.5, 1.5).astype(jnp.bfloat16),
        "experts": draw_experts(jax.random.fold_in(arg_keys[9], 71), 0),
        "routes": choose_distinct(arg_keys[7], TOKENS, EXPERTS, TOP, 0),
        "cotangent": gaussian(arg_keys[8], (TOKENS, D), 1.0, 6.0, ((0, 128),)),
    }


EPSILON = 1e-06
MULT = 0.015625
THETA = 10000.0
NEGATIVE = -1e+30
HIGH = lax.Precision.HIGHEST

@jax.custom_vjp
def low(v):
    return lax.optimization_barrier(v.astype(jnp.bfloat16)).astype(jnp.float32)

@jax.custom_vjp
def low_back(v):
    return v

def low_keep(v):
    return (low(v), None)

def low_pass(kept, grad):
    return (grad,)

def back_keep(v):
    return (v, None)

def back_low(kept, grad):
    return (low(grad),)
low.defvjp(low_keep, low_pass)
low_back.defvjp(back_keep, back_low)

def norm(values, gain):
    return values * lax.rsqrt(lax.optimization_barrier(jnp.mean(values * values, -1, keepdims=True)) + EPSILON) * gain

def rope_tables(length):
    half = HD // 2
    freqs = THETA ** (-(jnp.arange(half, dtype=jnp.float32) * 2.0 / HD))
    angles = jnp.arange(length, dtype=jnp.float32)[:, None] * freqs[None, :]
    return (jnp.cos(angles)[:, None, :], jnp.sin(angles)[:, None, :])

def rotate(values, cosine, sine):
    half = HD // 2
    first, second = (values[..., :half], values[..., half:])
    return jnp.concatenate([first * cosine - second * sine, second * cosine + first * sine], -1)

def attention(query, keys, values):
    length = query.shape[0]
    block = min(512, length)
    blocks = length // block
    positions = jnp.arange(length, dtype=jnp.int32)

    def attend(item):
        query_block, start = item
        scores = low_back(MULT * jnp.einsum('qhd,khd->hqk', query_block, keys, precision=HIGH))
        allowed = positions[None, :] <= (start + jnp.arange(block, dtype=jnp.int32))[:, None]
        scores = jnp.where(allowed[None], scores, NEGATIVE)
        probs = low(jax.nn.softmax(scores, -1))
        return jnp.einsum('hqk,khd->qhd', probs, values, precision=HIGH)
    starts = jnp.arange(blocks, dtype=jnp.int32) * block
    mixed = lax.map(jax.checkpoint(attend), (query.reshape(blocks, block, QH, HD), starts))
    return mixed.reshape(length, QH, HD)

def layer(x, w_qkv, w_out, w_router, gain_attn, gain_moe, experts, chosen, cosine, sine):
    length = x.shape[0]
    group = QH // KVH
    normed_one = low(norm(x, gain_attn))
    projected = low_back(jnp.dot(normed_one, w_qkv, precision=HIGH))
    query = rotate(projected[:, :QD].reshape(length, QH, HD), cosine, sine)
    keys = jnp.repeat(rotate(projected[:, QD:QD + KVD].reshape(length, KVH, HD), cosine, sine), group, axis=1)
    values = jnp.repeat(projected[:, QD + KVD:].reshape(length, KVH, HD), group, axis=1)
    query = low(low_back(query))
    keys = low(low_back(keys))
    values = low(low_back(values))
    mixed = low(low_back(attention(query, keys, values))).reshape(length, QD)
    residual = x + low_back(jnp.dot(mixed, w_out, precision=HIGH))
    normed_two = low(norm(residual, gain_moe))
    logits = low_back(jnp.dot(normed_two, w_router, precision=HIGH))
    masked = jnp.where(chosen > 0, logits, NEGATIVE)
    expo = jnp.exp(masked - lax.optimization_barrier(jnp.max(masked, -1, keepdims=True))) * chosen
    gates = expo / lax.optimization_barrier(jnp.sum(expo, -1, keepdims=True))
    gate_up = low_back(jnp.einsum('td,edf->etf', normed_two, experts[:, :, :2 * EXP_FF], precision=HIGH))
    activated = low(jax.nn.silu(gate_up[..., :EXP_FF]) * gate_up[..., EXP_FF:])
    returned = low_back(jnp.einsum('etf,edf->etd', activated, experts[:, :, 2 * EXP_FF:], precision=HIGH))
    return residual + jnp.einsum('te,etd->td', gates, returned, precision=HIGH)

def reference(tokens, w_qkv, w_out, w_router, gain_attn, gain_moe, experts, routes, cotangent):
    length = TOK_DEV * N_SEQ
    seqs = tokens.shape[0] // length
    weights = (w_qkv.astype(jnp.float32), w_out.astype(jnp.float32), w_router.astype(jnp.float32), gain_attn.astype(jnp.float32), gain_moe.astype(jnp.float32), experts.astype(jnp.float32))
    cosine, sine = rope_tables(length)
    inputs = tokens.astype(jnp.float32).reshape(seqs, length, D)
    chosen_all = routes.reshape(seqs, length, TOP)
    upstream = cotangent.astype(jnp.float32).reshape(seqs, length, D)
    labels = jnp.arange(EXPERTS, dtype=jnp.int32)

    def one(totals, item):
        x, route, cot = item
        chosen = lax.optimization_barrier(jnp.sum((route[:, :, None] == labels[None, None, :]).astype(jnp.float32), 1))

        def apply(xin, wa, wb, wc, wd, we, wf):
            return layer(xin, wa, wb, wc, wd, we, wf, chosen, cosine, sine)
        out, pull = jax.vjp(apply, x, *weights)
        grads = pull(cot)
        totals = tuple((total + grad for total, grad in zip(totals, grads[1:])))
        return (totals, (out.astype(jnp.bfloat16), grads[0]))
    zeros = tuple((jnp.zeros_like(weight) for weight in weights))
    totals, (outs, input_grads) = lax.scan(one, zeros, (inputs, chosen_all, upstream))
    return (outs.reshape(-1, D), input_grads.reshape(-1, D), totals[0], totals[1], totals[2], totals[3], totals[4], totals[5])
```

```python
import functools

import jax
import jax.numpy as jnp
import numpy as np
from jax import lax
from jax.experimental import pallas as pl
from jax.experimental.pallas import tpu as pltpu
from jax.sharding import PartitionSpec as P

D = 1024
QH = 16
HD = 64
HALF = 32
FF = 512
N_DP = 8
N_SEQ = 16
ROWS = 128
LENGTH = 2048
QBLOCK = 512

EPSILON = 1e-06
MULT = 0.015625
THETA = 10000.0
NEGATIVE = -1e30
LOG2E = 1.4426950408889634

F32 = jnp.float32
BF16 = jnp.bfloat16
MESH = pl.DeviceIdType.MESH
VMEM = pl.BlockSpec(memory_space=pltpu.VMEM)
ANY = pl.BlockSpec(memory_space=pl.ANY)

DP_ORDER = (1, 2, 6, 3, 7, 4, 5)
CHIP_ORDER = (4, 1, 3, 5, 7, 2, 6)


def dot_nn(a, b):
    return lax.dot_general(a, b, (((1,), (0,)), ((), ())), preferred_element_type=F32)


def dot_nt(a, b):
    return lax.dot_general(a, b, (((1,), (1,)), ((), ())), preferred_element_type=F32)


def dot_tn(a, b):
    return lax.dot_general(a, b, (((0,), (0,)), ((), ())), preferred_element_type=F32)


def dp_peer(d, k):
    return lax.rem(lax.div(d, 2) + k // 2, 4) * 2 + lax.rem(lax.rem(d, 2) + k % 2, 2)


def dp_back(k):
    return 2 * ((4 - k // 2) % 4) + k % 2


def chip_peer(s, k):
    z, y, c = lax.div(s, 8), lax.rem(lax.div(s, 2), 4), lax.rem(s, 2)
    return lax.rem(z + k // 4, 2) * 8 + lax.rem(y + k % 4, 4) * 2 + c


def chip_back(k):
    return 4 * (k // 4) + (4 - k % 4) % 4


def seq_peer(s, k):
    base = chip_peer(s, k // 2)
    c = lax.rem(s, 2)
    return base if k % 2 == 0 else base + 1 - 2 * c


SEQ_ORDER = tuple(2 * c + o for c in (0,) + CHIP_ORDER for o in (0, 1) if 2 * c + o)


def seq_back(k):
    return 2 * chip_back(k // 2) + k % 2


def sibling(s):
    return s + 1 - 2 * lax.rem(s, 2)


def copy_to(src, dst, send, recv, device):
    copy = pltpu.make_async_remote_copy(
        src_ref=src,
        dst_ref=dst,
        send_sem=send,
        recv_sem=recv,
        device_id=device,
        device_id_type=MESH,
    )
    copy.start()
    return copy


def greet(devices):
    barrier = pltpu.get_barrier_semaphore()
    for device in devices:
        pl.semaphore_signal(barrier, inc=1, device_id=device, device_id_type=MESH)
    pl.semaphore_wait(barrier, len(devices))


def rows(start, size):
    return pl.ds(pl.multiple_of(start, size), size)


def front_kernel(
    x_ref, pack_ref, perm_ref, wout_ref, cot_ref, routes_ref, cos_ref, sin_ref,
    n1_ref, qkv_ref, lse_ref, o_ref, h_ref, n2_ref, gates_ref, packs_ref, wouts_ref, cots_ref, perms_ref,
    sel_a, sel_b, o_own, k_nat,
    pack_s, pack_r, a_s, a_r, b_s, b_r, n1_s, n1_r, f_s, f_r, w_s, w_r, c_s, c_r, p_s, p_r, o_s, o_r, l_s, l_r, own_s,
):
    d, s = lax.axis_index("dp"), lax.axis_index("seq")
    core = lax.rem(s, 2)
    mate = (d, sibling(s))
    greet(
        [(dp_peer(d, k), s) for k in DP_ORDER] + [(d, seq_peer(s, k)) for k in SEQ_ORDER]
    )
    lanes = rows(d * ROWS, ROWS)
    sent = []
    small = []
    head_rows = rows(s * ROWS, ROWS)
    mate_rows = rows(sibling(s) * ROWS + HD, HD)
    for k in DP_ORDER:
        to = (dp_peer(d, k), s)
        small.append(copy_to(pack_ref, packs_ref.at[:, lanes], pack_s.at[k], pack_r.at[k], to))
    picks = []
    for k in DP_ORDER:
        to = (dp_peer(d, k), s)
        picks.append(copy_to(perm_ref.at[head_rows], sel_a.at[:, lanes], a_s.at[k], a_r.at[k], to))
        picks.append(copy_to(perm_ref.at[mate_rows], sel_b.at[:, lanes], b_s.at[k], b_r.at[k], to))
    own_a = pltpu.make_async_copy(perm_ref.at[head_rows], sel_a.at[:, lanes], own_s.at[0])
    own_b = pltpu.make_async_copy(perm_ref.at[mate_rows], sel_b.at[:, lanes], own_s.at[1])
    own_a.start()
    own_b.start()
    packs_ref[:, lanes] = pack_ref[...]
    x = x_ref[...].astype(F32)
    r1 = lax.rsqrt(jnp.mean(x * x, -1, keepdims=True) + EPSILON)
    for copy in small:
        copy.wait_recv()
    mine = rows(s * ROWS, ROWS)
    n1_ref[mine] = (x * r1 * packs_ref[0:1, :]).astype(BF16)
    direct = {}
    first = copy_to(n1_ref.at[mine], n1_ref.at[mine], f_s.at[0], f_r.at[0], mate)
    for k in CHIP_ORDER:
        direct[k] = copy_to(
            n1_ref.at[mine], n1_ref.at[mine], n1_s.at[k], n1_r.at[k], (d, chip_peer(s, k))
        )
    half = rows(core * 512, 512)
    weights = []
    for k in DP_ORDER:
        weights.append(
            copy_to(
                wout_ref.at[:, half],
                wouts_ref.at[lanes, half],
                w_s.at[k],
                w_r.at[k],
                (dp_peer(d, k), s),
            )
        )
    own_w = pltpu.make_async_copy(wout_ref.at[:, half], wouts_ref.at[lanes, half], own_s.at[2])
    own_w.start()
    for copy in picks:
        copy.wait_recv()
    own_a.wait()
    own_b.wait()

    def project(chip):
        block = rows(chip * 256, 256)
        tokens = n1_ref[block]
        cosine = cos_ref[:, block]
        sine = sin_ref[:, block]

        def turn(v):
            a, b = v[:HALF], v[HALF:]
            return jnp.concatenate([a * cosine - b * sine, b * cosine + a * sine], 0)

        pa = dot_nt(sel_a[...], tokens)
        pb = dot_nt(sel_b[...], tokens)
        even = core == 0
        keys = jnp.where(even, pa[HD:], pb)
        values = jnp.where(even, pb, pa[HD:])
        qkv_ref[:, block] = jnp.concatenate([turn(pa[:HD]), turn(keys), values], 0).astype(BF16)

    forwards = [first]
    last = 0
    for k in CHIP_ORDER:
        direct[k].wait_recv()
        source = rows(chip_peer(s, chip_back(k)) * ROWS, ROWS)
        forwards.append(
            copy_to(n1_ref.at[source], n1_ref.at[source], f_s.at[k], f_r.at[k], mate)
        )
        forwards[-2].wait_recv()
        project(lax.div(chip_peer(s, chip_back(last)), 2))
        last = k
    forwards[-1].wait_recv()
    project(lax.div(chip_peer(s, chip_back(last)), 2))

    cots = []
    for k in DP_ORDER:
        cots.append(
            copy_to(cot_ref, cots_ref.at[lanes], c_s.at[k], c_r.at[k], (dp_peer(d, k), s))
        )
    own_c = pltpu.make_async_copy(cot_ref, cots_ref.at[lanes], own_s.at[3])
    own_c.start()
    side = rows(core * 1024, 1024)
    for k in DP_ORDER:
        weights.append(
            copy_to(
                perm_ref.at[side],
                perms_ref.at[side, lanes],
                p_s.at[k],
                p_r.at[k],
                (dp_peer(d, k), s),
            )
        )
    own_p = pltpu.make_async_copy(perm_ref.at[side], perms_ref.at[side, lanes], own_s.at[4])
    own_p.start()

    k_nat[...] = jnp.transpose(qkv_ref[HD : 2 * HD].astype(F32)).astype(BF16)
    outs = []
    for block in range(LENGTH // QBLOCK):
        begin, end = block * QBLOCK, (block + 1) * QBLOCK
        query = qkv_ref[0:HD, begin:end]
        scores = dot_nn(k_nat[0:end], query)
        low = scores[begin:]
        key = lax.broadcasted_iota(jnp.int32, low.shape, 0)
        pos = lax.broadcasted_iota(jnp.int32, low.shape, 1)
        low = jnp.where(key <= pos, low, NEGATIVE)
        if block:
            scores = jnp.concatenate([scores[:begin], low], 0)
        else:
            scores = low
        top = jnp.max(scores, 0, keepdims=True)
        expo = jnp.exp2((scores - top) * (MULT * LOG2E))
        total = jnp.sum(expo, 0, keepdims=True)
        probs = (expo * (1.0 / total)).astype(BF16)
        lse_ref[:, begin:end] = top * MULT + jnp.log(total)
        o_own[:, begin:end] = dot_nn(qkv_ref[2 * HD :, 0:end], probs).astype(BF16)
    place = rows(s * HD, HD)
    for k in SEQ_ORDER:
        to = seq_peer(s, k)
        outs.append(
            copy_to(
                o_own.at[:, rows(to * ROWS, ROWS)], o_ref.at[place], o_s.at[k], o_r.at[k], (d, to)
            )
        )
    o_ref[place] = o_own[:, mine]
    for copy in weights[:7]:
        copy.wait_recv()
    own_w.wait()
    share = copy_to(wouts_ref.at[:, half], wouts_ref.at[:, half], l_s.at[0], l_r.at[0], mate)
    for copy in outs:
        copy.wait_recv()
    share.wait_recv()
    mixed = jnp.transpose(o_ref[...].astype(F32)).astype(BF16)
    h = x + dot_nn(mixed, wouts_ref[...])
    h_ref[...] = h
    r2 = lax.rsqrt(jnp.mean(h * h, -1, keepdims=True) + EPSILON)
    n2 = (h * r2 * packs_ref[1:2, :]).astype(BF16)
    n2_ref[...] = n2
    router = jnp.concatenate(
        [packs_ref[8:24, :], jnp.zeros((ROWS - 16, D), F32)], 0
    ).astype(BF16)
    logits = dot_nt(n2, router)
    label = lax.broadcasted_iota(jnp.int32, (ROWS, ROWS), 1)
    chosen = jnp.zeros((ROWS, ROWS), jnp.bool_)
    for j in range(8):
        chosen = chosen | (routes_ref[:, j : j + 1] == label)
    masked = jnp.where(chosen, logits, NEGATIVE)
    expo = jnp.where(chosen, jnp.exp(masked - jnp.max(masked, -1, keepdims=True)), 0.0)
    gates_ref[...] = expo / jnp.sum(expo, -1, keepdims=True)

    for copy in weights[7:]:
        copy.wait_recv()
    own_p.wait()
    share_p = copy_to(perms_ref.at[side], perms_ref.at[side], l_s.at[1], l_r.at[1], mate)
    for copy in cots:
        copy.wait_recv()
    own_c.wait()
    share_p.wait_recv()
    for copy in small + picks + list(direct.values()) + forwards + weights + cots + outs:
        copy.wait_send()
    share.wait_send()
    share_p.wait_send()


def experts_kernel(
    n2_ref, gates_ref, cots_ref, exp_ref,
    dn2_ref, dgate_ref, mix_ref, grad_ref,
    n2s, gs, part, dgp, recv, recvg, acts, dgus, dys,
    n_s, n_r, g_s, g_r, d_s, d_r, e_s, e_r,
):
    d, s = lax.axis_index("dp"), lax.axis_index("seq")
    greet([(dp_peer(d, k), s) for k in DP_ORDER])
    mine = rows(d * ROWS, ROWS)
    gathers = {}
    for k in DP_ORDER:
        to = (dp_peer(d, k), s)
        gathers[k] = (
            copy_to(gates_ref, gs.at[mine], g_s.at[k], g_r.at[k], to),
            copy_to(n2_ref, n2s.at[mine], n_s.at[k], n_r.at[k], to),
        )
    n2s[mine] = n2_ref[...]
    gs[mine] = gates_ref[...]
    x = lax.div(d, 2)
    backs = []
    for turn in (0, 1, 3, 2):
        for z in (0, 1):
            k = 2 * turn + z
            if k:
                for copy in gathers[dp_back(k)]:
                    copy.wait_recv()
        place = rows(lax.rem(x + turn, 4) * 256, 256)
        tokens = n2s[place]
        cot = cots_ref[place].astype(F32)
        gates = gs[place]
        lane = lax.broadcasted_iota(jnp.int32, gates.shape, 1)
        dn2 = jnp.zeros((256, D), F32)
        mix = jnp.zeros((256, D), F32)
        dgate = jnp.zeros(gates.shape, F32)
        for e in range(2):
            up_w = exp_ref[e, :, 0 : 2 * FF]
            down_w = exp_ref[e, :, 2 * FF :]
            here = lane == 2 * d + e
            gate = jnp.sum(jnp.where(here, gates, 0.0), -1, keepdims=True)
            gu = dot_nn(tokens, up_w)
            g, u = gu[:, :FF], gu[:, FF:]
            sigmoid = 1.0 / (1.0 + jnp.exp(-g))
            silu = g * sigmoid
            act = (silu * u).astype(BF16)
            acts[place, e * FF : (e + 1) * FF] = act
            y = dot_nt(act, down_w)
            dgate = jnp.where(here, jnp.sum(cot * y, -1, keepdims=True), dgate)
            mix = mix + gate * y
            dy = (gate * cot).astype(BF16)
            dys[place, e * D : (e + 1) * D] = dy
            dact = dot_nn(dy, down_w)
            dg = dact * u * (sigmoid * (1.0 + g * (1.0 - sigmoid)))
            du = dact * silu
            dgu = jnp.concatenate([dg, du], 1).astype(BF16)
            dgus[place, e * D : (e + 1) * D] = dgu
            dn2 = dn2 + dot_nt(dgu, up_w)
        mix_ref[place] = mix.astype(BF16)
        part[place] = dn2.astype(BF16)
        dgp[place] = dgate
        for z in (0, 1):
            k = 2 * turn + z
            if k:
                to = dp_peer(d, k)
                block = rows(to * ROWS, ROWS)
                backs.append(
                    copy_to(part.at[block], recv.at[k], d_s.at[k], d_r.at[k], (to, s))
                )
                backs.append(
                    copy_to(dgp.at[block], recvg.at[k], e_s.at[k], e_r.at[k], (to, s))
                )
    for e in range(2):
        grad_ref[e, :, 0 : 2 * FF] = dot_tn(n2s[...], dgus[:, e * D : (e + 1) * D]).astype(BF16)
        grad_ref[e, :, 2 * FF :] = dot_tn(
            dys[:, e * D : (e + 1) * D], acts[:, e * FF : (e + 1) * FF]
        ).astype(BF16)
    for copy in backs:
        copy.wait_recv()
    total = part[mine].astype(F32)
    totalg = dgp[mine]
    for k in range(1, 8):
        total = total + recv[k].astype(F32)
        totalg = totalg + recvg[k]
    dn2_ref[...] = total
    dgate_ref[...] = totalg
    for pair in gathers.values():
        for copy in pair:
            copy.wait_send()
    for copy in backs:
        copy.wait_send()


def back_kernel(
    dn2_ref, dgate_ref, gates_ref, mix_ref, x_ref, h_ref, n2_ref, cot_ref, packs_ref, wouts_ref, perms_ref,
    n1_ref, qkv_ref, lse_ref, o_ref, cos_ref, sin_ref,
    out_ref, gx_ref, gout_ref, fin_ref,
    recv_m, gop, recv_g, gosum, gopart, dot_own, dot_all, k_nat, v_nat, dq_acc, dk_acc, dv_acc, kv_own, kv_mate,
    dp_own, dp_tok, finp, recv_f, finsum,
    m_s, m_r, go_s, go_r, gp_s, gp_r, gq_s, gq_r, do_s, do_r, kv_s, kv_r, dp_s, dp_r, f_s, f_r, t_s, t_r,
):
    d, s = lax.axis_index("dp"), lax.axis_index("seq")
    core = lax.rem(s, 2)
    greet(
        [(dp_peer(d, k), s) for k in DP_ORDER] + [(d, seq_peer(s, k)) for k in SEQ_ORDER]
    )
    here = rows(d * ROWS, ROWS)
    mine = rows(s * ROWS, ROWS)
    head = rows(s * HD, HD)
    gates = gates_ref[...]
    dgate = dgate_ref[...]
    inner = jnp.sum(gates * dgate, -1, keepdims=True)
    dlogits = (gates * (dgate - inner)).astype(BF16)
    router = jnp.concatenate(
        [packs_ref[8:24, :], jnp.zeros((ROWS - 16, D), F32)], 0
    ).astype(BF16)
    dn2 = dn2_ref[...] + dot_nn(dlogits, router)
    h = h_ref[...]
    r2 = lax.rsqrt(jnp.mean(h * h, -1, keepdims=True) + EPSILON)
    c = dn2 * packs_ref[1:2, :]
    dh = cot_ref[...].astype(F32) + r2 * c - h * (
        r2 * r2 * r2 * jnp.mean(c * h, -1, keepdims=True)
    )
    da = dh.astype(BF16)
    dot_own[...] = dot_nt(wouts_ref[...], da).astype(BF16)
    moves = []
    for k in SEQ_ORDER:
        to = seq_peer(s, k)
        moves.append(
            copy_to(
                dot_own.at[rows(to * HD, HD)], dot_all.at[:, mine], do_s.at[k], do_r.at[k], (d, to)
            )
        )
    dot_all[:, mine] = dot_own[head]
    gop[...] = dot_nn(o_ref[...], da).astype(BF16)
    gos = []
    mixes = []
    for k in DP_ORDER:
        to = dp_peer(d, k)
        block = rows(to * ROWS, ROWS)
        gos.append(copy_to(gop.at[block], recv_g.at[k], go_s.at[k], go_r.at[k], (to, s)))
    for k in DP_ORDER:
        to = dp_peer(d, k)
        block = rows(to * ROWS, ROWS)
        mixes.append(copy_to(mix_ref.at[block], recv_m.at[k], m_s.at[k], m_r.at[k], (to, s)))
    finp[128:, :] = jnp.zeros((32, D), F32)
    finp[128:144, :] = dot_tn(dlogits, n2_ref[...])[0:16]
    finp[144:145, :] = jnp.sum(dn2 * h * r2, 0, keepdims=True)
    k_nat[...] = jnp.transpose(qkv_ref[HD : 2 * HD].astype(F32)).astype(BF16)
    v_nat[...] = jnp.transpose(qkv_ref[2 * HD :].astype(F32)).astype(BF16)
    for copy in moves:
        copy.wait_recv()
    blocks = LENGTH // QBLOCK
    for block in reversed(range(blocks)):
        begin, end = block * QBLOCK, (block + 1) * QBLOCK
        query = qkv_ref[0:HD, begin:end]
        grad = dot_all[:, begin:end]
        scores = dot_nn(k_nat[0:end], query)
        probs = jnp.exp2(scores * (MULT * LOG2E) - lse_ref[:, begin:end] * LOG2E)
        low = probs[begin:]
        key = lax.broadcasted_iota(jnp.int32, low.shape, 0)
        pos = lax.broadcasted_iota(jnp.int32, low.shape, 1)
        low = jnp.where(key <= pos, low, 0.0)
        if block:
            probs = jnp.concatenate([probs[:begin], low], 0)
        else:
            probs = low
        pgrad = dot_nn(v_nat[0:end], grad)
        inner = jnp.sum(probs * pgrad, 0, keepdims=True)
        ds = (probs * (pgrad - inner)).astype(BF16)
        dv = dot_nt(grad, probs.astype(BF16))
        dk = dot_nt(query, ds)
        if block == blocks - 1:
            dv_acc[...] = dv
            dk_acc[...] = dk
        else:
            dv_acc[:, 0:end] += dv
            dk_acc[:, 0:end] += dk
        dq_acc[:, begin:end] = dot_nn(qkv_ref[HD : 2 * HD, 0:end], ds)
    kv_own[0:HD] = (dk_acc[...] * MULT).astype(BF16)
    kv_own[HD:] = dv_acc[...].astype(BF16)
    mate = (d, sibling(s))
    swap = copy_to(kv_own, kv_mate, kv_s.at[0], kv_r.at[0], mate)
    cosine = cos_ref[...]
    sine = sin_ref[...]

    def unturn(v):
        a, b = v[:HALF], v[HALF:]
        return jnp.concatenate([a * cosine + b * sine, b * cosine - a * sine], 0)

    dp_own[0:HD] = unturn((dq_acc[...] * MULT).astype(BF16).astype(F32)).astype(BF16)
    swap.wait_recv()
    both = kv_own[...].astype(F32) + kv_mate[...].astype(F32)
    dp_own[HD:] = jnp.where(core == 0, unturn(both[:HD]), both[HD:]).astype(BF16)
    shares = []
    slot = rows(s * ROWS, ROWS)
    for k in SEQ_ORDER:
        to = seq_peer(s, k)
        shares.append(
            copy_to(
                dp_own.at[:, rows(to * ROWS, ROWS)],
                dp_tok.at[slot],
                dp_s.at[k],
                dp_r.at[k],
                (d, to),
            )
        )
    dp_tok[slot] = dp_own[:, mine]
    finp[0:128, :] = dot_nn(dp_own[...], n1_ref[...])

    for copy in gos:
        copy.wait_recv()
    total = gop[here].astype(F32)
    for k in range(1, 8):
        total = total + recv_g[k].astype(F32)
    gosum[...] = total
    pieces = []
    for k in SEQ_ORDER:
        to = seq_peer(s, k)
        pieces.append(
            copy_to(gosum.at[rows(to * 8, 8)], gopart.at[k], gp_s.at[k], gp_r.at[k], (d, to))
        )
    for copy in shares:
        copy.wait_recv()
    dn1 = dot_tn(dp_tok[...], perms_ref[...])
    x = x_ref[...].astype(F32)
    r1 = lax.rsqrt(jnp.mean(x * x, -1, keepdims=True) + EPSILON)
    c = dn1 * packs_ref[0:1, :]
    gx_ref[...] = dh + r1 * c - x * (r1 * r1 * r1 * jnp.mean(c * x, -1, keepdims=True))
    finp[145:146, :] = jnp.sum(dn1 * x * r1, 0, keepdims=True)
    finals = []
    for k in DP_ORDER:
        to = dp_peer(d, k)
        finals.append(
            copy_to(
                finp.at[:, rows(to * ROWS, ROWS)], recv_f.at[k], f_s.at[k], f_r.at[k], (to, s)
            )
        )
    for copy in pieces:
        copy.wait_recv()
    slab = rows(s * 8, 8)
    total = gosum[slab]
    for k in range(1, 16):
        total = total + gopart[k]
    gout_ref[slab] = total
    wholes = []
    for k in SEQ_ORDER:
        wholes.append(
            copy_to(
                gout_ref.at[slab], gout_ref.at[slab], gq_s.at[k], gq_r.at[k], (d, seq_peer(s, k))
            )
        )
    for copy in finals:
        copy.wait_recv()
    total = finp[:, here]
    for k in range(1, 8):
        total = total + recv_f[k]
    finsum[...] = total.astype(BF16)
    tails = []
    for k in SEQ_ORDER:
        tails.append(
            copy_to(finsum, fin_ref.at[s], t_s.at[k], t_r.at[k], (d, seq_peer(s, k)))
        )
    fin_ref[s] = finsum[...]
    for copy in mixes:
        copy.wait_recv()
    total = h + mix_ref[here].astype(F32)
    for k in range(1, 8):
        total = total + recv_m[k].astype(F32)
    out_ref[...] = total.astype(BF16)
    for copy in wholes + tails:
        copy.wait_recv()
    for copy in moves + gos + mixes + [swap] + shares + pieces + finals + wholes + tails:
        copy.wait_send()


def sems(count):
    return pltpu.SemaphoreType.DMA((count,))


def params(identity):
    return pltpu.CompilerParams(
        collective_id=identity, has_side_effects=True, vmem_limit_bytes=60 << 20
    )


def angle_tables():
    freqs = np.float32(THETA) ** (
        -(np.arange(HALF, dtype=np.float32) * np.float32(2.0) / np.float32(HD))
    )
    angles = freqs.astype(np.float32)[:, None] * np.arange(LENGTH, dtype=np.float32)[None, :]
    angles = angles.astype(np.float64)
    return np.cos(angles).astype(np.float32), np.sin(angles).astype(np.float32)


def sds(shape, dtype):
    return jax.ShapeDtypeStruct(shape, dtype)


def shards(tokens, w_qkv, w_out, w_router, gain_attn, gain_moe, experts, routes, cotangent):
    cosine, sine = angle_tables()
    cosine, sine = jnp.asarray(cosine), jnp.asarray(sine)
    pack = jnp.concatenate(
        [
            gain_attn.astype(F32)[None],
            gain_moe.astype(F32)[None],
            jnp.zeros((6, ROWS), F32),
            w_router.astype(F32).T,
        ],
        0,
    )
    query_w = w_qkv[:, :D].reshape(ROWS, QH, HD)
    keys_w = w_qkv[:, D:].reshape(ROWS, 2, QH // 2, HD).transpose(0, 2, 1, 3).reshape(ROWS, QH, HD)
    perm = jnp.concatenate([query_w, keys_w], -1).reshape(ROWS, 2 * D).T

    n1, qkv, lse, o_tok, h, n2, gates, packs, wouts, cots, perms = pl.pallas_call(
        front_kernel,
        out_shape=(
            sds((LENGTH, D), BF16),
            sds((3 * HD, LENGTH), BF16),
            sds((1, LENGTH), F32),
            sds((D, ROWS), BF16),
            sds((ROWS, D), F32),
            sds((ROWS, D), BF16),
            sds((ROWS, ROWS), F32),
            sds((24, D), F32),
            sds((D, D), BF16),
            sds((D, D), BF16),
            sds((2 * D, D), BF16),
        ),
        in_specs=[VMEM, VMEM, VMEM, VMEM, VMEM, VMEM, VMEM, VMEM],
        out_specs=(VMEM,) * 9 + (ANY, ANY),
        scratch_shapes=[
            pltpu.VMEM((ROWS, D), BF16),
            pltpu.VMEM((HD, D), BF16),
            pltpu.VMEM((HD, LENGTH), BF16),
            pltpu.VMEM((LENGTH, HD), BF16),
        ]
        + [sems(8)] * 16
        + [sems(16)] * 2
        + [sems(2)] * 2
        + [sems(5)],
        compiler_params=params(1),
        name="front",
    )(tokens, pack, perm, w_out, cotangent, routes, cosine, sine)

    dn2, dgate, mix, expert_grads = pl.pallas_call(
        experts_kernel,
        out_shape=(
            sds((ROWS, D), F32),
            sds((ROWS, ROWS), F32),
            sds((D, D), BF16),
            sds((2, D, 3 * FF), BF16),
        ),
        in_specs=[VMEM] * 4,
        out_specs=(VMEM,) * 4,
        scratch_shapes=[
            pltpu.VMEM((D, D), BF16),
            pltpu.VMEM((D, ROWS), F32),
            pltpu.VMEM((D, D), BF16),
            pltpu.VMEM((D, ROWS), F32),
            pltpu.VMEM((8, ROWS, D), BF16),
            pltpu.VMEM((8, ROWS, ROWS), F32),
            pltpu.VMEM((D, 2 * FF), BF16),
            pltpu.VMEM((D, 2 * D), BF16),
            pltpu.VMEM((D, 2 * D), BF16),
        ]
        + [sems(8)] * 8,
        compiler_params=params(2),
        name="experts",
    )(n2, gates, cots, experts)

    grad_experts = lax.psum(expert_grads, "seq").astype(F32)

    out, grad_x, grad_out, fin = pl.pallas_call(
        back_kernel,
        out_shape=(
            sds((ROWS, D), BF16),
            sds((ROWS, D), F32),
            sds((ROWS, D), F32),
            sds((N_SEQ, 160, ROWS), BF16),
        ),
        in_specs=[VMEM] * 17,
        out_specs=(VMEM,) * 4,
        scratch_shapes=[
            pltpu.VMEM((8, ROWS, D), BF16),
            pltpu.VMEM((D, D), BF16),
            pltpu.VMEM((8, ROWS, D), BF16),
            pltpu.VMEM((ROWS, D), F32),
            pltpu.VMEM((16, 8, D), F32),
            pltpu.VMEM((D, ROWS), BF16),
            pltpu.VMEM((HD, LENGTH), BF16),
            pltpu.VMEM((LENGTH, HD), BF16),
            pltpu.VMEM((LENGTH, HD), BF16),
            pltpu.VMEM((HD, LENGTH), F32),
            pltpu.VMEM((HD, LENGTH), F32),
            pltpu.VMEM((HD, LENGTH), F32),
            pltpu.VMEM((ROWS, LENGTH), BF16),
            pltpu.VMEM((ROWS, LENGTH), BF16),
            pltpu.VMEM((ROWS, LENGTH), BF16),
            pltpu.VMEM((2 * D, ROWS), BF16),
            pltpu.VMEM((160, D), F32),
            pltpu.VMEM((8, 160, ROWS), F32),
            pltpu.VMEM((160, ROWS), BF16),
        ]
        + [sems(8)] * 4
        + [sems(16)] * 6
        + [sems(1)] * 2
        + [sems(16)] * 2
        + [sems(8)] * 2
        + [sems(16)] * 2,
        compiler_params=params(3),
        name="back",
    )(
        dn2, dgate, gates, mix, tokens, h, n2, cotangent, packs, wouts, perms,
        n1, qkv, lse, o_tok, cosine, sine,
    )

    grads = fin[:, :128].astype(F32)
    query_g = grads[:, :HD].reshape(D, ROWS).T
    keys_g = (
        grads[:, HD:].reshape(QH // 2, 2, HD, ROWS).transpose(3, 1, 0, 2).reshape(ROWS, D)
    )
    grad_qkv = jnp.concatenate([query_g, keys_g], -1)
    small = jnp.sum(fin[:, 128:].astype(F32), 0)
    return (
        out,
        grad_x,
        grad_qkv,
        grad_out,
        small[:16].T,
        small[17],
        small[16],
        grad_experts,
    )


def solution(mesh):
    placed = (
        P(("dp", "seq"), None),
        P("dp", None),
        P("dp", None),
        P("dp", None),
        P("dp"),
        P("dp"),
        P("dp", None, None),
        P(("dp", "seq"), None),
        P(("dp", "seq"), None),
    )
    return jax.shard_map(
        shards,
        mesh=mesh,
        in_specs=placed,
        out_specs=(
            P(("dp", "seq"), None),
            P(("dp", "seq"), None),
            P("dp", None),
            P("dp", None),
            P("dp", None),
            P("dp"),
            P("dp"),
            P("dp", None, None),
        ),
        check_vma=False,
    )
```

```python
import functools

import jax
import jax.numpy as jnp
import numpy as np
from jax import lax
from jax.experimental import pallas as pl
from jax.experimental.pallas import tpu as pltpu
from jax.sharding import PartitionSpec as P

D = 1024
QH = 16
HD = 64
HALF = 32
FF = 512
N_DP = 8
N_SEQ = 16
ROWS = 128
LENGTH = 2048
QBLOCK = 512

EPSILON = 1e-06
MULT = 0.015625
THETA = 10000.0
NEGATIVE = -1e30
LOG2E = 1.4426950408889634

F32 = jnp.float32
BF16 = jnp.bfloat16
MESH = pl.DeviceIdType.MESH
VMEM = pl.BlockSpec(memory_space=pltpu.VMEM)
ANY = pl.BlockSpec(memory_space=pl.ANY)

DP_ORDER = (1, 2, 6, 3, 7, 4, 5)
CHIP_ORDER = (4, 1, 3, 5, 7, 2, 6)


def dot_nn(a, b):
    return lax.dot_general(a, b, (((1,), (0,)), ((), ())), preferred_element_type=F32)


def dot_nt(a, b):
    return lax.dot_general(a, b, (((1,), (1,)), ((), ())), preferred_element_type=F32)


def dot_tn(a, b):
    return lax.dot_general(a, b, (((0,), (0,)), ((), ())), preferred_element_type=F32)


def dp_peer(d, k):
    return lax.rem(lax.div(d, 2) + k // 2, 4) * 2 + lax.rem(lax.rem(d, 2) + k % 2, 2)


def dp_back(k):
    return 2 * ((4 - k // 2) % 4) + k % 2


def chip_peer(s, k):
    z, y, c = lax.div(s, 8), lax.rem(lax.div(s, 2), 4), lax.rem(s, 2)
    return lax.rem(z + k // 4, 2) * 8 + lax.rem(y + k % 4, 4) * 2 + c


def chip_back(k):
    return 4 * (k // 4) + (4 - k % 4) % 4


def seq_peer(s, k):
    base = chip_peer(s, k // 2)
    c = lax.rem(s, 2)
    return base if k % 2 == 0 else base + 1 - 2 * c


SEQ_ORDER = tuple(2 * c + o for c in (0,) + CHIP_ORDER for o in (0, 1) if 2 * c + o)


def seq_back(k):
    return 2 * chip_back(k // 2) + k % 2


def sibling(s):
    return s + 1 - 2 * lax.rem(s, 2)


def copy_to(src, dst, send, recv, device):
    copy = pltpu.make_async_remote_copy(
        src_ref=src,
        dst_ref=dst,
        send_sem=send,
        recv_sem=recv,
        device_id=device,
        device_id_type=MESH,
    )
    copy.start()
    return copy


def greet(devices):
    barrier = pltpu.get_barrier_semaphore()
    for device in devices:
        pl.semaphore_signal(barrier, inc=1, device_id=device, device_id_type=MESH)
    pl.semaphore_wait(barrier, len(devices))


def rows(start, size):
    return pl.ds(pl.multiple_of(start, size), size)


def front_kernel(
    x_ref, pack_ref, perm_ref, wout_ref, cot_ref, routes_ref, cos_ref, sin_ref,
    n1_ref, qkv_ref, lse_ref, o_ref, h_ref, n2_ref, gates_ref, gates_t_ref, packs_ref, wouts_ref, cots_ref, perms_ref,
    sel_a, sel_b, o_own, k_nat,
    pack_s, pack_r, a_s, a_r, b_s, b_r, n1_s, n1_r, f_s, f_r, w_s, w_r, c_s, c_r, p_s, p_r, o_s, o_r, l_s, l_r, own_s,
):
    d, s = lax.axis_index("dp"), lax.axis_index("seq")
    core = lax.rem(s, 2)
    mate = (d, sibling(s))
    greet(
        [(dp_peer(d, k), s) for k in DP_ORDER] + [(d, seq_peer(s, k)) for k in SEQ_ORDER]
    )
    lanes = rows(d * ROWS, ROWS)
    small = []
    head_rows = rows(s * ROWS, ROWS)
    mate_rows = rows(sibling(s) * ROWS + HD, HD)
    for k in DP_ORDER:
        to = (dp_peer(d, k), s)
        small.append(copy_to(pack_ref, packs_ref.at[:, lanes], pack_s.at[k], pack_r.at[k], to))
    picks = []
    for k in DP_ORDER:
        to = (dp_peer(d, k), s)
        picks.append(copy_to(perm_ref.at[head_rows], sel_a.at[:, lanes], a_s.at[k], a_r.at[k], to))
        picks.append(copy_to(perm_ref.at[mate_rows], sel_b.at[:, lanes], b_s.at[k], b_r.at[k], to))
    own_a = pltpu.make_async_copy(perm_ref.at[head_rows], sel_a.at[:, lanes], own_s.at[0])
    own_b = pltpu.make_async_copy(perm_ref.at[mate_rows], sel_b.at[:, lanes], own_s.at[1])
    own_a.start()
    own_b.start()
    packs_ref[:, lanes] = pack_ref[...]
    x = x_ref[...].astype(F32)
    r1 = lax.rsqrt(jnp.mean(x * x, -1, keepdims=True) + EPSILON)
    for copy in small:
        copy.wait_recv()
    mine = rows(s * ROWS, ROWS)
    n1_ref[mine] = (x * r1 * packs_ref[0:1, :]).astype(BF16)
    direct = {}
    forwards = {0: copy_to(n1_ref.at[mine], n1_ref.at[mine], f_s.at[0], f_r.at[0], mate)}
    for k in (4, 1, 3, 2):
        direct[k] = copy_to(
            n1_ref.at[mine], n1_ref.at[mine], n1_s.at[k], n1_r.at[k], (d, chip_peer(s, k))
        )
    half = rows(core * 512, 512)
    side = rows(core * 1024, 1024)
    other = rows(dp_peer(d, 1) * ROWS, ROWS)

    def spread(source, place, send, recv):
        return {
            k: copy_to(source, place(lanes), send.at[k], recv.at[k], (dp_peer(d, k), s))
            for k in (1, 2, 6, 4)
        }

    def pass_on(copies, place, send, recv):
        copies[1].wait_recv()
        for k in (3, 7, 5):
            copies[k] = copy_to(
                place(other), place(other), send.at[k], recv.at[k], (dp_peer(d, k - 1), s)
            )

    def keep(source, place, k):
        copy = pltpu.make_async_copy(source, place(lanes), own_s.at[k])
        copy.start()
        return copy

    out_source, out_place = wout_ref.at[:, half], lambda at: wouts_ref.at[at, half]
    cot_place = lambda at: cots_ref.at[at]
    perm_source, perm_place = perm_ref.at[side], lambda at: perms_ref.at[side, at]
    outs_w = spread(out_source, out_place, w_s, w_r)
    own_w = keep(out_source, out_place, 2)
    direct[4].wait_recv()
    partner = rows(chip_peer(s, 4) * ROWS, ROWS)
    forwards[4] = copy_to(n1_ref.at[partner], n1_ref.at[partner], f_s.at[4], f_r.at[4], mate)
    for k in (5, 7, 6):
        direct[k] = copy_to(
            n1_ref.at[partner],
            n1_ref.at[partner],
            n1_s.at[k],
            n1_r.at[k],
            (d, chip_peer(s, k - 4)),
        )
    cots = spread(cot_ref, cot_place, c_s, c_r)
    own_c = keep(cot_ref, cot_place, 3)
    pass_on(outs_w, out_place, w_s, w_r)
    for copy in picks:
        copy.wait_recv()
    own_a.wait()
    own_b.wait()

    def project(chip):
        block = rows(chip * 256, 256)
        tokens = n1_ref[block]
        cosine = cos_ref[:, block]
        sine = sin_ref[:, block]

        def turn(v):
            a, b = v[:HALF], v[HALF:]
            return jnp.concatenate([a * cosine - b * sine, b * cosine + a * sine], 0)

        pa = dot_nt(sel_a[...], tokens)
        pb = dot_nt(sel_b[...], tokens)
        even = core == 0
        keys = jnp.where(even, pa[HD:], pb)
        values = jnp.where(even, pb, pa[HD:])
        qkv_ref[:, block] = jnp.concatenate([turn(pa[:HD]), turn(keys), values], 0).astype(BF16)

    last = 0
    for k in (4, 1, 3, 2, 5, 7, 6):
        if k != 4:
            direct[k].wait_recv()
            source = rows(chip_peer(s, chip_back(k)) * ROWS, ROWS)
            forwards[k] = copy_to(
                n1_ref.at[source], n1_ref.at[source], f_s.at[k], f_r.at[k], mate
            )
        forwards[last].wait_recv()
        project(lax.div(chip_peer(s, chip_back(last)), 2))
        last = k
        if k == 3:
            pass_on(cots, cot_place, c_s, c_r)
            sides = spread(perm_source, perm_place, p_s, p_r)
            own_p = keep(perm_source, perm_place, 4)
    forwards[last].wait_recv()
    project(lax.div(chip_peer(s, chip_back(last)), 2))

    k_nat[...] = jnp.transpose(qkv_ref[HD : 2 * HD].astype(F32)).astype(BF16)
    outs = []
    for block in range(LENGTH // QBLOCK):
        begin, end = block * QBLOCK, (block + 1) * QBLOCK
        query = qkv_ref[0:HD, begin:end]
        scores = dot_nn(k_nat[0:end], query)
        low = scores[begin:]
        key = lax.broadcasted_iota(jnp.int32, low.shape, 0)
        pos = lax.broadcasted_iota(jnp.int32, low.shape, 1)
        low = jnp.where(key <= pos, low, NEGATIVE)
        if block:
            scores = jnp.concatenate([scores[:begin], low], 0)
        else:
            scores = low
        top = jnp.max(scores, 0, keepdims=True)
        expo = jnp.exp2((scores - top) * (MULT * LOG2E))
        total = jnp.sum(expo, 0, keepdims=True)
        probs = (expo * (1.0 / total)).astype(BF16)
        lse_ref[:, begin:end] = top * MULT + jnp.log(total)
        o_own[:, begin:end] = dot_nn(qkv_ref[2 * HD :, 0:end], probs).astype(BF16)
    place = rows(s * HD, HD)
    for k in SEQ_ORDER:
        to = seq_peer(s, k)
        outs.append(
            copy_to(
                o_own.at[:, rows(to * ROWS, ROWS)], o_ref.at[place], o_s.at[k], o_r.at[k], (d, to)
            )
        )
    o_ref[place] = o_own[:, mine]
    pass_on(sides, perm_place, p_s, p_r)
    for k in (2, 6, 4, 3, 7, 5):
        outs_w[k].wait_recv()
    own_w.wait()
    share = copy_to(wouts_ref.at[:, half], wouts_ref.at[:, half], l_s.at[0], l_r.at[0], mate)
    for copy in outs:
        copy.wait_recv()
    share.wait_recv()
    mixed = jnp.transpose(o_ref[...].astype(F32)).astype(BF16)
    h = x + dot_nn(mixed, wouts_ref[...])
    h_ref[...] = h
    r2 = lax.rsqrt(jnp.mean(h * h, -1, keepdims=True) + EPSILON)
    n2 = (h * r2 * packs_ref[1:2, :]).astype(BF16)
    n2_ref[...] = n2
    router = jnp.concatenate(
        [packs_ref[8:24, :], jnp.zeros((ROWS - 16, D), F32)], 0
    ).astype(BF16)
    logits = dot_nt(n2, router)
    label = lax.broadcasted_iota(jnp.int32, (ROWS, ROWS), 1)
    chosen = jnp.zeros((ROWS, ROWS), jnp.bool_)
    for j in range(8):
        chosen = chosen | (routes_ref[:, j : j + 1] == label)
    masked = jnp.where(chosen, logits, NEGATIVE)
    expo = jnp.where(chosen, jnp.exp(masked - jnp.max(masked, -1, keepdims=True)), 0.0)
    gates = expo / jnp.sum(expo, -1, keepdims=True)
    gates_ref[...] = gates
    gates_t_ref[...] = jnp.transpose(gates)[0:16]

    for k in (2, 6, 4, 3, 7, 5):
        cots[k].wait_recv()
    own_c.wait()
    for k in (2, 6, 4, 3, 7, 5):
        sides[k].wait_recv()
    own_p.wait()
    share_p = copy_to(perms_ref.at[side], perms_ref.at[side], l_s.at[1], l_r.at[1], mate)
    share_p.wait_recv()
    for copies in (direct, forwards, outs_w, cots, sides):
        for copy in copies.values():
            copy.wait_send()
    for copy in small + picks + outs:
        copy.wait_send()
    share.wait_send()
    share_p.wait_send()


def experts_kernel(
    n2_ref, gates_ref, cots_ref, exp_ref,
    dn2_ref, dgate_ref, mix_ref, grad_ref,
    n2s, gs, part, dgp, recv, recvg, acts, dgus, dys, for_mate, from_mate,
    n_s, n_r, g_s, g_r, d_s, d_r, e_s, e_r, m_s, m_r,
):
    d, s = lax.axis_index("dp"), lax.axis_index("seq")
    core = lax.rem(s, 2)
    mate = (d, sibling(s))
    greet([(dp_peer(d, k), s) for k in DP_ORDER] + [mate])
    mine = rows(d * ROWS, ROWS)
    other = rows(dp_peer(d, 1) * ROWS, ROWS)
    gathers = {}
    gate_gathers = {}
    for k in DP_ORDER:
        gate_gathers[k] = copy_to(
            gates_ref, gs.at[:, mine], g_s.at[k], g_r.at[k], (dp_peer(d, k), s)
        )
    for k in (1, 2, 6, 4):
        gathers[k] = copy_to(n2_ref, n2s.at[mine], n_s.at[k], n_r.at[k], (dp_peer(d, k), s))
    n2s[mine] = n2_ref[...]
    gs[:, mine] = gates_ref[...]
    gathers[1].wait_recv()
    for k in (3, 7, 5):
        gathers[k] = copy_to(
            n2s.at[other], n2s.at[other], n_s.at[k], n_r.at[k], (dp_peer(d, k - 1), s)
        )
    x = lax.div(d, 2)
    backs = []
    for turn in (0, 1, 3, 2):
        for z in (0, 1):
            k = 2 * turn + z
            if k:
                if k != 1:
                    gathers[dp_back(k)].wait_recv()
                gate_gathers[dp_back(k)].wait_recv()
        place = rows(lax.rem(x + turn, 4) * 256, 256)
        tokens = n2s[place]
        cot = cots_ref[place].astype(F32)
        gates = jnp.transpose(jnp.concatenate([gs[:, place], jnp.zeros((ROWS - 16, 256), F32)], 0))
        lane = lax.broadcasted_iota(jnp.int32, gates.shape, 1)
        dn2 = jnp.zeros((256, D), F32)
        mix = jnp.zeros((256, D), F32)
        dgate = jnp.zeros(gates.shape, F32)
        for e in range(2):
            up_w = exp_ref[e, :, 0 : 2 * FF]
            down_w = exp_ref[e, :, 2 * FF :]
            here = lane == 2 * d + e
            gate = jnp.sum(jnp.where(here, gates, 0.0), -1, keepdims=True)
            gu = dot_nn(tokens, up_w)
            g, u = gu[:, :FF], gu[:, FF:]
            sigmoid = 1.0 / (1.0 + jnp.exp(-g))
            silu = g * sigmoid
            act = (silu * u).astype(BF16)
            acts[place, e * FF : (e + 1) * FF] = act
            y = dot_nt(act, down_w)
            dgate = jnp.where(here, jnp.sum(cot * y, -1, keepdims=True), dgate)
            mix = mix + gate * y
            dy = (gate * cot).astype(BF16)
            dys[place, e * D : (e + 1) * D] = dy
            dact = dot_nn(dy, down_w)
            dg = dact * u * (sigmoid * (1.0 + g * (1.0 - sigmoid)))
            du = dact * silu
            dgu = jnp.concatenate([dg, du], 1).astype(BF16)
            dgus[place, e * D : (e + 1) * D] = dgu
            dn2 = dn2 + dot_nt(dgu, up_w)
        mix_ref[place] = mix.astype(BF16)
        part[place] = dn2.astype(BF16)
        dgp[:, place] = jnp.transpose(dgate)[0:16]
        for z in (0, 1):
            k = 2 * turn + z
            if k:
                to = dp_peer(d, k)
                block = rows(to * ROWS, ROWS)
                backs.append(
                    copy_to(part.at[block], recv.at[k], d_s.at[k], d_r.at[k], (to, s))
                )
                backs.append(
                    copy_to(dgp.at[:, block], recvg.at[k], e_s.at[k], e_r.at[k], (to, s))
                )

    def grads(e):
        wide = rows(e * D, D)
        return (
            dot_tn(n2s[...], dgus[:, wide]),
            dot_tn(dys[:, wide], acts[:, rows(e * FF, FF)]),
        )

    first, second = grads(1 - core)
    for_mate[:, 0 : 2 * FF] = first.astype(BF16)
    for_mate[:, 2 * FF :] = second.astype(BF16)
    swap = copy_to(for_mate, from_mate, m_s.at[0], m_r.at[0], mate)
    first, second = grads(core)
    swap.wait_recv()
    grad_ref[:, 0 : 2 * FF] = (first + from_mate[:, 0 : 2 * FF].astype(F32)).astype(BF16)
    grad_ref[:, 2 * FF :] = (second + from_mate[:, 2 * FF :].astype(F32)).astype(BF16)
    for copy in backs:
        copy.wait_recv()
    total = part[mine].astype(F32)
    totalg = dgp[:, mine]
    for k in range(1, 8):
        total = total + recv[k].astype(F32)
        totalg = totalg + recvg[k]
    dn2_ref[...] = total
    dgate_ref[...] = jnp.transpose(
        jnp.concatenate([totalg, jnp.zeros((ROWS - 16, ROWS), F32)], 0)
    )
    for copies in (gathers, gate_gathers):
        for copy in copies.values():
            copy.wait_send()
    for copy in backs:
        copy.wait_send()
    swap.wait_send()


def back_kernel(
    dn2_ref, dgate_ref, gates_ref, mix_ref, x_ref, h_ref, n2_ref, cot_ref, packs_ref, wouts_ref, perms_ref,
    n1_ref, qkv_ref, lse_ref, o_ref, cos_ref, sin_ref, ge_ref,
    out_ref, gx_ref, gout_ref, fin_ref, full_ref,
    recv_e, part_e, sum_e, recv_m, gop, recv_g, gosum, gopart, gomate, dot_own, dot_all, k_nat, v_nat, dq_acc, dk_acc, dv_acc, kv_own, kv_mate,
    dp_own, dp_tok, finp, recv_f,
    b_s, b_r, ag_s, ag_r, fs_s, fs_r,
    m_s, m_r, go_s, go_r, gp_s, gp_r, gm_s, gm_r, gq_s, gq_r, do_s, do_r, kv_s, kv_r, dp_s, dp_r, f_s, f_r, t_s, t_r, u_s, u_r,
):
    d, s = lax.axis_index("dp"), lax.axis_index("seq")
    core = lax.rem(s, 2)
    greet(
        [(dp_peer(d, k), s) for k in DP_ORDER] + [(d, seq_peer(s, k)) for k in SEQ_ORDER]
    )
    here = rows(d * ROWS, ROWS)
    mine = rows(s * ROWS, ROWS)
    head = rows(s * HD, HD)
    mate = (d, sibling(s))

    def slab(k):
        return rows(lax.div(chip_peer(s, k), 2) * ROWS, ROWS)

    scatter = {}
    for k in (5, 7, 6, 1, 3, 2):
        scatter[k] = copy_to(
            ge_ref.at[slab(k)], recv_e.at[k], b_s.at[k], b_r.at[k], (d, chip_peer(s, k % 4))
        )
    gates = gates_ref[...]
    dgate = dgate_ref[...]
    inner = jnp.sum(gates * dgate, -1, keepdims=True)
    dlogits = (gates * (dgate - inner)).astype(BF16)
    router = jnp.concatenate(
        [packs_ref[8:24, :], jnp.zeros((ROWS - 16, D), F32)], 0
    ).astype(BF16)
    dn2 = dn2_ref[...] + dot_nn(dlogits, router)
    h = h_ref[...]
    r2 = lax.rsqrt(jnp.mean(h * h, -1, keepdims=True) + EPSILON)
    c = dn2 * packs_ref[1:2, :]
    dh = cot_ref[...].astype(F32) + r2 * c - h * (
        r2 * r2 * r2 * jnp.mean(c * h, -1, keepdims=True)
    )
    da = dh.astype(BF16)
    dot_own[...] = dot_nt(wouts_ref[...], da).astype(BF16)
    moves = []
    for k in SEQ_ORDER:
        to = seq_peer(s, k)
        moves.append(
            copy_to(
                dot_own.at[rows(to * HD, HD)], dot_all.at[:, mine], do_s.at[k], do_r.at[k], (d, to)
            )
        )
    dot_all[:, mine] = dot_own[head]
    gop[...] = dot_nn(o_ref[...], da).astype(BF16)
    gos = []
    mixes = []
    for k in DP_ORDER:
        to = dp_peer(d, k)
        block = rows(to * ROWS, ROWS)
        gos.append(copy_to(gop.at[block], recv_g.at[k], go_s.at[k], go_r.at[k], (to, s)))
    for k in DP_ORDER:
        to = dp_peer(d, k)
        block = rows(to * ROWS, ROWS)
        mixes.append(copy_to(mix_ref.at[block], recv_m.at[k], m_s.at[k], m_r.at[k], (to, s)))
    finp[128:, :] = jnp.zeros((32, D), F32)
    finp[128:144, :] = dot_tn(dlogits, n2_ref[...])[0:16]
    finp[144:145, :] = jnp.sum(dn2 * h * r2, 0, keepdims=True)
    k_nat[...] = jnp.transpose(qkv_ref[HD : 2 * HD].astype(F32)).astype(BF16)
    v_nat[...] = jnp.transpose(qkv_ref[2 * HD :].astype(F32)).astype(BF16)
    for copy in moves:
        copy.wait_recv()
    blocks = LENGTH // QBLOCK
    for block in reversed(range(blocks)):
        begin, end = block * QBLOCK, (block + 1) * QBLOCK
        query = qkv_ref[0:HD, begin:end]
        grad = dot_all[:, begin:end]
        scores = dot_nn(k_nat[0:end], query)
        probs = jnp.exp2(scores * (MULT * LOG2E) - lse_ref[:, begin:end] * LOG2E)
        low = probs[begin:]
        key = lax.broadcasted_iota(jnp.int32, low.shape, 0)
        pos = lax.broadcasted_iota(jnp.int32, low.shape, 1)
        low = jnp.where(key <= pos, low, 0.0)
        if block:
            probs = jnp.concatenate([probs[:begin], low], 0)
        else:
            probs = low
        pgrad = dot_nn(v_nat[0:end], grad)
        inner = jnp.sum(probs * pgrad, 0, keepdims=True)
        ds = (probs * (pgrad - inner)).astype(BF16)
        dv = dot_nt(grad, probs.astype(BF16))
        dk = dot_nt(query, ds)
        if block == blocks - 1:
            dv_acc[...] = dv
            dk_acc[...] = dk
        else:
            dv_acc[:, 0:end] += dv
            dk_acc[:, 0:end] += dk
        dq_acc[:, begin:end] = dot_nn(qkv_ref[HD : 2 * HD, 0:end], ds)
        if block == 1:
            for k in (5, 7, 6):
                scatter[k].wait_recv()
            part_e[...] = (
                ge_ref[slab(4)].astype(F32)
                + recv_e[5].astype(F32)
                + recv_e[6].astype(F32)
                + recv_e[7].astype(F32)
            ).astype(BF16)
            scatter[4] = copy_to(
                part_e, recv_e.at[4], b_s.at[4], b_r.at[4], (d, chip_peer(s, 4))
            )
    kv_own[0:HD] = (dk_acc[...] * MULT).astype(BF16)
    kv_own[HD:] = dv_acc[...].astype(BF16)
    swap = copy_to(kv_own, kv_mate, kv_s.at[0], kv_r.at[0], mate)
    cosine = cos_ref[...]
    sine = sin_ref[...]

    def unturn(v):
        a, b = v[:HALF], v[HALF:]
        return jnp.concatenate([a * cosine + b * sine, b * cosine - a * sine], 0)

    dp_own[0:HD] = unturn((dq_acc[...] * MULT).astype(BF16).astype(F32)).astype(BF16)
    swap.wait_recv()
    both = kv_own[...].astype(F32) + kv_mate[...].astype(F32)
    dp_own[HD:] = jnp.where(core == 0, unturn(both[:HD]), both[HD:]).astype(BF16)
    shares = []
    slot = rows(s * ROWS, ROWS)
    for k in SEQ_ORDER:
        to = seq_peer(s, k)
        shares.append(
            copy_to(
                dp_own.at[:, rows(to * ROWS, ROWS)],
                dp_tok.at[slot],
                dp_s.at[k],
                dp_r.at[k],
                (d, to),
            )
        )
    dp_tok[slot] = dp_own[:, mine]
    finp[0:128, :] = dot_nn(dp_own[...], n1_ref[...])

    for k in (1, 3, 2, 4):
        scatter[k].wait_recv()
    sum_e[...] = (
        ge_ref[slab(0)].astype(F32)
        + recv_e[1].astype(F32)
        + recv_e[2].astype(F32)
        + recv_e[3].astype(F32)
        + recv_e[4].astype(F32)
    ).astype(BF16)
    gather = {}
    spare = {}
    own_e = full_ref.at[core, slab(0)]
    keep = pltpu.make_async_copy(sum_e, own_e, fs_s.at[8])
    keep.start()
    for k in (4, 1, 3, 2):
        gather[k] = copy_to(sum_e, own_e, ag_s.at[k], ag_r.at[k], (d, chip_peer(s, k)))
    spare[0] = copy_to(sum_e, own_e, fs_s.at[0], fs_r.at[0], mate)

    def arrived(k):
        gather[k].wait_recv()
        at = full_ref.at[core, slab(chip_back(k))]
        spare[k] = copy_to(at, at, fs_s.at[k], fs_r.at[k], mate)
        return at

    for copy in gos:
        copy.wait_recv()
    total = gop[here].astype(F32)
    for k in range(1, 8):
        total = total + recv_g[k].astype(F32)
    gosum[...] = total.astype(BF16)
    pieces = []
    for k in CHIP_ORDER:
        pieces.append(
            copy_to(
                gosum.at[:, slab(k)], gopart.at[k], gp_s.at[k], gp_r.at[k], (d, chip_peer(s, k))
            )
        )
    for copy in shares:
        copy.wait_recv()
    dn1 = dot_tn(dp_tok[...], perms_ref[...])
    x = x_ref[...].astype(F32)
    r1 = lax.rsqrt(jnp.mean(x * x, -1, keepdims=True) + EPSILON)
    c = dn1 * packs_ref[0:1, :]
    gx_ref[...] = dh + r1 * c - x * (r1 * r1 * r1 * jnp.mean(c * x, -1, keepdims=True))
    finp[145:146, :] = jnp.sum(dn1 * x * r1, 0, keepdims=True)
    finals = []
    for k in DP_ORDER:
        to = dp_peer(d, k)
        finals.append(
            copy_to(
                finp.at[:, rows(to * ROWS, ROWS)], recv_f.at[k], f_s.at[k], f_r.at[k], (to, s)
            )
        )
    partner = arrived(4)
    for k in (5, 7, 6):
        gather[k] = copy_to(partner, partner, ag_s.at[k], ag_r.at[k], (d, chip_peer(s, k - 4)))
    for copy in pieces:
        copy.wait_recv()
    total = gosum[:, slab(0)].astype(F32)
    for k in range(1, 8):
        total = total + gopart[k].astype(F32)
    gomate[0] = total
    pair = copy_to(gomate.at[0], gomate.at[1], gm_s.at[0], gm_r.at[0], mate)
    pair.wait_recv()
    gout_ref[:, slab(0)] = (total + gomate[1]).astype(BF16)
    wholes = []
    for k in CHIP_ORDER:
        wholes.append(
            copy_to(
                gout_ref.at[:, slab(0)],
                gout_ref.at[:, slab(0)],
                gq_s.at[k],
                gq_r.at[k],
                (d, chip_peer(s, k)),
            )
        )
    for copy in finals:
        copy.wait_recv()
    total = finp[:, here]
    for k in range(1, 8):
        total = total + recv_f[k]
    fin_ref[s] = total.astype(BF16)
    tails = {}
    for k in CHIP_ORDER:
        tails[k] = copy_to(
            fin_ref.at[s], fin_ref.at[s], t_s.at[k], t_r.at[k], (d, chip_peer(s, k))
        )
    passed = [copy_to(fin_ref.at[s], fin_ref.at[s], u_s.at[0], u_r.at[0], mate)]
    for copy in mixes:
        copy.wait_recv()
    total = h + mix_ref[here].astype(F32)
    for k in range(1, 8):
        total = total + recv_m[k].astype(F32)
    out_ref[...] = total.astype(BF16)
    for k in (1, 3, 2):
        arrived(k)
    for k in CHIP_ORDER:
        tails[k].wait_recv()
        at = fin_ref.at[chip_peer(s, chip_back(k))]
        passed.append(copy_to(at, at, u_s.at[k], u_r.at[k], mate))
    for k in (5, 7, 6):
        arrived(k)
    keep.wait()
    for copy in wholes + passed:
        copy.wait_recv()
    for copy in spare.values():
        copy.wait_recv()
    for copies in (scatter, gather, spare, tails):
        for copy in copies.values():
            copy.wait_send()
    for copy in moves + gos + mixes + [swap, pair] + shares + pieces + finals + wholes + passed:
        copy.wait_send()


def sems(count):
    return pltpu.SemaphoreType.DMA((count,))


def params(identity):
    return pltpu.CompilerParams(
        collective_id=identity, has_side_effects=True, vmem_limit_bytes=60 << 20
    )


def angle_tables():
    freqs = np.float32(THETA) ** (
        -(np.arange(HALF, dtype=np.float32) * np.float32(2.0) / np.float32(HD))
    )
    angles = freqs.astype(np.float32)[:, None] * np.arange(LENGTH, dtype=np.float32)[None, :]
    angles = angles.astype(np.float64)
    return np.cos(angles).astype(np.float32), np.sin(angles).astype(np.float32)


def sds(shape, dtype):
    return jax.ShapeDtypeStruct(shape, dtype)


def shards(tokens, w_qkv, w_out, w_router, gain_attn, gain_moe, experts, routes, cotangent):
    cosine, sine = angle_tables()
    cosine, sine = jnp.asarray(cosine), jnp.asarray(sine)
    pack = jnp.concatenate(
        [
            gain_attn.astype(F32)[None],
            gain_moe.astype(F32)[None],
            jnp.zeros((6, ROWS), F32),
            w_router.astype(F32).T,
        ],
        0,
    )
    query_w = w_qkv[:, :D].reshape(ROWS, QH, HD)
    keys_w = w_qkv[:, D:].reshape(ROWS, 2, QH // 2, HD).transpose(0, 2, 1, 3).reshape(ROWS, QH, HD)
    perm = jnp.concatenate([query_w, keys_w], -1).reshape(ROWS, 2 * D).T

    n1, qkv, lse, o_tok, h, n2, gates, gates_t, packs, wouts, cots, perms = pl.pallas_call(
        front_kernel,
        out_shape=(
            sds((LENGTH, D), BF16),
            sds((3 * HD, LENGTH), BF16),
            sds((1, LENGTH), F32),
            sds((D, ROWS), BF16),
            sds((ROWS, D), F32),
            sds((ROWS, D), BF16),
            sds((ROWS, ROWS), F32),
            sds((16, ROWS), F32),
            sds((24, D), F32),
            sds((D, D), BF16),
            sds((D, D), BF16),
            sds((2 * D, D), BF16),
        ),
        in_specs=[VMEM, VMEM, VMEM, VMEM, VMEM, VMEM, VMEM, VMEM],
        out_specs=(VMEM,) * 10 + (ANY, ANY),
        scratch_shapes=[
            pltpu.VMEM((ROWS, D), BF16),
            pltpu.VMEM((HD, D), BF16),
            pltpu.VMEM((HD, LENGTH), BF16),
            pltpu.VMEM((LENGTH, HD), BF16),
        ]
        + [sems(8)] * 16
        + [sems(16)] * 2
        + [sems(2)] * 2
        + [sems(5)],
        compiler_params=params(1),
        name="front",
    )(tokens, pack, perm, w_out, cotangent, routes, cosine, sine)

    dn2, dgate, mix, expert_grads = pl.pallas_call(
        experts_kernel,
        out_shape=(
            sds((ROWS, D), F32),
            sds((ROWS, ROWS), F32),
            sds((D, D), BF16),
            sds((D, 3 * FF), BF16),
        ),
        in_specs=[VMEM] * 4,
        out_specs=(VMEM,) * 4,
        scratch_shapes=[
            pltpu.VMEM((D, D), BF16),
            pltpu.VMEM((16, D), F32),
            pltpu.VMEM((D, D), BF16),
            pltpu.VMEM((16, D), F32),
            pltpu.VMEM((8, ROWS, D), BF16),
            pltpu.VMEM((8, 16, ROWS), F32),
            pltpu.VMEM((D, 2 * FF), BF16),
            pltpu.VMEM((D, 2 * D), BF16),
            pltpu.VMEM((D, 2 * D), BF16),
            pltpu.VMEM((D, 3 * FF), BF16),
            pltpu.VMEM((D, 3 * FF), BF16),
        ]
        + [sems(8)] * 8
        + [sems(1)] * 2,
        compiler_params=params(2),
        name="experts",
    )(n2, gates_t, cots, experts)

    out, grad_x, grad_out, fin, grad_experts = pl.pallas_call(
        back_kernel,
        out_shape=(
            sds((ROWS, D), BF16),
            sds((ROWS, D), F32),
            sds((ROWS, D), BF16),
            sds((N_SEQ, 160, ROWS), BF16),
            sds((2, D, 3 * FF), BF16),
        ),
        in_specs=[VMEM] * 18,
        out_specs=(VMEM,) * 4 + (ANY,),
        scratch_shapes=[
            pltpu.VMEM((8, ROWS, 3 * FF), BF16),
            pltpu.VMEM((ROWS, 3 * FF), BF16),
            pltpu.VMEM((ROWS, 3 * FF), BF16),
            pltpu.VMEM((8, ROWS, D), BF16),
            pltpu.VMEM((D, D), BF16),
            pltpu.VMEM((8, ROWS, D), BF16),
            pltpu.VMEM((ROWS, D), BF16),
            pltpu.VMEM((8, ROWS, ROWS), BF16),
            pltpu.VMEM((2, ROWS, ROWS), F32),
            pltpu.VMEM((D, ROWS), BF16),
            pltpu.VMEM((HD, LENGTH), BF16),
            pltpu.VMEM((LENGTH, HD), BF16),
            pltpu.VMEM((LENGTH, HD), BF16),
            pltpu.VMEM((HD, LENGTH), F32),
            pltpu.VMEM((HD, LENGTH), F32),
            pltpu.VMEM((HD, LENGTH), F32),
            pltpu.VMEM((ROWS, LENGTH), BF16),
            pltpu.VMEM((ROWS, LENGTH), BF16),
            pltpu.VMEM((ROWS, LENGTH), BF16),
            pltpu.VMEM((2 * D, ROWS), BF16),
            pltpu.VMEM((160, D), F32),
            pltpu.VMEM((8, 160, ROWS), F32),
        ]
        + [sems(8)] * 4
        + [sems(9)] * 2
        + [sems(8)] * 6
        + [sems(1)] * 2
        + [sems(8)] * 2
        + [sems(16)] * 2
        + [sems(1)] * 2
        + [sems(16)] * 2
        + [sems(8)] * 6,
        compiler_params=params(3),
        name="back",
    )(
        dn2, dgate, gates, mix, tokens, h, n2, cotangent, packs, wouts, perms,
        n1, qkv, lse, o_tok, cosine, sine, expert_grads,
    )

    grads = fin[:, :128].astype(F32)
    query_g = grads[:, :HD].reshape(D, ROWS).T
    keys_g = (
        grads[:, HD:].reshape(QH // 2, 2, HD, ROWS).transpose(3, 1, 0, 2).reshape(ROWS, D)
    )
    grad_qkv = jnp.concatenate([query_g, keys_g], -1)
    small = jnp.sum(fin[:, 128:].astype(F32), 0)
    return (
        out,
        grad_x,
        grad_qkv,
        grad_out.astype(F32),
        small[:16].T,
        small[17],
        small[16],
        grad_experts.astype(F32),
    )


def solution(mesh):
    placed = (
        P(("dp", "seq"), None),
        P("dp", None),
        P("dp", None),
        P("dp", None),
        P("dp"),
        P("dp"),
        P("dp", None, None),
        P(("dp", "seq"), None),
        P(("dp", "seq"), None),
    )
    return jax.shard_map(
        shards,
        mesh=mesh,
        in_specs=placed,
        out_specs=(
            P(("dp", "seq"), None),
            P(("dp", "seq"), None),
            P("dp", None),
            P("dp", None),
            P("dp", None),
            P("dp"),
            P("dp"),
            P("dp", None, None),
        ),
        check_vma=False,
    )
```

```python
import functools

import jax
import jax.numpy as jnp
import numpy as np
from jax import lax
from jax.experimental import pallas as pl
from jax.experimental.pallas import tpu as pltpu
from jax.sharding import PartitionSpec as P

D = 1024
QH = 16
HD = 64
HALF = 32
FF = 512
N_DP = 8
N_SEQ = 16
ROWS = 128
LENGTH = 2048
QBLOCK = 512

EPSILON = 1e-06
MULT = 0.015625
THETA = 10000.0
NEGATIVE = -1e30
LOG2E = 1.4426950408889634

F32 = jnp.float32
BF16 = jnp.bfloat16
MESH = pl.DeviceIdType.MESH
VMEM = pl.BlockSpec(memory_space=pltpu.VMEM)
ANY = pl.BlockSpec(memory_space=pl.ANY)

DP_ORDER = (1, 2, 6, 3, 7, 4, 5)
CHIP_ORDER = (4, 1, 3, 5, 7, 2, 6)


def dot_nn(a, b):
    return lax.dot_general(a, b, (((1,), (0,)), ((), ())), preferred_element_type=F32)


def dot_nt(a, b):
    return lax.dot_general(a, b, (((1,), (1,)), ((), ())), preferred_element_type=F32)


def dot_tn(a, b):
    return lax.dot_general(a, b, (((0,), (0,)), ((), ())), preferred_element_type=F32)


def dp_peer(d, k):
    return lax.rem(lax.div(d, 2) + k // 2, 4) * 2 + lax.rem(lax.rem(d, 2) + k % 2, 2)


def dp_back(k):
    return 2 * ((4 - k // 2) % 4) + k % 2


def chip_peer(s, k):
    z, y, c = lax.div(s, 8), lax.rem(lax.div(s, 2), 4), lax.rem(s, 2)
    return lax.rem(z + k // 4, 2) * 8 + lax.rem(y + k % 4, 4) * 2 + c


def chip_back(k):
    return 4 * (k // 4) + (4 - k % 4) % 4


def seq_peer(s, k):
    base = chip_peer(s, k // 2)
    c = lax.rem(s, 2)
    return base if k % 2 == 0 else base + 1 - 2 * c


SEQ_ORDER = tuple(2 * c + o for c in (0,) + CHIP_ORDER for o in (0, 1) if 2 * c + o)


def seq_back(k):
    return 2 * chip_back(k // 2) + k % 2


def sibling(s):
    return s + 1 - 2 * lax.rem(s, 2)


def copy_to(src, dst, send, recv, device):
    copy = pltpu.make_async_remote_copy(
        src_ref=src,
        dst_ref=dst,
        send_sem=send,
        recv_sem=recv,
        device_id=device,
        device_id_type=MESH,
    )
    copy.start()
    return copy


def greet(devices):
    barrier = pltpu.get_barrier_semaphore()
    for device in devices:
        pl.semaphore_signal(barrier, inc=1, device_id=device, device_id_type=MESH)
    pl.semaphore_wait(barrier, len(devices))


def rows(start, size):
    return pl.ds(pl.multiple_of(start, size), size)


def front_kernel(
    x_ref, pack_ref, perm_ref, wout_ref, cot_ref, routes_ref, cos_ref, sin_ref,
    n1_ref, qkv_ref, lse_ref, o_ref, h_ref, n2_ref, gates_ref, gates_t_ref, packs_ref, wouts_ref, cots_ref,
    sel_a, sel_b, o_own, k_nat,
    pack_s, pack_r, a_s, a_r, b_s, b_r, n1_s, n1_r, f_s, f_r, w_s, w_r, c_s, c_r, o_s, o_r, l_s, l_r, own_s,
):
    d, s = lax.axis_index("dp"), lax.axis_index("seq")
    core = lax.rem(s, 2)
    mate = (d, sibling(s))
    greet(
        [(dp_peer(d, k), s) for k in DP_ORDER] + [(d, seq_peer(s, k)) for k in SEQ_ORDER]
    )
    lanes = rows(d * ROWS, ROWS)
    small = []
    head_rows = rows(s * ROWS, ROWS)
    mate_rows = rows(sibling(s) * ROWS + HD, HD)
    for k in DP_ORDER:
        to = (dp_peer(d, k), s)
        small.append(copy_to(pack_ref, packs_ref.at[:, lanes], pack_s.at[k], pack_r.at[k], to))
    picks = []
    for k in DP_ORDER:
        to = (dp_peer(d, k), s)
        picks.append(copy_to(perm_ref.at[head_rows], sel_a.at[:, lanes], a_s.at[k], a_r.at[k], to))
        picks.append(copy_to(perm_ref.at[mate_rows], sel_b.at[:, lanes], b_s.at[k], b_r.at[k], to))
    own_a = pltpu.make_async_copy(perm_ref.at[head_rows], sel_a.at[:, lanes], own_s.at[0])
    own_b = pltpu.make_async_copy(perm_ref.at[mate_rows], sel_b.at[:, lanes], own_s.at[1])
    own_a.start()
    own_b.start()
    packs_ref[:, lanes] = pack_ref[...]
    x = x_ref[...].astype(F32)
    r1 = lax.rsqrt(jnp.mean(x * x, -1, keepdims=True) + EPSILON)
    for copy in small:
        copy.wait_recv()
    mine = rows(s * ROWS, ROWS)
    n1_ref[mine] = (x * r1 * packs_ref[0:1, :]).astype(BF16)
    direct = {}
    forwards = {0: copy_to(n1_ref.at[mine], n1_ref.at[mine], f_s.at[0], f_r.at[0], mate)}
    for k in (4, 1, 3):
        direct[k] = copy_to(
            n1_ref.at[mine], n1_ref.at[mine], n1_s.at[k], n1_r.at[k], (d, chip_peer(s, k))
        )
    half = rows(core * 512, 512)
    other = rows(dp_peer(d, 1) * ROWS, ROWS)

    def spread(source, place, send, recv):
        return {
            k: copy_to(source, place(lanes), send.at[k], recv.at[k], (dp_peer(d, k), s))
            for k in (1, 2, 6, 4)
        }

    def pass_on(copies, place, send, recv):
        copies[1].wait_recv()
        for k in (3, 7, 5):
            copies[k] = copy_to(
                place(other), place(other), send.at[k], recv.at[k], (dp_peer(d, k - 1), s)
            )

    def keep(source, place, k):
        copy = pltpu.make_async_copy(source, place(lanes), own_s.at[k])
        copy.start()
        return copy

    out_source, out_place = wout_ref.at[:, half], lambda at: wouts_ref.at[at, half]
    cot_place = lambda at: cots_ref.at[at]
    outs_w = spread(out_source, out_place, w_s, w_r)
    own_w = keep(out_source, out_place, 2)
    direct[4].wait_recv()
    partner = rows(chip_peer(s, 4) * ROWS, ROWS)
    forwards[4] = copy_to(n1_ref.at[partner], n1_ref.at[partner], f_s.at[4], f_r.at[4], mate)
    for k in (5, 7):
        direct[k] = copy_to(
            n1_ref.at[partner],
            n1_ref.at[partner],
            n1_s.at[k],
            n1_r.at[k],
            (d, chip_peer(s, k - 4)),
        )
    cots = spread(cot_ref, cot_place, c_s, c_r)
    own_c = keep(cot_ref, cot_place, 3)
    pass_on(outs_w, out_place, w_s, w_r)
    for copy in picks:
        copy.wait_recv()
    own_a.wait()
    own_b.wait()

    def project(chip):
        block = rows(chip * 256, 256)
        tokens = n1_ref[block]
        cosine = cos_ref[:, block]
        sine = sin_ref[:, block]

        def turn(v):
            a, b = v[:HALF], v[HALF:]
            return jnp.concatenate([a * cosine - b * sine, b * cosine + a * sine], 0)

        pa = dot_nt(sel_a[...], tokens)
        pb = dot_nt(sel_b[...], tokens)
        even = core == 0
        keys = jnp.where(even, pa[HD:], pb)
        values = jnp.where(even, pb, pa[HD:])
        qkv_ref[:, block] = jnp.concatenate([turn(pa[:HD]), turn(keys), values], 0).astype(BF16)

    last = 0
    for k in (4, 1, 3, 5, 7, 2, 6):
        start = chip_peer(s, chip_back(k)) * ROWS
        source = rows(start, ROWS)
        if k != 4:
            direct[k].wait_recv()
            if k in (2, 6):
                direct[8 + k // 6].wait_recv()
            else:
                low = k % 4 == 1
                piece = rows(start if low else start + 64, 64)
                index = k + 1 if low else 7 + (k + 1) // 4
                direct[index] = copy_to(
                    n1_ref.at[piece],
                    n1_ref.at[piece],
                    n1_s.at[index],
                    n1_r.at[index],
                    (d, chip_peer(s, k % 4)),
                )
            forwards[k] = copy_to(
                n1_ref.at[source], n1_ref.at[source], f_s.at[k], f_r.at[k], mate
            )
        forwards[last].wait_recv()
        project(lax.div(chip_peer(s, chip_back(last)), 2))
        last = k
        if k == 3:
            pass_on(cots, cot_place, c_s, c_r)
    forwards[last].wait_recv()
    project(lax.div(chip_peer(s, chip_back(last)), 2))

    k_nat[...] = jnp.transpose(qkv_ref[HD : 2 * HD].astype(F32)).astype(BF16)
    outs = []
    for block in range(LENGTH // QBLOCK):
        begin, end = block * QBLOCK, (block + 1) * QBLOCK
        query = qkv_ref[0:HD, begin:end]
        scores = dot_nn(k_nat[0:end], query)
        low = scores[begin:]
        key = lax.broadcasted_iota(jnp.int32, low.shape, 0)
        pos = lax.broadcasted_iota(jnp.int32, low.shape, 1)
        low = jnp.where(key <= pos, low, NEGATIVE)
        if block:
            scores = jnp.concatenate([scores[:begin], low], 0)
        else:
            scores = low
        top = jnp.max(scores, 0, keepdims=True)
        expo = jnp.exp2((scores - top) * (MULT * LOG2E))
        total = jnp.sum(expo, 0, keepdims=True)
        probs = (expo * (1.0 / total)).astype(BF16)
        lse_ref[:, begin:end] = top * MULT + jnp.log(total)
        o_own[:, begin:end] = dot_nn(qkv_ref[2 * HD :, 0:end], probs).astype(BF16)
    place = rows(s * HD, HD)
    for k in SEQ_ORDER:
        to = seq_peer(s, k)
        outs.append(
            copy_to(
                o_own.at[:, rows(to * ROWS, ROWS)], o_ref.at[place], o_s.at[k], o_r.at[k], (d, to)
            )
        )
    o_ref[place] = o_own[:, mine]
    for k in (2, 6, 4, 3, 7, 5):
        outs_w[k].wait_recv()
    own_w.wait()
    share = copy_to(wouts_ref.at[:, half], wouts_ref.at[:, half], l_s.at[0], l_r.at[0], mate)
    for copy in outs:
        copy.wait_recv()
    share.wait_recv()
    mixed = jnp.transpose(o_ref[...].astype(F32)).astype(BF16)
    h = x + dot_nn(mixed, wouts_ref[...])
    h_ref[...] = h
    r2 = lax.rsqrt(jnp.mean(h * h, -1, keepdims=True) + EPSILON)
    n2 = (h * r2 * packs_ref[1:2, :]).astype(BF16)
    n2_ref[...] = n2
    router = jnp.concatenate(
        [packs_ref[8:24, :], jnp.zeros((ROWS - 16, D), F32)], 0
    ).astype(BF16)
    logits = dot_nt(n2, router)
    label = lax.broadcasted_iota(jnp.int32, (ROWS, ROWS), 1)
    chosen = jnp.zeros((ROWS, ROWS), jnp.bool_)
    for j in range(8):
        chosen = chosen | (routes_ref[:, j : j + 1] == label)
    masked = jnp.where(chosen, logits, NEGATIVE)
    expo = jnp.where(chosen, jnp.exp(masked - jnp.max(masked, -1, keepdims=True)), 0.0)
    gates = expo / jnp.sum(expo, -1, keepdims=True)
    gates_ref[...] = gates
    gates_t_ref[...] = jnp.transpose(gates)[0:16]

    for k in (2, 6, 4, 3, 7, 5):
        cots[k].wait_recv()
    own_c.wait()
    for copies in (direct, forwards, outs_w, cots):
        for copy in copies.values():
            copy.wait_send()
    for copy in small + picks + outs:
        copy.wait_send()
    share.wait_send()


def experts_kernel(
    n2_ref, gates_ref, cots_hbm, exp_hbm,
    dn2_ref, dgate_ref, mix_ref, grad_ref,
    cots_ref, exp_ref, n2s, gs, part, dgp, recv_z, recv, recvg, acts, dgus, dys, for_mate, from_mate,
    n_s, n_r, g_s, g_r, z_s, z_r, d_s, d_r, e_s, e_r, m_s, m_r, own_s,
):
    d, s = lax.axis_index("dp"), lax.axis_index("seq")
    core = lax.rem(s, 2)
    mate = (d, sibling(s))
    fetches = [
        pltpu.make_async_copy(exp_hbm, exp_ref, own_s.at[0]),
        pltpu.make_async_copy(cots_hbm, cots_ref, own_s.at[1]),
    ]
    for copy in fetches:
        copy.start()
    greet([(dp_peer(d, k), s) for k in DP_ORDER] + [mate])
    mine = rows(d * ROWS, ROWS)
    other = rows(dp_peer(d, 1) * ROWS, ROWS)
    gathers = {}
    gate_gathers = {}
    for k in DP_ORDER:
        gate_gathers[k] = copy_to(
            gates_ref, gs.at[:, mine], g_s.at[k], g_r.at[k], (dp_peer(d, k), s)
        )
    for k in (1, 2, 6):
        gathers[k] = copy_to(n2_ref, n2s.at[mine], n_s.at[k], n_r.at[k], (dp_peer(d, k), s))
    n2s[mine] = n2_ref[...]
    gs[:, mine] = gates_ref[...]
    gathers[1].wait_recv()
    for k in (3, 7):
        gathers[k] = copy_to(
            n2s.at[other], n2s.at[other], n_s.at[k], n_r.at[k], (dp_peer(d, k - 1), s)
        )
    x = lax.div(d, 2)
    for copy in fetches:
        copy.wait()
    backs = []
    pairs = {}
    sums = {}
    z = lax.rem(d, 2)

    def onward(turn):
        pairs[turn].wait_recv()
        block = rows(dp_peer(d, 2 * turn) * ROWS, ROWS)
        part[block] = (part[block].astype(F32) + recv_z[turn].astype(F32)).astype(BF16)
        if turn:
            sums[turn] = copy_to(
                part.at[block],
                recv.at[turn],
                d_s.at[turn],
                d_r.at[turn],
                (dp_peer(d, 2 * turn), s),
            )

    for step, turn in enumerate((0, 1, 3, 2)):
        if step == 1:
            for k in (2, 6, 3, 7):
                gathers[k].wait_recv()
                start = dp_peer(d, dp_back(k)) * ROWS
                low = k < 4
                piece = rows(start if low else start + 64, 64)
                index = k + 2
                gathers[index] = copy_to(
                    n2s.at[piece],
                    n2s.at[piece],
                    n_s.at[index],
                    n_r.at[index],
                    (dp_peer(d, 2 if low else 6), s),
                )
        for z_off in (0, 1):
            k = 2 * turn + z_off
            if k:
                gate_gathers[dp_back(k)].wait_recv()
            if turn == 2:
                gathers[k].wait_recv()
                gathers[k + 4].wait_recv()
        place = rows(lax.rem(x + turn, 4) * 256, 256)
        tokens = n2s[place]
        cot = cots_ref[place].astype(F32)
        gates = jnp.transpose(jnp.concatenate([gs[:, place], jnp.zeros((ROWS - 16, 256), F32)], 0))
        lane = lax.broadcasted_iota(jnp.int32, gates.shape, 1)
        dn2 = jnp.zeros((256, D), F32)
        mix = jnp.zeros((256, D), F32)
        dgate = jnp.zeros(gates.shape, F32)
        for e in range(2):
            up_w = exp_ref[e, :, 0 : 2 * FF]
            down_w = exp_ref[e, :, 2 * FF :]
            here = lane == 2 * d + e
            gate = jnp.sum(jnp.where(here, gates, 0.0), -1, keepdims=True)
            gu = dot_nn(tokens, up_w)
            g, u = gu[:, :FF], gu[:, FF:]
            sigmoid = 1.0 / (1.0 + jnp.exp(-g))
            silu = g * sigmoid
            act = (silu * u).astype(BF16)
            acts[place, e * FF : (e + 1) * FF] = act
            y = dot_nt(act, down_w)
            dgate = jnp.where(here, jnp.sum(cot * y, -1, keepdims=True), dgate)
            mix = mix + gate * y
            dy = (gate * cot).astype(BF16)
            dys[place, e * D : (e + 1) * D] = dy
            dact = dot_nn(dy, down_w)
            dg = dact * u * (sigmoid * (1.0 + g * (1.0 - sigmoid)))
            du = dact * silu
            dgu = jnp.concatenate([dg, du], 1).astype(BF16)
            dgus[place, e * D : (e + 1) * D] = dgu
            dn2 = dn2 + dot_nt(dgu, up_w)
        mix_ref[place] = mix.astype(BF16)
        part[place] = dn2.astype(BF16)
        dgp[:, place] = jnp.transpose(dgate)[0:16]
        away = rows(dp_peer(d, 2 * turn + 1) * ROWS, ROWS)
        pairs[turn] = copy_to(
            part.at[away], recv_z.at[turn], z_s.at[turn], z_r.at[turn], (dp_peer(d, 1), s)
        )
        for z_off in (0, 1):
            k = 2 * turn + z_off
            if k:
                to = dp_peer(d, k)
                block = rows(to * ROWS, ROWS)
                backs.append(
                    copy_to(dgp.at[:, block], recvg.at[k], e_s.at[k], e_r.at[k], (to, s))
                )
        if step:
            onward((0, 1, 3, 2)[step - 1])

    def grads(e):
        wide = rows(e * D, D)
        return (
            dot_tn(n2s[...], dgus[:, wide]),
            dot_tn(dys[:, wide], acts[:, rows(e * FF, FF)]),
        )

    first, second = grads(1 - core)
    for_mate[:, 0 : 2 * FF] = first.astype(BF16)
    for_mate[:, 2 * FF :] = second.astype(BF16)
    swap = copy_to(for_mate, from_mate, m_s.at[0], m_r.at[0], mate)
    onward(2)
    first, second = grads(core)
    swap.wait_recv()
    grad_ref[:, 0 : 2 * FF] = (first + from_mate[:, 0 : 2 * FF].astype(F32)).astype(BF16)
    grad_ref[:, 2 * FF :] = (second + from_mate[:, 2 * FF :].astype(F32)).astype(BF16)
    for copy in list(sums.values()) + backs:
        copy.wait_recv()
    total = part[mine].astype(F32)
    for k in range(1, 4):
        total = total + recv[k].astype(F32)
    totalg = dgp[:, mine]
    for k in range(1, 8):
        totalg = totalg + recvg[k]
    dn2_ref[...] = total
    dgate_ref[...] = jnp.transpose(
        jnp.concatenate([totalg, jnp.zeros((ROWS - 16, ROWS), F32)], 0)
    )
    for copies in (gathers, gate_gathers, pairs, sums):
        for copy in copies.values():
            copy.wait_send()
    for copy in backs:
        copy.wait_send()
    swap.wait_send()


def back_kernel(
    dn2_ref, dgate_ref, gates_ref, mix_ref, x_ref, h_ref, n2_ref, cot_ref, packs_ref, wouts_ref, perm_ref,
    n1_hbm, qkv_ref, lse_ref, o_ref, cos_ref, sin_ref, ge_ref,
    out_ref, gx_ref, gout_ref, fin_ref, full_ref,
    n1_ref, mix_own, mix_far, perms_ref, half_e, whole_e, stage_e, recv_z, part_e, sum_e, recv_m, gop, recv_g, zout, zin, gosum, gopart, gomate, dot_own, dot_all, k_nat, v_nat, dq_acc, dk_acc, dv_acc, kv_own, kv_mate,
    dp_own, dp_tok, finp, recv_f,
    w_s, w_r, l_s, l_r, b_s, b_r, c_s, c_r, z_s, z_r, ag_s, ag_r, fs_s, fs_r,
    m_s, m_r, go_s, go_r, zz_s, zz_r, own_s, gp_s, gp_r, gm_s, gm_r, gq_s, gq_r, do_s, do_r, kv_s, kv_r, dp_s, dp_r, f_s, f_r, t_s, t_r, u_s, u_r,
):
    d, s = lax.axis_index("dp"), lax.axis_index("seq")
    core = lax.rem(s, 2)
    greet(
        [(dp_peer(d, k), s) for k in DP_ORDER] + [(d, seq_peer(s, k)) for k in SEQ_ORDER]
    )
    here = rows(d * ROWS, ROWS)
    mine = rows(s * ROWS, ROWS)
    head = rows(s * HD, HD)
    mate = (d, sibling(s))

    def slab(k):
        return rows(lax.div(chip_peer(s, k), 2) * ROWS, ROWS)

    lanes = rows(d * ROWS, ROWS)
    side = rows(core * 1024, 1024)

    halves = {}
    wholes_e = {}

    def begin_scatter():
        for base in (4, 0):
            far = lax.div(chip_peer(s, base + 2), 2) * ROWS
            for low in (True, False):
                k = base + (1 if low else 3)
                piece = rows(far if low else far + 64, 64)
                halves[k] = copy_to(
                    ge_ref.at[piece],
                    half_e.at[k],
                    b_s.at[k],
                    b_r.at[k],
                    (d, chip_peer(s, k % 4)),
                )

    def mid_scatter(base):
        for low in (True, False):
            k = base + (1 if low else 3)
            halves[k].wait_recv()
            start = lax.div(chip_peer(s, k), 2) * ROWS
            first, second = rows(start, 64), rows(start + 64, 64)
            added = half_e[k].astype(F32)
            if low:
                stage_e[k, 0:64] = (ge_ref[first].astype(F32) + added).astype(BF16)
                stage_e[k, 64:128] = ge_ref[second]
            else:
                stage_e[k, 0:64] = ge_ref[first]
                stage_e[k, 64:128] = (ge_ref[second].astype(F32) + added).astype(BF16)
            wholes_e[k] = copy_to(
                stage_e.at[k], whole_e.at[k], c_s.at[k], c_r.at[k], (d, chip_peer(s, k % 4))
            )

    def end_scatter(base):
        wholes_e[base + 1].wait_recv()
        wholes_e[base + 3].wait_recv()
        return (
            ge_ref[slab(base)].astype(F32)
            + whole_e[base + 1].astype(F32)
            + whole_e[base + 3].astype(F32)
        )

    fetch_n1 = pltpu.make_async_copy(n1_hbm, n1_ref, own_s.at[0])
    fetch_mix = pltpu.make_async_copy(mix_ref.at[here], mix_own, own_s.at[1])
    fetch_far = pltpu.make_async_copy(
        mix_ref.at[rows(dp_peer(d, 1) * ROWS, ROWS)], mix_far, own_s.at[2]
    )
    fetch_n1.start()
    fetch_far.start()
    fetch_mix.start()

    def along_x(source, landing, send, recv):
        copies = {}
        for k in (3, 7, 5, 2, 6, 4):
            block = rows(dp_peer(d, k) * ROWS, ROWS)
            copies[k] = copy_to(
                source.at[block],
                landing.at[k],
                send.at[k],
                recv.at[k],
                (dp_peer(d, k - k % 2), s),
            )
        return copies

    def partner_sum(copies, own, landing, index):
        for k in (3, 7, 5):
            copies[k].wait_recv()
        total = own.astype(F32)
        for k in (3, 7, 5):
            total = total + landing[k].astype(F32)
        zout[index] = total.astype(BF16)
        return copy_to(
            zout.at[index],
            zin.at[index],
            zz_s.at[index],
            zz_r.at[index],
            (dp_peer(d, 1), s),
        )

    def full_sum(copies, beside, own, landing, index):
        for k in (2, 6, 4):
            copies[k].wait_recv()
        total = own.astype(F32)
        for k in (2, 6, 4):
            total = total + landing[k].astype(F32)
        beside.wait_recv()
        return total + zin[index].astype(F32)

    apart = rows(dp_peer(d, 1) * ROWS, ROWS)
    gates = gates_ref[...]
    dgate = dgate_ref[...]
    inner = jnp.sum(gates * dgate, -1, keepdims=True)
    dlogits = (gates * (dgate - inner)).astype(BF16)
    router = jnp.concatenate(
        [packs_ref[8:24, :], jnp.zeros((ROWS - 16, D), F32)], 0
    ).astype(BF16)
    dn2 = dn2_ref[...] + dot_nn(dlogits, router)
    h = h_ref[...]
    r2 = lax.rsqrt(jnp.mean(h * h, -1, keepdims=True) + EPSILON)
    c = dn2 * packs_ref[1:2, :]
    dh = cot_ref[...].astype(F32) + r2 * c - h * (
        r2 * r2 * r2 * jnp.mean(c * h, -1, keepdims=True)
    )
    da = dh.astype(BF16)
    dot_own[...] = dot_nt(wouts_ref[...], da).astype(BF16)
    moves = []
    for k in SEQ_ORDER:
        to = seq_peer(s, k)
        moves.append(
            copy_to(
                dot_own.at[rows(to * HD, HD)], dot_all.at[:, mine], do_s.at[k], do_r.at[k], (d, to)
            )
        )
    dot_all[:, mine] = dot_own[head]
    begin_scatter()

    sides = {}
    for k in (1, 2, 6, 4):
        sides[k] = copy_to(
            perm_ref.at[side],
            perms_ref.at[side, lanes],
            w_s.at[k],
            w_r.at[k],
            (dp_peer(d, k), s),
        )
    perms_ref[side, lanes] = perm_ref[side]
    gop[...] = dot_nn(o_ref[...], da).astype(BF16)
    router_grad = dot_tn(dlogits, n2_ref[...])[0:16].astype(BF16)
    gain_two = jnp.sum(dn2 * h * r2, 0, keepdims=True)
    k_nat[...] = jnp.transpose(qkv_ref[HD : 2 * HD].astype(F32)).astype(BF16)
    v_nat[...] = jnp.transpose(qkv_ref[2 * HD :].astype(F32)).astype(BF16)
    for copy in moves:
        copy.wait_recv()
    blocks = LENGTH // QBLOCK
    for block in reversed(range(blocks)):
        begin, end = block * QBLOCK, (block + 1) * QBLOCK
        query = qkv_ref[0:HD, begin:end]
        grad = dot_all[:, begin:end]
        scores = dot_nn(k_nat[0:end], query)
        probs = jnp.exp2(scores * (MULT * LOG2E) - lse_ref[:, begin:end] * LOG2E)
        low = probs[begin:]
        key = lax.broadcasted_iota(jnp.int32, low.shape, 0)
        pos = lax.broadcasted_iota(jnp.int32, low.shape, 1)
        low = jnp.where(key <= pos, low, 0.0)
        if block:
            probs = jnp.concatenate([probs[:begin], low], 0)
        else:
            probs = low
        pgrad = dot_nn(v_nat[0:end], grad)
        inner = jnp.sum(probs * pgrad, 0, keepdims=True)
        ds = (probs * (pgrad - inner)).astype(BF16)
        dv = dot_nt(grad, probs.astype(BF16))
        dk = dot_nt(query, ds)
        if block == blocks - 1:
            dv_acc[...] = dv
            dk_acc[...] = dk
        else:
            dv_acc[:, 0:end] += dv
            dk_acc[:, 0:end] += dk
        dq_acc[:, begin:end] = dot_nn(qkv_ref[HD : 2 * HD, 0:end], ds)
        if block == 3:
            mid_scatter(4)
            sides[1].wait_recv()
            next_to = perms_ref.at[side, rows(dp_peer(d, 1) * ROWS, ROWS)]
            for k in (3, 7, 5):
                sides[k] = copy_to(
                    next_to, next_to, w_s.at[k], w_r.at[k], (dp_peer(d, k - 1), s)
                )
            gos = along_x(gop, recv_g, go_s, go_r)
        if block == 2:
            mid_scatter(0)
    kv_own[0:HD] = (dk_acc[...] * MULT).astype(BF16)
    kv_own[HD:] = dv_acc[...].astype(BF16)
    swap = copy_to(kv_own, kv_mate, kv_s.at[0], kv_r.at[0], mate)
    cosine = cos_ref[...]
    sine = sin_ref[...]

    def unturn(v):
        a, b = v[:HALF], v[HALF:]
        return jnp.concatenate([a * cosine + b * sine, b * cosine - a * sine], 0)

    dp_own[0:HD] = unturn((dq_acc[...] * MULT).astype(BF16).astype(F32)).astype(BF16)
    swap.wait_recv()
    both = kv_own[...].astype(F32) + kv_mate[...].astype(F32)
    dp_own[HD:] = jnp.where(core == 0, unturn(both[:HD]), both[HD:]).astype(BF16)
    shares = []
    slot = rows(s * ROWS, ROWS)
    for k in SEQ_ORDER:
        to = seq_peer(s, k)
        shares.append(
            copy_to(
                dp_own.at[:, rows(to * ROWS, ROWS)],
                dp_tok.at[slot],
                dp_s.at[k],
                dp_r.at[k],
                (d, to),
            )
        )
    dp_tok[slot] = dp_own[:, mine]
    part_e[...] = end_scatter(4).astype(BF16)
    beside = copy_to(part_e, recv_z, z_s.at[0], z_r.at[0], (d, chip_peer(s, 4)))
    fetch_n1.wait()
    finp[0:128, :] = dot_nn(dp_own[...], n1_ref[...]).astype(BF16)

    total = end_scatter(0)
    beside.wait_recv()
    sum_e[...] = (total + recv_z[...].astype(F32)).astype(BF16)
    gather = {}
    spare = {}
    own_e = full_ref.at[core, slab(0)]
    keep = pltpu.make_async_copy(sum_e, own_e, fs_s.at[8])
    keep.start()
    for k in (4, 1, 3):
        gather[k] = copy_to(sum_e, own_e, ag_s.at[k], ag_r.at[k], (d, chip_peer(s, k)))
    spare[0] = copy_to(sum_e, own_e, fs_s.at[0], fs_r.at[0], mate)

    def arrived(k):
        gather[k].wait_recv()
        if k in (2, 6):
            gather[8 + k // 6].wait_recv()
        at = full_ref.at[core, slab(chip_back(k))]
        spare[k] = copy_to(at, at, fs_s.at[k], fs_r.at[k], mate)
        if k % 2:
            low = k % 4 == 1
            start = lax.div(chip_peer(s, chip_back(k)), 2) * ROWS
            piece = full_ref.at[core, rows(start if low else start + 64, 64)]
            index = k + 1 if low else 7 + (k + 1) // 4
            gather[index] = copy_to(
                piece, piece, ag_s.at[index], ag_r.at[index], (d, chip_peer(s, k % 4))
            )
        return at

    for copy in shares:
        copy.wait_recv()
    for k in (2, 6, 4, 3, 7, 5):
        sides[k].wait_recv()
    share = copy_to(perms_ref.at[side], perms_ref.at[side], l_s.at[0], l_r.at[0], mate)
    share.wait_recv()
    dn1 = dot_tn(dp_tok[...], perms_ref[...])
    x = x_ref[...].astype(F32)
    r1 = lax.rsqrt(jnp.mean(x * x, -1, keepdims=True) + EPSILON)
    c = dn1 * packs_ref[0:1, :]
    gx_ref[...] = dh + r1 * c - x * (r1 * r1 * r1 * jnp.mean(c * x, -1, keepdims=True))
    gain_one = jnp.sum(dn1 * x * r1, 0, keepdims=True)
    finp[128:144, :] = router_grad
    finp[144:160, :] = jnp.concatenate([gain_two, gain_one, jnp.zeros((14, D), F32)], 0).astype(
        BF16
    )
    finals = []
    for k in DP_ORDER:
        to = dp_peer(d, k)
        finals.append(
            copy_to(
                finp.at[:, rows(to * ROWS, ROWS)], recv_f.at[k], f_s.at[k], f_r.at[k], (to, s)
            )
        )
    mixes = along_x(mix_ref, recv_m, m_s, m_r)
    go_z = partner_sum(gos, gop[apart], recv_g, 0)
    partner = arrived(4)
    for k in (5, 7):
        gather[k] = copy_to(partner, partner, ag_s.at[k], ag_r.at[k], (d, chip_peer(s, k - 4)))
    for k in (1, 3):
        arrived(k)
    gosum[...] = full_sum(gos, go_z, gop[here], recv_g, 0).astype(BF16)
    pieces = []
    for k in CHIP_ORDER:
        pieces.append(
            copy_to(
                gosum.at[:, slab(k)], gopart.at[k], gp_s.at[k], gp_r.at[k], (d, chip_peer(s, k))
            )
        )
    for copy in finals:
        copy.wait_recv()
    total = finp[:, here].astype(F32)
    for k in range(1, 8):
        total = total + recv_f[k].astype(F32)
    fin_ref[s] = total.astype(BF16)
    tails = {}
    for k in CHIP_ORDER:
        tails[k] = copy_to(
            fin_ref.at[s], fin_ref.at[s], t_s.at[k], t_r.at[k], (d, chip_peer(s, k))
        )
    passed = [copy_to(fin_ref.at[s], fin_ref.at[s], u_s.at[0], u_r.at[0], mate)]
    for k in (5, 7):
        arrived(k)
    for copy in pieces:
        copy.wait_recv()
    total = gosum[:, slab(0)].astype(F32)
    for k in range(1, 8):
        total = total + gopart[k].astype(F32)
    gomate[0] = total
    pair = copy_to(gomate.at[0], gomate.at[1], gm_s.at[0], gm_r.at[0], mate)
    pair.wait_recv()
    gout_ref[:, slab(0)] = (total + gomate[1]).astype(BF16)
    wholes = []
    for k in CHIP_ORDER:
        wholes.append(
            copy_to(
                gout_ref.at[:, slab(0)],
                gout_ref.at[:, slab(0)],
                gq_s.at[k],
                gq_r.at[k],
                (d, chip_peer(s, k)),
            )
        )
    fetch_mix.wait()
    fetch_far.wait()
    mix_z = partner_sum(mixes, mix_far[...], recv_m, 1)
    for k in CHIP_ORDER:
        tails[k].wait_recv()
        at = fin_ref.at[chip_peer(s, chip_back(k))]
        passed.append(copy_to(at, at, u_s.at[k], u_r.at[k], mate))
    for k in (2, 6):
        arrived(k)
    total = h + full_sum(mixes, mix_z, mix_own[...], recv_m, 1)
    out_ref[...] = total.astype(BF16)
    keep.wait()
    for copy in wholes + passed:
        copy.wait_recv()
    for copy in spare.values():
        copy.wait_recv()
    share.wait_send()
    beside.wait_send()
    go_z.wait_send()
    mix_z.wait_send()
    for copies in (gos, mixes, sides, halves, wholes_e, gather, spare, tails):
        for copy in copies.values():
            copy.wait_send()
    for copy in moves + [swap, pair] + shares + pieces + finals + wholes + passed:
        copy.wait_send()


def sems(count):
    return pltpu.SemaphoreType.DMA((count,))


def params(identity):
    return pltpu.CompilerParams(
        collective_id=identity, has_side_effects=True, vmem_limit_bytes=60 << 20
    )


def angle_tables():
    freqs = np.float32(THETA) ** (
        -(np.arange(HALF, dtype=np.float32) * np.float32(2.0) / np.float32(HD))
    )
    angles = freqs.astype(np.float32)[:, None] * np.arange(LENGTH, dtype=np.float32)[None, :]
    angles = angles.astype(np.float64)
    return np.cos(angles).astype(np.float32), np.sin(angles).astype(np.float32)


def sds(shape, dtype):
    return jax.ShapeDtypeStruct(shape, dtype)


def shards(tokens, w_qkv, w_out, w_router, gain_attn, gain_moe, experts, routes, cotangent):
    cosine, sine = angle_tables()
    cosine, sine = jnp.asarray(cosine), jnp.asarray(sine)
    pack = jnp.concatenate(
        [
            gain_attn.astype(F32)[None],
            gain_moe.astype(F32)[None],
            jnp.zeros((6, ROWS), F32),
            w_router.astype(F32).T,
        ],
        0,
    )
    query_w = w_qkv[:, :D].reshape(ROWS, QH, HD)
    keys_w = w_qkv[:, D:].reshape(ROWS, 2, QH // 2, HD).transpose(0, 2, 1, 3).reshape(ROWS, QH, HD)
    perm = jnp.concatenate([query_w, keys_w], -1).reshape(ROWS, 2 * D).T

    n1, qkv, lse, o_tok, h, n2, gates, gates_t, packs, wouts, cots = pl.pallas_call(
        front_kernel,
        out_shape=(
            sds((LENGTH, D), BF16),
            sds((3 * HD, LENGTH), BF16),
            sds((1, LENGTH), F32),
            sds((D, ROWS), BF16),
            sds((ROWS, D), F32),
            sds((ROWS, D), BF16),
            sds((ROWS, ROWS), F32),
            sds((16, ROWS), F32),
            sds((24, D), F32),
            sds((D, D), BF16),
            sds((D, D), BF16),
        ),
        in_specs=[VMEM, VMEM, VMEM, VMEM, VMEM, VMEM, VMEM, VMEM],
        out_specs=(VMEM,) * 10 + (ANY,),
        scratch_shapes=[
            pltpu.VMEM((ROWS, D), BF16),
            pltpu.VMEM((HD, D), BF16),
            pltpu.VMEM((HD, LENGTH), BF16),
            pltpu.VMEM((LENGTH, HD), BF16),
        ]
        + [sems(8)] * 6
        + [sems(10)] * 2
        + [sems(8)] * 6
        + [sems(16)] * 2
        + [sems(2)] * 2
        + [sems(5)],
        compiler_params=params(1),
        name="front",
    )(tokens, pack, perm, w_out, cotangent, routes, cosine, sine)

    dn2, dgate, mix, expert_grads = pl.pallas_call(
        experts_kernel,
        out_shape=(
            sds((ROWS, D), F32),
            sds((ROWS, ROWS), F32),
            sds((D, D), BF16),
            sds((D, 3 * FF), BF16),
        ),
        in_specs=[VMEM] * 2 + [ANY] * 2,
        out_specs=(VMEM,) * 4,
        scratch_shapes=[
            pltpu.VMEM((D, D), BF16),
            pltpu.VMEM((2, D, 3 * FF), BF16),
            pltpu.VMEM((D, D), BF16),
            pltpu.VMEM((16, D), F32),
            pltpu.VMEM((D, D), BF16),
            pltpu.VMEM((16, D), F32),
            pltpu.VMEM((4, ROWS, D), BF16),
            pltpu.VMEM((4, ROWS, D), BF16),
            pltpu.VMEM((8, 16, ROWS), F32),
            pltpu.VMEM((D, 2 * FF), BF16),
            pltpu.VMEM((D, 2 * D), BF16),
            pltpu.VMEM((D, 2 * D), BF16),
            pltpu.VMEM((D, 3 * FF), BF16),
            pltpu.VMEM((D, 3 * FF), BF16),
        ]
        + [sems(10)] * 2
        + [sems(8)] * 2
        + [sems(4)] * 4
        + [sems(8)] * 2
        + [sems(1)] * 2
        + [sems(2)],
        compiler_params=params(2),
        name="experts",
    )(n2, gates_t, cots, experts)

    out, grad_x, grad_out, fin, grad_experts = pl.pallas_call(
        back_kernel,
        out_shape=(
            sds((ROWS, D), BF16),
            sds((ROWS, D), F32),
            sds((ROWS, D), BF16),
            sds((N_SEQ, 160, ROWS), BF16),
            sds((2, D, 3 * FF), BF16),
        ),
        in_specs=[VMEM] * 3 + [ANY] + [VMEM] * 7 + [ANY] + [VMEM] * 6,
        out_specs=(VMEM,) * 4 + (ANY,),
        scratch_shapes=[
            pltpu.VMEM((LENGTH, D), BF16),
            pltpu.VMEM((ROWS, D), BF16),
            pltpu.VMEM((ROWS, D), BF16),
            pltpu.VMEM((2 * D, D), BF16),
            pltpu.VMEM((8, 64, 3 * FF), BF16),
            pltpu.VMEM((8, ROWS, 3 * FF), BF16),
            pltpu.VMEM((8, ROWS, 3 * FF), BF16),
            pltpu.VMEM((ROWS, 3 * FF), BF16),
            pltpu.VMEM((ROWS, 3 * FF), BF16),
            pltpu.VMEM((ROWS, 3 * FF), BF16),
            pltpu.VMEM((8, ROWS, D), BF16),
            pltpu.VMEM((D, D), BF16),
            pltpu.VMEM((8, ROWS, D), BF16),
            pltpu.VMEM((2, ROWS, D), BF16),
            pltpu.VMEM((2, ROWS, D), BF16),
            pltpu.VMEM((ROWS, D), BF16),
            pltpu.VMEM((8, ROWS, ROWS), BF16),
            pltpu.VMEM((2, ROWS, ROWS), F32),
            pltpu.VMEM((D, ROWS), BF16),
            pltpu.VMEM((HD, LENGTH), BF16),
            pltpu.VMEM((LENGTH, HD), BF16),
            pltpu.VMEM((LENGTH, HD), BF16),
            pltpu.VMEM((HD, LENGTH), F32),
            pltpu.VMEM((HD, LENGTH), F32),
            pltpu.VMEM((HD, LENGTH), F32),
            pltpu.VMEM((ROWS, LENGTH), BF16),
            pltpu.VMEM((ROWS, LENGTH), BF16),
            pltpu.VMEM((ROWS, LENGTH), BF16),
            pltpu.VMEM((2 * D, ROWS), BF16),
            pltpu.VMEM((160, D), BF16),
            pltpu.VMEM((8, 160, ROWS), BF16),
        ]
        + [sems(8)] * 2
        + [sems(1)] * 2
        + [sems(8)] * 4
        + [sems(1)] * 2
        + [sems(10)] * 2
        + [sems(9)] * 2
        + [sems(8)] * 4
        + [sems(2)] * 2
        + [sems(3)]
        + [sems(8)] * 2
        + [sems(1)] * 2
        + [sems(8)] * 2
        + [sems(16)] * 2
        + [sems(1)] * 2
        + [sems(16)] * 2
        + [sems(8)] * 6,
        compiler_params=params(3),
        name="back",
    )(
        dn2, dgate, gates, mix, tokens, h, n2, cotangent, packs, wouts, perm,
        n1, qkv, lse, o_tok, cosine, sine, expert_grads,
    )

    grads = fin[:, :128].astype(F32)
    query_g = grads[:, :HD].reshape(D, ROWS).T
    keys_g = (
        grads[:, HD:].reshape(QH // 2, 2, HD, ROWS).transpose(3, 1, 0, 2).reshape(ROWS, D)
    )
    grad_qkv = jnp.concatenate([query_g, keys_g], -1)
    small = jnp.sum(fin[:, 128:].astype(F32), 0)
    return (
        out,
        grad_x,
        grad_qkv,
        grad_out.astype(F32),
        small[:16].T,
        small[17],
        small[16],
        grad_experts.astype(F32),
    )


def solution(mesh):
    placed = (
        P(("dp", "seq"), None),
        P("dp", None),
        P("dp", None),
        P("dp", None),
        P("dp"),
        P("dp"),
        P("dp", None, None),
        P(("dp", "seq"), None),
        P(("dp", "seq"), None),
    )
    return jax.shard_map(
        shards,
        mesh=mesh,
        in_specs=placed,
        out_specs=(
            P(("dp", "seq"), None),
            P(("dp", "seq"), None),
            P("dp", None),
            P("dp", None),
            P("dp", None),
            P("dp"),
            P("dp"),
            P("dp", None, None),
        ),
        check_vma=False,
    )
```

```python
import functools

import jax
import jax.numpy as jnp
import numpy as np
from jax import lax
from jax.experimental import pallas as pl
from jax.experimental.pallas import tpu as pltpu
from jax.sharding import PartitionSpec as P

D = 1024
QH = 16
HD = 64
HALF = 32
FF = 512
N_DP = 8
N_SEQ = 16
ROWS = 128
LENGTH = 2048
QBLOCK = 512

EPSILON = 1e-06
MULT = 0.015625
THETA = 10000.0
NEGATIVE = -1e30
LOG2E = 1.4426950408889634

F32 = jnp.float32
BF16 = jnp.bfloat16
MESH = pl.DeviceIdType.MESH
VMEM = pl.BlockSpec(memory_space=pltpu.VMEM)
ANY = pl.BlockSpec(memory_space=pl.ANY)

DP_ORDER = (1, 2, 6, 3, 7, 4, 5)
CHIP_ORDER = (4, 1, 3, 5, 7, 2, 6)


def dot_nn(a, b):
    return lax.dot_general(a, b, (((1,), (0,)), ((), ())), preferred_element_type=F32)


def dot_nt(a, b):
    return lax.dot_general(a, b, (((1,), (1,)), ((), ())), preferred_element_type=F32)


def dot_tn(a, b):
    return lax.dot_general(a, b, (((0,), (0,)), ((), ())), preferred_element_type=F32)


def dp_peer(d, k):
    return lax.rem(lax.div(d, 2) + k // 2, 4) * 2 + lax.rem(lax.rem(d, 2) + k % 2, 2)


def dp_back(k):
    return 2 * ((4 - k // 2) % 4) + k % 2


def chip_peer(s, k):
    z, y, c = lax.div(s, 8), lax.rem(lax.div(s, 2), 4), lax.rem(s, 2)
    return lax.rem(z + k // 4, 2) * 8 + lax.rem(y + k % 4, 4) * 2 + c


def chip_back(k):
    return 4 * (k // 4) + (4 - k % 4) % 4


def seq_peer(s, k):
    base = chip_peer(s, k // 2)
    c = lax.rem(s, 2)
    return base if k % 2 == 0 else base + 1 - 2 * c


SEQ_ORDER = tuple(2 * c + o for c in (0,) + CHIP_ORDER for o in (0, 1) if 2 * c + o)


def seq_back(k):
    return 2 * chip_back(k // 2) + k % 2


def sibling(s):
    return s + 1 - 2 * lax.rem(s, 2)


def copy_to(src, dst, send, recv, device):
    copy = pltpu.make_async_remote_copy(
        src_ref=src,
        dst_ref=dst,
        send_sem=send,
        recv_sem=recv,
        device_id=device,
        device_id_type=MESH,
    )
    copy.start()
    return copy


def greet(devices):
    barrier = pltpu.get_barrier_semaphore()
    for device in devices:
        pl.semaphore_signal(barrier, inc=1, device_id=device, device_id_type=MESH)
    pl.semaphore_wait(barrier, len(devices))


def rows(start, size):
    return pl.ds(pl.multiple_of(start, size), size)


def front_kernel(
    x_ref, pack_ref, perm_ref, wout_ref, cot_ref, routes_ref, cos_ref, sin_ref,
    n1_ref, qkv_ref, lse_ref, o_ref, h_ref, n2_ref, gates_ref, gates_t_ref, packs_ref, wouts_ref, cots_ref,
    sel_a, sel_b, o_own, k_nat,
    pack_s, pack_r, a_s, a_r, b_s, b_r, n1_s, n1_r, f_s, f_r, w_s, w_r, c_s, c_r, o_s, o_r, l_s, l_r, own_s,
):
    d, s = lax.axis_index("dp"), lax.axis_index("seq")
    core = lax.rem(s, 2)
    mate = (d, sibling(s))
    greet(
        [(dp_peer(d, k), s) for k in DP_ORDER] + [(d, seq_peer(s, k)) for k in SEQ_ORDER]
    )
    lanes = rows(d * ROWS, ROWS)
    small = []
    head_rows = rows(s * ROWS, ROWS)
    mate_rows = rows(sibling(s) * ROWS + HD, HD)
    for k in DP_ORDER:
        to = (dp_peer(d, k), s)
        small.append(copy_to(pack_ref, packs_ref.at[:, lanes], pack_s.at[k], pack_r.at[k], to))
    picks = []
    for k in DP_ORDER:
        to = (dp_peer(d, k), s)
        picks.append(copy_to(perm_ref.at[head_rows], sel_a.at[:, lanes], a_s.at[k], a_r.at[k], to))
        picks.append(copy_to(perm_ref.at[mate_rows], sel_b.at[:, lanes], b_s.at[k], b_r.at[k], to))
    own_a = pltpu.make_async_copy(perm_ref.at[head_rows], sel_a.at[:, lanes], own_s.at[0])
    own_b = pltpu.make_async_copy(perm_ref.at[mate_rows], sel_b.at[:, lanes], own_s.at[1])
    own_a.start()
    own_b.start()
    packs_ref[:, lanes] = pack_ref[...]
    x = x_ref[...].astype(F32)
    r1 = lax.rsqrt(jnp.mean(x * x, -1, keepdims=True) + EPSILON)
    for copy in small:
        copy.wait_recv()
    mine = rows(s * ROWS, ROWS)
    n1_ref[mine] = (x * r1 * packs_ref[0:1, :]).astype(BF16)
    direct = {}
    forwards = {0: copy_to(n1_ref.at[mine], n1_ref.at[mine], f_s.at[0], f_r.at[0], mate)}
    for k in (4, 1, 3):
        direct[k] = copy_to(
            n1_ref.at[mine], n1_ref.at[mine], n1_s.at[k], n1_r.at[k], (d, chip_peer(s, k))
        )
    half = rows(core * 512, 512)
    other = rows(dp_peer(d, 1) * ROWS, ROWS)

    def spread(source, place, send, recv):
        return {
            k: copy_to(source, place(lanes), send.at[k], recv.at[k], (dp_peer(d, k), s))
            for k in (1, 2, 6, 4)
        }

    def pass_on(copies, place, send, recv):
        copies[1].wait_recv()
        for k in (3, 7, 5):
            copies[k] = copy_to(
                place(other), place(other), send.at[k], recv.at[k], (dp_peer(d, k - 1), s)
            )

    def keep(source, place, k):
        copy = pltpu.make_async_copy(source, place(lanes), own_s.at[k])
        copy.start()
        return copy

    out_source, out_place = wout_ref.at[:, half], lambda at: wouts_ref.at[at, half]
    cot_place = lambda at: cots_ref.at[at]
    outs_w = spread(out_source, out_place, w_s, w_r)
    own_w = keep(out_source, out_place, 2)
    direct[4].wait_recv()
    partner = rows(chip_peer(s, 4) * ROWS, ROWS)
    forwards[4] = copy_to(n1_ref.at[partner], n1_ref.at[partner], f_s.at[4], f_r.at[4], mate)
    for k in (5, 7):
        direct[k] = copy_to(
            n1_ref.at[partner],
            n1_ref.at[partner],
            n1_s.at[k],
            n1_r.at[k],
            (d, chip_peer(s, k - 4)),
        )
    cots = spread(cot_ref, cot_place, c_s, c_r)
    own_c = keep(cot_ref, cot_place, 3)
    pass_on(outs_w, out_place, w_s, w_r)
    for copy in picks:
        copy.wait_recv()
    own_a.wait()
    own_b.wait()

    def project(chip):
        block = rows(chip * 256, 256)
        tokens = n1_ref[block]
        cosine = cos_ref[:, block]
        sine = sin_ref[:, block]

        def turn(v):
            a, b = v[:HALF], v[HALF:]
            return jnp.concatenate([a * cosine - b * sine, b * cosine + a * sine], 0)

        pa = dot_nt(sel_a[...], tokens)
        pb = dot_nt(sel_b[...], tokens)
        even = core == 0
        keys = jnp.where(even, pa[HD:], pb)
        values = jnp.where(even, pb, pa[HD:])
        qkv_ref[:, block] = jnp.concatenate([turn(pa[:HD]), turn(keys), values], 0).astype(BF16)

    last = 0
    for k in (4, 1, 3, 5, 7, 2, 6):
        start = chip_peer(s, chip_back(k)) * ROWS
        source = rows(start, ROWS)
        if k != 4:
            direct[k].wait_recv()
            if k in (2, 6):
                direct[8 + k // 6].wait_recv()
            else:
                low = k % 4 == 1
                piece = rows(start if low else start + 64, 64)
                index = k + 1 if low else 7 + (k + 1) // 4
                direct[index] = copy_to(
                    n1_ref.at[piece],
                    n1_ref.at[piece],
                    n1_s.at[index],
                    n1_r.at[index],
                    (d, chip_peer(s, k % 4)),
                )
            forwards[k] = copy_to(
                n1_ref.at[source], n1_ref.at[source], f_s.at[k], f_r.at[k], mate
            )
        forwards[last].wait_recv()
        project(lax.div(chip_peer(s, chip_back(last)), 2))
        last = k
        if k == 3:
            pass_on(cots, cot_place, c_s, c_r)
    forwards[last].wait_recv()
    project(lax.div(chip_peer(s, chip_back(last)), 2))

    k_nat[...] = jnp.transpose(qkv_ref[HD : 2 * HD].astype(F32)).astype(BF16)
    outs = []
    for block in range(LENGTH // QBLOCK):
        begin, end = block * QBLOCK, (block + 1) * QBLOCK
        query = qkv_ref[0:HD, begin:end]
        scores = dot_nn(k_nat[0:end], query)
        low = scores[begin:]
        key = lax.broadcasted_iota(jnp.int32, low.shape, 0)
        pos = lax.broadcasted_iota(jnp.int32, low.shape, 1)
        low = jnp.where(key <= pos, low, NEGATIVE)
        if block:
            scores = jnp.concatenate([scores[:begin], low], 0)
        else:
            scores = low
        top = jnp.max(scores, 0, keepdims=True)
        expo = jnp.exp2((scores - top) * (MULT * LOG2E))
        total = jnp.sum(expo, 0, keepdims=True)
        probs = (expo * (1.0 / total)).astype(BF16)
        lse_ref[:, begin:end] = top * MULT + jnp.log(total)
        o_own[:, begin:end] = dot_nn(qkv_ref[2 * HD :, 0:end], probs).astype(BF16)
    place = rows(s * HD, HD)
    for k in SEQ_ORDER:
        to = seq_peer(s, k)
        outs.append(
            copy_to(
                o_own.at[:, rows(to * ROWS, ROWS)], o_ref.at[place], o_s.at[k], o_r.at[k], (d, to)
            )
        )
    o_ref[place] = o_own[:, mine]
    for k in (2, 6, 4, 3, 7, 5):
        outs_w[k].wait_recv()
    own_w.wait()
    share = copy_to(wouts_ref.at[:, half], wouts_ref.at[:, half], l_s.at[0], l_r.at[0], mate)
    for copy in outs:
        copy.wait_recv()
    share.wait_recv()
    mixed = jnp.transpose(o_ref[...].astype(F32)).astype(BF16)
    h = x + dot_nn(mixed, wouts_ref[...])
    h_ref[...] = h
    r2 = lax.rsqrt(jnp.mean(h * h, -1, keepdims=True) + EPSILON)
    n2 = (h * r2 * packs_ref[1:2, :]).astype(BF16)
    n2_ref[...] = n2
    router = jnp.concatenate(
        [packs_ref[8:24, :], jnp.zeros((ROWS - 16, D), F32)], 0
    ).astype(BF16)
    logits = dot_nt(n2, router)
    label = lax.broadcasted_iota(jnp.int32, (ROWS, ROWS), 0)
    named = jnp.zeros((ROWS, ROWS), F32)
    for j in range(8):
        named = jnp.where(routes_ref[j : j + 1, :] == label, 1.0, named)
    chosen = jnp.transpose(named) > 0.0
    masked = jnp.where(chosen, logits, NEGATIVE)
    expo = jnp.where(chosen, jnp.exp(masked - jnp.max(masked, -1, keepdims=True)), 0.0)
    gates = expo / jnp.sum(expo, -1, keepdims=True)
    gates_ref[...] = gates
    gates_t_ref[...] = jnp.transpose(gates)[0:16]

    for k in (2, 6, 4, 3, 7, 5):
        cots[k].wait_recv()
    own_c.wait()
    for copies in (direct, forwards, outs_w, cots):
        for copy in copies.values():
            copy.wait_send()
    for copy in small + picks + outs:
        copy.wait_send()
    share.wait_send()


def experts_kernel(
    n2_ref, gates_ref, cots_hbm, exp_hbm,
    dn2_ref, dgate_ref, mix_ref, grad_ref,
    cots_ref, exp_ref, n2s, gs, part, dgp, recv_z, recv, recvg, acts, dgus, dys, for_mate, from_mate,
    n_s, n_r, g_s, g_r, z_s, z_r, d_s, d_r, e_s, e_r, m_s, m_r, own_s,
):
    d, s = lax.axis_index("dp"), lax.axis_index("seq")
    core = lax.rem(s, 2)
    mate = (d, sibling(s))
    fetches = [
        pltpu.make_async_copy(exp_hbm, exp_ref, own_s.at[0]),
        pltpu.make_async_copy(cots_hbm, cots_ref, own_s.at[1]),
    ]
    for copy in fetches:
        copy.start()
    greet([(dp_peer(d, k), s) for k in DP_ORDER] + [mate])
    mine = rows(d * ROWS, ROWS)
    other = rows(dp_peer(d, 1) * ROWS, ROWS)
    gathers = {}
    gate_gathers = {}
    for k in DP_ORDER:
        gate_gathers[k] = copy_to(
            gates_ref, gs.at[:, mine], g_s.at[k], g_r.at[k], (dp_peer(d, k), s)
        )
    for k in (1, 2, 6):
        gathers[k] = copy_to(n2_ref, n2s.at[mine], n_s.at[k], n_r.at[k], (dp_peer(d, k), s))
    n2s[mine] = n2_ref[...]
    gs[:, mine] = gates_ref[...]
    gathers[1].wait_recv()
    for k in (3, 7):
        gathers[k] = copy_to(
            n2s.at[other], n2s.at[other], n_s.at[k], n_r.at[k], (dp_peer(d, k - 1), s)
        )
    x = lax.div(d, 2)
    for copy in fetches:
        copy.wait()
    backs = []
    pairs = {}
    sums = {}
    z = lax.rem(d, 2)

    def onward(turn):
        pairs[turn].wait_recv()
        block = rows(dp_peer(d, 2 * turn) * ROWS, ROWS)
        part[block] = (part[block].astype(F32) + recv_z[turn].astype(F32)).astype(BF16)
        if turn:
            sums[turn] = copy_to(
                part.at[block],
                recv.at[turn],
                d_s.at[turn],
                d_r.at[turn],
                (dp_peer(d, 2 * turn), s),
            )

    for step, turn in enumerate((0, 1, 3, 2)):
        if step == 1:
            for k in (2, 6, 3, 7):
                gathers[k].wait_recv()
                start = dp_peer(d, dp_back(k)) * ROWS
                low = k < 4
                piece = rows(start if low else start + 64, 64)
                index = k + 2
                gathers[index] = copy_to(
                    n2s.at[piece],
                    n2s.at[piece],
                    n_s.at[index],
                    n_r.at[index],
                    (dp_peer(d, 2 if low else 6), s),
                )
        for z_off in (0, 1):
            k = 2 * turn + z_off
            if k:
                gate_gathers[dp_back(k)].wait_recv()
            if turn == 2:
                gathers[k].wait_recv()
                gathers[k + 4].wait_recv()
        place = rows(lax.rem(x + turn, 4) * 256, 256)
        tokens = n2s[place]
        cot = cots_ref[place].astype(F32)
        gates = jnp.transpose(jnp.concatenate([gs[:, place], jnp.zeros((ROWS - 16, 256), F32)], 0))
        lane = lax.broadcasted_iota(jnp.int32, gates.shape, 1)
        dn2 = jnp.zeros((256, D), F32)
        mix = jnp.zeros((256, D), F32)
        dgate = jnp.zeros(gates.shape, F32)
        for e in range(2):
            up_w = exp_ref[e, :, 0 : 2 * FF]
            down_w = exp_ref[e, :, 2 * FF :]
            here = lane == 2 * d + e
            gate = jnp.sum(jnp.where(here, gates, 0.0), -1, keepdims=True)
            gu = dot_nn(tokens, up_w)
            g, u = gu[:, :FF], gu[:, FF:]
            sigmoid = 1.0 / (1.0 + jnp.exp(-g))
            silu = g * sigmoid
            act = (silu * u).astype(BF16)
            acts[place, e * FF : (e + 1) * FF] = act
            y = dot_nt(act, down_w)
            dgate = jnp.where(here, jnp.sum(cot * y, -1, keepdims=True), dgate)
            mix = mix + gate * y
            dy = (gate * cot).astype(BF16)
            dys[place, e * D : (e + 1) * D] = dy
            dact = dot_nn(dy, down_w)
            dg = dact * u * (sigmoid * (1.0 + g * (1.0 - sigmoid)))
            du = dact * silu
            dgu = jnp.concatenate([dg, du], 1).astype(BF16)
            dgus[place, e * D : (e + 1) * D] = dgu
            dn2 = dn2 + dot_nt(dgu, up_w)
        mix_ref[place] = mix.astype(BF16)
        part[place] = dn2.astype(BF16)
        dgp[:, place] = jnp.transpose(dgate)[0:16]
        away = rows(dp_peer(d, 2 * turn + 1) * ROWS, ROWS)
        pairs[turn] = copy_to(
            part.at[away], recv_z.at[turn], z_s.at[turn], z_r.at[turn], (dp_peer(d, 1), s)
        )
        for z_off in (0, 1):
            k = 2 * turn + z_off
            if k:
                to = dp_peer(d, k)
                block = rows(to * ROWS, ROWS)
                backs.append(
                    copy_to(dgp.at[:, block], recvg.at[k], e_s.at[k], e_r.at[k], (to, s))
                )
        if step:
            onward((0, 1, 3, 2)[step - 1])

    def grads(e):
        wide = rows(e * D, D)
        return (
            dot_tn(n2s[...], dgus[:, wide]),
            dot_tn(dys[:, wide], acts[:, rows(e * FF, FF)]),
        )

    first, second = grads(1 - core)
    for_mate[:, 0 : 2 * FF] = first.astype(BF16)
    for_mate[:, 2 * FF :] = second.astype(BF16)
    swap = copy_to(for_mate, from_mate, m_s.at[0], m_r.at[0], mate)
    onward(2)
    first, second = grads(core)
    swap.wait_recv()
    grad_ref[:, 0 : 2 * FF] = (first + from_mate[:, 0 : 2 * FF].astype(F32)).astype(BF16)
    grad_ref[:, 2 * FF :] = (second + from_mate[:, 2 * FF :].astype(F32)).astype(BF16)
    for copy in list(sums.values()) + backs:
        copy.wait_recv()
    total = part[mine].astype(F32)
    for k in range(1, 4):
        total = total + recv[k].astype(F32)
    totalg = dgp[:, mine]
    for k in range(1, 8):
        totalg = totalg + recvg[k]
    dn2_ref[...] = total
    dgate_ref[...] = jnp.transpose(
        jnp.concatenate([totalg, jnp.zeros((ROWS - 16, ROWS), F32)], 0)
    )
    for copies in (gathers, gate_gathers, pairs, sums):
        for copy in copies.values():
            copy.wait_send()
    for copy in backs:
        copy.wait_send()
    swap.wait_send()


def back_kernel(
    dn2_ref, dgate_ref, gates_ref, mix_ref, x_ref, h_ref, n2_ref, cot_ref, packs_ref, wouts_ref, perm_ref,
    n1_hbm, qkv_ref, lse_ref, o_ref, cos_ref, sin_ref, ge_ref,
    out_ref, gx_ref, gout_ref, fin_ref, full_ref,
    n1_ref, mix_own, mix_far, perms_ref, half_e, whole_e, stage_e, recv_z, part_e, sum_e, recv_m, gop, recv_g, zout, zin, gosum, gopart, gomate, dot_own, dot_all, k_nat, v_nat, dq_acc, dk_acc, dv_acc, kv_own, kv_mate,
    dp_own, dp_tok, finp, recv_f,
    w_s, w_r, l_s, l_r, b_s, b_r, c_s, c_r, z_s, z_r, ag_s, ag_r, fs_s, fs_r,
    m_s, m_r, go_s, go_r, zz_s, zz_r, own_s, gp_s, gp_r, gm_s, gm_r, gq_s, gq_r, do_s, do_r, kv_s, kv_r, dp_s, dp_r, f_s, f_r, t_s, t_r, u_s, u_r,
):
    d, s = lax.axis_index("dp"), lax.axis_index("seq")
    core = lax.rem(s, 2)
    greet(
        [(dp_peer(d, k), s) for k in DP_ORDER] + [(d, seq_peer(s, k)) for k in SEQ_ORDER]
    )
    here = rows(d * ROWS, ROWS)
    mine = rows(s * ROWS, ROWS)
    head = rows(s * HD, HD)
    mate = (d, sibling(s))

    def slab(k):
        return rows(lax.div(chip_peer(s, k), 2) * ROWS, ROWS)

    lanes = rows(d * ROWS, ROWS)
    side = rows(core * 1024, 1024)

    halves = {}
    wholes_e = {}

    def begin_scatter():
        for base in (4, 0):
            far = lax.div(chip_peer(s, base + 2), 2) * ROWS
            for low in (True, False):
                k = base + (1 if low else 3)
                piece = rows(far if low else far + 64, 64)
                halves[k] = copy_to(
                    ge_ref.at[piece],
                    half_e.at[k],
                    b_s.at[k],
                    b_r.at[k],
                    (d, chip_peer(s, k % 4)),
                )

    def mid_scatter(base):
        for low in (True, False):
            k = base + (1 if low else 3)
            halves[k].wait_recv()
            start = lax.div(chip_peer(s, k), 2) * ROWS
            first, second = rows(start, 64), rows(start + 64, 64)
            added = half_e[k].astype(F32)
            if low:
                stage_e[k, 0:64] = (ge_ref[first].astype(F32) + added).astype(BF16)
                stage_e[k, 64:128] = ge_ref[second]
            else:
                stage_e[k, 0:64] = ge_ref[first]
                stage_e[k, 64:128] = (ge_ref[second].astype(F32) + added).astype(BF16)
            wholes_e[k] = copy_to(
                stage_e.at[k], whole_e.at[k], c_s.at[k], c_r.at[k], (d, chip_peer(s, k % 4))
            )

    def end_scatter(base):
        wholes_e[base + 1].wait_recv()
        wholes_e[base + 3].wait_recv()
        return (
            ge_ref[slab(base)].astype(F32)
            + whole_e[base + 1].astype(F32)
            + whole_e[base + 3].astype(F32)
        )

    fetch_n1 = pltpu.make_async_copy(n1_hbm, n1_ref, own_s.at[0])
    fetch_mix = pltpu.make_async_copy(mix_ref.at[here], mix_own, own_s.at[1])
    fetch_far = pltpu.make_async_copy(
        mix_ref.at[rows(dp_peer(d, 1) * ROWS, ROWS)], mix_far, own_s.at[2]
    )
    fetch_n1.start()
    fetch_far.start()
    fetch_mix.start()

    def along_x(source, landing, send, recv):
        copies = {}
        for k in (3, 7, 5, 2, 6, 4):
            block = rows(dp_peer(d, k) * ROWS, ROWS)
            copies[k] = copy_to(
                source.at[block],
                landing.at[k],
                send.at[k],
                recv.at[k],
                (dp_peer(d, k - k % 2), s),
            )
        return copies

    def partner_sum(copies, own, landing, index):
        for k in (3, 7, 5):
            copies[k].wait_recv()
        total = own.astype(F32)
        for k in (3, 7, 5):
            total = total + landing[k].astype(F32)
        zout[index] = total.astype(BF16)
        return copy_to(
            zout.at[index],
            zin.at[index],
            zz_s.at[index],
            zz_r.at[index],
            (dp_peer(d, 1), s),
        )

    def full_sum(copies, beside, own, landing, index):
        for k in (2, 6, 4):
            copies[k].wait_recv()
        total = own.astype(F32)
        for k in (2, 6, 4):
            total = total + landing[k].astype(F32)
        beside.wait_recv()
        return total + zin[index].astype(F32)

    apart = rows(dp_peer(d, 1) * ROWS, ROWS)
    begin_scatter()
    gates = gates_ref[...]
    dgate = dgate_ref[...]
    inner = jnp.sum(gates * dgate, -1, keepdims=True)
    dlogits = (gates * (dgate - inner)).astype(BF16)
    router = jnp.concatenate(
        [packs_ref[8:24, :], jnp.zeros((ROWS - 16, D), F32)], 0
    ).astype(BF16)
    dn2 = dn2_ref[...] + dot_nn(dlogits, router)
    h = h_ref[...]
    r2 = lax.rsqrt(jnp.mean(h * h, -1, keepdims=True) + EPSILON)
    c = dn2 * packs_ref[1:2, :]
    dh = cot_ref[...].astype(F32) + r2 * c - h * (
        r2 * r2 * r2 * jnp.mean(c * h, -1, keepdims=True)
    )
    da = dh.astype(BF16)
    dot_own[...] = dot_nt(wouts_ref[...], da).astype(BF16)
    moves = []
    for k in SEQ_ORDER:
        to = seq_peer(s, k)
        moves.append(
            copy_to(
                dot_own.at[rows(to * HD, HD)], dot_all.at[:, mine], do_s.at[k], do_r.at[k], (d, to)
            )
        )
    dot_all[:, mine] = dot_own[head]

    sides = {}
    for k in (1, 2, 6, 4):
        sides[k] = copy_to(
            perm_ref.at[side],
            perms_ref.at[side, lanes],
            w_s.at[k],
            w_r.at[k],
            (dp_peer(d, k), s),
        )
    perms_ref[side, lanes] = perm_ref[side]
    gop[...] = dot_nn(o_ref[...], da).astype(BF16)
    router_grad = dot_tn(dlogits, n2_ref[...])[0:16].astype(BF16)
    gain_two = jnp.sum(dn2 * h * r2, 0, keepdims=True)
    k_nat[...] = jnp.transpose(qkv_ref[HD : 2 * HD].astype(F32)).astype(BF16)
    v_nat[...] = jnp.transpose(qkv_ref[2 * HD :].astype(F32)).astype(BF16)
    mid_scatter(4)
    for copy in moves:
        copy.wait_recv()
    blocks = LENGTH // QBLOCK
    for block in reversed(range(blocks)):
        begin, end = block * QBLOCK, (block + 1) * QBLOCK
        query = qkv_ref[0:HD, begin:end]
        grad = dot_all[:, begin:end]
        scores = dot_nn(k_nat[0:end], query)
        probs = jnp.exp2(scores * (MULT * LOG2E) - lse_ref[:, begin:end] * LOG2E)
        low = probs[begin:]
        key = lax.broadcasted_iota(jnp.int32, low.shape, 0)
        pos = lax.broadcasted_iota(jnp.int32, low.shape, 1)
        low = jnp.where(key <= pos, low, 0.0)
        if block:
            probs = jnp.concatenate([probs[:begin], low], 0)
        else:
            probs = low
        pgrad = dot_nn(v_nat[0:end], grad)
        inner = jnp.sum(probs * pgrad, 0, keepdims=True)
        ds = (probs * (pgrad - inner)).astype(BF16)
        dv = dot_nt(grad, probs.astype(BF16))
        dk = dot_nt(query, ds)
        if block == blocks - 1:
            dv_acc[...] = dv
            dk_acc[...] = dk
        else:
            dv_acc[:, 0:end] += dv
            dk_acc[:, 0:end] += dk
        dq_acc[:, begin:end] = dot_nn(qkv_ref[HD : 2 * HD, 0:end], ds)
        if block == 3:
            mid_scatter(0)
            sides[1].wait_recv()
            next_to = perms_ref.at[side, rows(dp_peer(d, 1) * ROWS, ROWS)]
            for k in (3, 7, 5):
                sides[k] = copy_to(
                    next_to, next_to, w_s.at[k], w_r.at[k], (dp_peer(d, k - 1), s)
                )
            gos = along_x(gop, recv_g, go_s, go_r)
    kv_own[0:HD] = (dk_acc[...] * MULT).astype(BF16)
    kv_own[HD:] = dv_acc[...].astype(BF16)
    swap = copy_to(kv_own, kv_mate, kv_s.at[0], kv_r.at[0], mate)
    part_e[...] = end_scatter(4).astype(BF16)
    beside = copy_to(part_e, recv_z, z_s.at[0], z_r.at[0], (d, chip_peer(s, 4)))
    cosine = cos_ref[...]
    sine = sin_ref[...]

    def unturn(v):
        a, b = v[:HALF], v[HALF:]
        return jnp.concatenate([a * cosine + b * sine, b * cosine - a * sine], 0)

    dp_own[0:HD] = unturn((dq_acc[...] * MULT).astype(BF16).astype(F32)).astype(BF16)
    swap.wait_recv()
    both = kv_own[...].astype(F32) + kv_mate[...].astype(F32)
    dp_own[HD:] = jnp.where(core == 0, unturn(both[:HD]), both[HD:]).astype(BF16)
    shares = []
    slot = rows(s * ROWS, ROWS)
    for k in SEQ_ORDER:
        to = seq_peer(s, k)
        shares.append(
            copy_to(
                dp_own.at[:, rows(to * ROWS, ROWS)],
                dp_tok.at[slot],
                dp_s.at[k],
                dp_r.at[k],
                (d, to),
            )
        )
    dp_tok[slot] = dp_own[:, mine]
    fetch_n1.wait()
    finp[0:128, :] = dot_nn(dp_own[...], n1_ref[...]).astype(BF16)

    total = end_scatter(0)
    beside.wait_recv()
    sum_e[...] = (total + recv_z[...].astype(F32)).astype(BF16)
    gather = {}
    spare = {}
    own_e = full_ref.at[core, slab(0)]
    keep = pltpu.make_async_copy(sum_e, own_e, fs_s.at[8])
    keep.start()
    for k in (4, 1, 3):
        gather[k] = copy_to(sum_e, own_e, ag_s.at[k], ag_r.at[k], (d, chip_peer(s, k)))
    spare[0] = copy_to(sum_e, own_e, fs_s.at[0], fs_r.at[0], mate)

    def arrived(k):
        gather[k].wait_recv()
        if k in (2, 6):
            gather[8 + k // 6].wait_recv()
        at = full_ref.at[core, slab(chip_back(k))]
        spare[k] = copy_to(at, at, fs_s.at[k], fs_r.at[k], mate)
        if k % 2:
            low = k % 4 == 1
            start = lax.div(chip_peer(s, chip_back(k)), 2) * ROWS
            piece = full_ref.at[core, rows(start if low else start + 64, 64)]
            index = k + 1 if low else 7 + (k + 1) // 4
            gather[index] = copy_to(
                piece, piece, ag_s.at[index], ag_r.at[index], (d, chip_peer(s, k % 4))
            )
        return at

    for copy in shares:
        copy.wait_recv()
    for k in (2, 6, 4, 3, 7, 5):
        sides[k].wait_recv()
    share = copy_to(perms_ref.at[side], perms_ref.at[side], l_s.at[0], l_r.at[0], mate)
    share.wait_recv()
    dn1 = dot_tn(dp_tok[...], perms_ref[...])
    x = x_ref[...].astype(F32)
    r1 = lax.rsqrt(jnp.mean(x * x, -1, keepdims=True) + EPSILON)
    c = dn1 * packs_ref[0:1, :]
    gx_ref[...] = dh + r1 * c - x * (r1 * r1 * r1 * jnp.mean(c * x, -1, keepdims=True))
    gain_one = jnp.sum(dn1 * x * r1, 0, keepdims=True)
    finp[128:144, :] = router_grad
    finp[144:160, :] = jnp.concatenate([gain_two, gain_one, jnp.zeros((14, D), F32)], 0).astype(
        BF16
    )
    finals = []
    for k in DP_ORDER:
        to = dp_peer(d, k)
        finals.append(
            copy_to(
                finp.at[:, rows(to * ROWS, ROWS)], recv_f.at[k], f_s.at[k], f_r.at[k], (to, s)
            )
        )
    mixes = along_x(mix_ref, recv_m, m_s, m_r)
    go_z = partner_sum(gos, gop[apart], recv_g, 0)
    partner = arrived(4)
    for k in (5, 7):
        gather[k] = copy_to(partner, partner, ag_s.at[k], ag_r.at[k], (d, chip_peer(s, k - 4)))
    for k in (1, 3):
        arrived(k)
    gosum[...] = full_sum(gos, go_z, gop[here], recv_g, 0).astype(BF16)
    pieces = []
    for k in CHIP_ORDER:
        pieces.append(
            copy_to(
                gosum.at[:, slab(k)], gopart.at[k], gp_s.at[k], gp_r.at[k], (d, chip_peer(s, k))
            )
        )
    for copy in finals:
        copy.wait_recv()
    total = finp[:, here].astype(F32)
    for k in range(1, 8):
        total = total + recv_f[k].astype(F32)
    fin_ref[s] = total.astype(BF16)
    tails = {}
    for k in CHIP_ORDER:
        tails[k] = copy_to(
            fin_ref.at[s], fin_ref.at[s], t_s.at[k], t_r.at[k], (d, chip_peer(s, k))
        )
    passed = [copy_to(fin_ref.at[s], fin_ref.at[s], u_s.at[0], u_r.at[0], mate)]
    for k in (5, 7):
        arrived(k)
    for copy in pieces:
        copy.wait_recv()
    total = gosum[:, slab(0)].astype(F32)
    for k in range(1, 8):
        total = total + gopart[k].astype(F32)
    gomate[0] = total
    pair = copy_to(gomate.at[0], gomate.at[1], gm_s.at[0], gm_r.at[0], mate)
    pair.wait_recv()
    gout_ref[:, slab(0)] = (total + gomate[1]).astype(BF16)
    wholes = []
    for k in CHIP_ORDER:
        wholes.append(
            copy_to(
                gout_ref.at[:, slab(0)],
                gout_ref.at[:, slab(0)],
                gq_s.at[k],
                gq_r.at[k],
                (d, chip_peer(s, k)),
            )
        )
    fetch_mix.wait()
    fetch_far.wait()
    mix_z = partner_sum(mixes, mix_far[...], recv_m, 1)
    for k in CHIP_ORDER:
        tails[k].wait_recv()
        at = fin_ref.at[chip_peer(s, chip_back(k))]
        passed.append(copy_to(at, at, u_s.at[k], u_r.at[k], mate))
    for k in (2, 6):
        arrived(k)
    total = h + full_sum(mixes, mix_z, mix_own[...], recv_m, 1)
    out_ref[...] = total.astype(BF16)
    keep.wait()
    for copy in wholes + passed:
        copy.wait_recv()
    for copy in spare.values():
        copy.wait_recv()
    share.wait_send()
    beside.wait_send()
    go_z.wait_send()
    mix_z.wait_send()
    for copies in (gos, mixes, sides, halves, wholes_e, gather, spare, tails):
        for copy in copies.values():
            copy.wait_send()
    for copy in moves + [swap, pair] + shares + pieces + finals + wholes + passed:
        copy.wait_send()


def widen_kernel(narrow_ref, wide_ref):
    wide_ref[...] = narrow_ref[...].astype(F32)


def widen(narrow):
    block = pl.BlockSpec((1, 256, 3 * FF), lambda e, i: (e, i, 0))
    return pl.pallas_call(
        widen_kernel,
        out_shape=sds((2, D, 3 * FF), F32),
        grid=(2, 4),
        in_specs=[block],
        out_specs=block,
        compiler_params=pltpu.CompilerParams(vmem_limit_bytes=32 << 20),
        name="widen",
    )(narrow)


def sems(count):
    return pltpu.SemaphoreType.DMA((count,))


def params(identity):
    return pltpu.CompilerParams(
        collective_id=identity, has_side_effects=True, vmem_limit_bytes=60 << 20
    )


def angle_tables():
    freqs = np.float32(THETA) ** (
        -(np.arange(HALF, dtype=np.float32) * np.float32(2.0) / np.float32(HD))
    )
    angles = freqs.astype(np.float32)[:, None] * np.arange(LENGTH, dtype=np.float32)[None, :]
    angles = angles.astype(np.float64)
    return np.cos(angles).astype(np.float32), np.sin(angles).astype(np.float32)


def sds(shape, dtype):
    return jax.ShapeDtypeStruct(shape, dtype)


def shards(tokens, w_qkv, w_out, w_router, gain_attn, gain_moe, experts, routes, cotangent):
    cosine, sine = angle_tables()
    cosine, sine = jnp.asarray(cosine), jnp.asarray(sine)
    pack = jnp.concatenate(
        [
            gain_attn.astype(F32)[None],
            gain_moe.astype(F32)[None],
            jnp.zeros((6, ROWS), F32),
            w_router.astype(F32).T,
        ],
        0,
    )
    query_w = w_qkv[:, :D].reshape(ROWS, QH, HD)
    keys_w = w_qkv[:, D:].reshape(ROWS, 2, QH // 2, HD).transpose(0, 2, 1, 3).reshape(ROWS, QH, HD)
    perm = jnp.concatenate([query_w, keys_w], -1).reshape(ROWS, 2 * D).T

    n1, qkv, lse, o_tok, h, n2, gates, gates_t, packs, wouts, cots = pl.pallas_call(
        front_kernel,
        out_shape=(
            sds((LENGTH, D), BF16),
            sds((3 * HD, LENGTH), BF16),
            sds((1, LENGTH), F32),
            sds((D, ROWS), BF16),
            sds((ROWS, D), F32),
            sds((ROWS, D), BF16),
            sds((ROWS, ROWS), F32),
            sds((16, ROWS), F32),
            sds((24, D), F32),
            sds((D, D), BF16),
            sds((D, D), BF16),
        ),
        in_specs=[VMEM, VMEM, VMEM, VMEM, VMEM, VMEM, VMEM, VMEM],
        out_specs=(VMEM,) * 10 + (ANY,),
        scratch_shapes=[
            pltpu.VMEM((ROWS, D), BF16),
            pltpu.VMEM((HD, D), BF16),
            pltpu.VMEM((HD, LENGTH), BF16),
            pltpu.VMEM((LENGTH, HD), BF16),
        ]
        + [sems(8)] * 6
        + [sems(10)] * 2
        + [sems(8)] * 6
        + [sems(16)] * 2
        + [sems(2)] * 2
        + [sems(5)],
        compiler_params=params(1),
        name="front",
    )(tokens, pack, perm, w_out, cotangent, routes.T, cosine, sine)

    dn2, dgate, mix, expert_grads = pl.pallas_call(
        experts_kernel,
        out_shape=(
            sds((ROWS, D), F32),
            sds((ROWS, ROWS), F32),
            sds((D, D), BF16),
            sds((D, 3 * FF), BF16),
        ),
        in_specs=[VMEM] * 2 + [ANY] * 2,
        out_specs=(VMEM,) * 4,
        scratch_shapes=[
            pltpu.VMEM((D, D), BF16),
            pltpu.VMEM((2, D, 3 * FF), BF16),
            pltpu.VMEM((D, D), BF16),
            pltpu.VMEM((16, D), F32),
            pltpu.VMEM((D, D), BF16),
            pltpu.VMEM((16, D), F32),
            pltpu.VMEM((4, ROWS, D), BF16),
            pltpu.VMEM((4, ROWS, D), BF16),
            pltpu.VMEM((8, 16, ROWS), F32),
            pltpu.VMEM((D, 2 * FF), BF16),
            pltpu.VMEM((D, 2 * D), BF16),
            pltpu.VMEM((D, 2 * D), BF16),
            pltpu.VMEM((D, 3 * FF), BF16),
            pltpu.VMEM((D, 3 * FF), BF16),
        ]
        + [sems(10)] * 2
        + [sems(8)] * 2
        + [sems(4)] * 4
        + [sems(8)] * 2
        + [sems(1)] * 2
        + [sems(2)],
        compiler_params=params(2),
        name="experts",
    )(n2, gates_t, cots, experts)

    out, grad_x, grad_out, fin, grad_experts = pl.pallas_call(
        back_kernel,
        out_shape=(
            sds((ROWS, D), BF16),
            sds((ROWS, D), F32),
            sds((ROWS, D), BF16),
            sds((N_SEQ, 160, ROWS), BF16),
            sds((2, D, 3 * FF), BF16),
        ),
        in_specs=[VMEM] * 3 + [ANY] + [VMEM] * 7 + [ANY] + [VMEM] * 6,
        out_specs=(VMEM,) * 4 + (ANY,),
        scratch_shapes=[
            pltpu.VMEM((LENGTH, D), BF16),
            pltpu.VMEM((ROWS, D), BF16),
            pltpu.VMEM((ROWS, D), BF16),
            pltpu.VMEM((2 * D, D), BF16),
            pltpu.VMEM((8, 64, 3 * FF), BF16),
            pltpu.VMEM((8, ROWS, 3 * FF), BF16),
            pltpu.VMEM((8, ROWS, 3 * FF), BF16),
            pltpu.VMEM((ROWS, 3 * FF), BF16),
            pltpu.VMEM((ROWS, 3 * FF), BF16),
            pltpu.VMEM((ROWS, 3 * FF), BF16),
            pltpu.VMEM((8, ROWS, D), BF16),
            pltpu.VMEM((D, D), BF16),
            pltpu.VMEM((8, ROWS, D), BF16),
            pltpu.VMEM((2, ROWS, D), BF16),
            pltpu.VMEM((2, ROWS, D), BF16),
            pltpu.VMEM((ROWS, D), BF16),
            pltpu.VMEM((8, ROWS, ROWS), BF16),
            pltpu.VMEM((2, ROWS, ROWS), F32),
            pltpu.VMEM((D, ROWS), BF16),
            pltpu.VMEM((HD, LENGTH), BF16),
            pltpu.VMEM((LENGTH, HD), BF16),
            pltpu.VMEM((LENGTH, HD), BF16),
            pltpu.VMEM((HD, LENGTH), F32),
            pltpu.VMEM((HD, LENGTH), F32),
            pltpu.VMEM((HD, LENGTH), F32),
            pltpu.VMEM((ROWS, LENGTH), BF16),
            pltpu.VMEM((ROWS, LENGTH), BF16),
            pltpu.VMEM((ROWS, LENGTH), BF16),
            pltpu.VMEM((2 * D, ROWS), BF16),
            pltpu.VMEM((160, D), BF16),
            pltpu.VMEM((8, 160, ROWS), BF16),
        ]
        + [sems(8)] * 2
        + [sems(1)] * 2
        + [sems(8)] * 4
        + [sems(1)] * 2
        + [sems(10)] * 2
        + [sems(9)] * 2
        + [sems(8)] * 4
        + [sems(2)] * 2
        + [sems(3)]
        + [sems(8)] * 2
        + [sems(1)] * 2
        + [sems(8)] * 2
        + [sems(16)] * 2
        + [sems(1)] * 2
        + [sems(16)] * 2
        + [sems(8)] * 6,
        compiler_params=params(3),
        name="back",
    )(
        dn2, dgate, gates, mix, tokens, h, n2, cotangent, packs, wouts, perm,
        n1, qkv, lse, o_tok, cosine, sine, expert_grads,
    )

    grads = fin[:, :128].astype(F32)
    query_g = grads[:, :HD].reshape(D, ROWS).T
    keys_g = (
        grads[:, HD:].reshape(QH // 2, 2, HD, ROWS).transpose(3, 1, 0, 2).reshape(ROWS, D)
    )
    grad_qkv = jnp.concatenate([query_g, keys_g], -1)
    small = jnp.sum(fin[:, 128:].astype(F32), 0)
    return (
        out,
        grad_x,
        grad_qkv,
        grad_out.astype(F32),
        small[:16].T,
        small[17],
        small[16],
        widen(grad_experts),
    )


def solution(mesh):
    placed = (
        P(("dp", "seq"), None),
        P("dp", None),
        P("dp", None),
        P("dp", None),
        P("dp"),
        P("dp"),
        P("dp", None, None),
        P(("dp", "seq"), None),
        P(("dp", "seq"), None),
    )
    return jax.shard_map(
        shards,
        mesh=mesh,
        in_specs=placed,
        out_specs=(
            P(("dp", "seq"), None),
            P(("dp", "seq"), None),
            P("dp", None),
            P("dp", None),
            P("dp", None),
            P("dp"),
            P("dp"),
            P("dp", None, None),
        ),
        check_vma=False,
    )
```

```python
import functools

import jax
import jax.numpy as jnp
import numpy as np
from jax import lax
from jax.experimental import pallas as pl
from jax.experimental.pallas import tpu as pltpu
from jax.sharding import PartitionSpec as P

D = 1024
QH = 16
HD = 64
HALF = 32
FF = 512
N_DP = 8
N_SEQ = 16
ROWS = 128
LENGTH = 2048
QBLOCK = 512

EPSILON = 1e-06
MULT = 0.015625
THETA = 10000.0
NEGATIVE = -1e30
LOG2E = 1.4426950408889634

F32 = jnp.float32
BF16 = jnp.bfloat16
MESH = pl.DeviceIdType.MESH
VMEM = pl.BlockSpec(memory_space=pltpu.VMEM)
ANY = pl.BlockSpec(memory_space=pl.ANY)

DP_ORDER = (1, 2, 6, 3, 7, 4, 5)
CHIP_ORDER = (4, 1, 3, 5, 7, 2, 6)


def dot_nn(a, b):
    return lax.dot_general(a, b, (((1,), (0,)), ((), ())), preferred_element_type=F32)


def dot_nt(a, b):
    return lax.dot_general(a, b, (((1,), (1,)), ((), ())), preferred_element_type=F32)


def dot_tn(a, b):
    return lax.dot_general(a, b, (((0,), (0,)), ((), ())), preferred_element_type=F32)


def dp_peer(d, k):
    return lax.rem(lax.div(d, 2) + k // 2, 4) * 2 + lax.rem(lax.rem(d, 2) + k % 2, 2)


def dp_back(k):
    return 2 * ((4 - k // 2) % 4) + k % 2


def chip_peer(s, k):
    z, y, c = lax.div(s, 8), lax.rem(lax.div(s, 2), 4), lax.rem(s, 2)
    return lax.rem(z + k // 4, 2) * 8 + lax.rem(y + k % 4, 4) * 2 + c


def chip_back(k):
    return 4 * (k // 4) + (4 - k % 4) % 4


def seq_peer(s, k):
    base = chip_peer(s, k // 2)
    c = lax.rem(s, 2)
    return base if k % 2 == 0 else base + 1 - 2 * c


SEQ_ORDER = tuple(2 * c + o for c in (0,) + CHIP_ORDER for o in (0, 1) if 2 * c + o)


def seq_back(k):
    return 2 * chip_back(k // 2) + k % 2


def sibling(s):
    return s + 1 - 2 * lax.rem(s, 2)


def copy_to(src, dst, send, recv, device):
    copy = pltpu.make_async_remote_copy(
        src_ref=src,
        dst_ref=dst,
        send_sem=send,
        recv_sem=recv,
        device_id=device,
        device_id_type=MESH,
    )
    copy.start()
    return copy


def greet(devices):
    barrier = pltpu.get_barrier_semaphore()
    for device in devices:
        pl.semaphore_signal(barrier, inc=1, device_id=device, device_id_type=MESH)
    pl.semaphore_wait(barrier, len(devices))


def rows(start, size):
    return pl.ds(pl.multiple_of(start, size), size)


def front_kernel(
    x_ref, pack_ref, perm_ref, wout_ref, cot_ref, routes_ref, cos_ref, sin_ref,
    n1_ref, qkv_ref, lse_ref, o_ref, h_ref, n2_ref, gates_ref, gates_t_ref, packs_ref, wouts_ref, cots_ref,
    sel_a, sel_b, o_own, k_nat,
    pack_s, pack_r, a_s, a_r, b_s, b_r, n1_s, n1_r, f_s, f_r, w_s, w_r, c_s, c_r, o_s, o_r, l_s, l_r, own_s,
):
    d, s = lax.axis_index("dp"), lax.axis_index("seq")
    core = lax.rem(s, 2)
    mate = (d, sibling(s))
    greet(
        [(dp_peer(d, k), s) for k in DP_ORDER] + [(d, seq_peer(s, k)) for k in SEQ_ORDER]
    )
    lanes = rows(d * ROWS, ROWS)
    small = []
    head_rows = rows(s * ROWS, ROWS)
    mate_rows = rows(sibling(s) * ROWS + HD, HD)
    for k in DP_ORDER:
        to = (dp_peer(d, k), s)
        small.append(copy_to(pack_ref, packs_ref.at[:, lanes], pack_s.at[k], pack_r.at[k], to))
    picks = []
    for k in DP_ORDER:
        to = (dp_peer(d, k), s)
        picks.append(copy_to(perm_ref.at[head_rows], sel_a.at[:, lanes], a_s.at[k], a_r.at[k], to))
        picks.append(copy_to(perm_ref.at[mate_rows], sel_b.at[:, lanes], b_s.at[k], b_r.at[k], to))
    own_a = pltpu.make_async_copy(perm_ref.at[head_rows], sel_a.at[:, lanes], own_s.at[0])
    own_b = pltpu.make_async_copy(perm_ref.at[mate_rows], sel_b.at[:, lanes], own_s.at[1])
    own_a.start()
    own_b.start()
    packs_ref[:, lanes] = pack_ref[...]
    x = x_ref[...].astype(F32)
    r1 = lax.rsqrt(jnp.mean(x * x, -1, keepdims=True) + EPSILON)
    for copy in small:
        copy.wait_recv()
    mine = rows(s * ROWS, ROWS)
    n1_ref[mine] = (x * r1 * packs_ref[0:1, :]).astype(BF16)
    direct = {}
    forwards = {0: copy_to(n1_ref.at[mine], n1_ref.at[mine], f_s.at[0], f_r.at[0], mate)}
    for k in (4, 1, 3):
        direct[k] = copy_to(
            n1_ref.at[mine], n1_ref.at[mine], n1_s.at[k], n1_r.at[k], (d, chip_peer(s, k))
        )
    half = rows(core * 512, 512)
    other = rows(dp_peer(d, 1) * ROWS, ROWS)

    def spread(source, place, send, recv):
        return {
            k: copy_to(source, place(lanes), send.at[k], recv.at[k], (dp_peer(d, k), s))
            for k in (1, 2, 6, 4)
        }

    def pass_on(copies, place, send, recv):
        copies[1].wait_recv()
        for k in (3, 7, 5):
            copies[k] = copy_to(
                place(other), place(other), send.at[k], recv.at[k], (dp_peer(d, k - 1), s)
            )

    def keep(source, place, k):
        copy = pltpu.make_async_copy(source, place(lanes), own_s.at[k])
        copy.start()
        return copy

    out_source, out_place = wout_ref.at[:, half], lambda at: wouts_ref.at[at, half]
    cot_place = lambda at: cots_ref.at[at]
    outs_w = spread(out_source, out_place, w_s, w_r)
    own_w = keep(out_source, out_place, 2)
    direct[4].wait_recv()
    partner = rows(chip_peer(s, 4) * ROWS, ROWS)
    forwards[4] = copy_to(n1_ref.at[partner], n1_ref.at[partner], f_s.at[4], f_r.at[4], mate)
    for k in (5, 7):
        direct[k] = copy_to(
            n1_ref.at[partner],
            n1_ref.at[partner],
            n1_s.at[k],
            n1_r.at[k],
            (d, chip_peer(s, k - 4)),
        )
    cots = spread(cot_ref, cot_place, c_s, c_r)
    own_c = keep(cot_ref, cot_place, 3)
    pass_on(outs_w, out_place, w_s, w_r)
    for copy in picks:
        copy.wait_recv()
    own_a.wait()
    own_b.wait()

    def project(chip):
        block = rows(chip * 256, 256)
        tokens = n1_ref[block]
        cosine = cos_ref[:, block]
        sine = sin_ref[:, block]

        def turn(v):
            a, b = v[:HALF], v[HALF:]
            return jnp.concatenate([a * cosine - b * sine, b * cosine + a * sine], 0)

        pa = dot_nt(sel_a[...], tokens)
        pb = dot_nt(sel_b[...], tokens)
        even = core == 0
        keys = jnp.where(even, pa[HD:], pb)
        values = jnp.where(even, pb, pa[HD:])
        qkv_ref[:, block] = jnp.concatenate([turn(pa[:HD]), turn(keys), values], 0).astype(BF16)

    last = 0
    for k in (4, 1, 3, 5, 7, 2, 6):
        start = chip_peer(s, chip_back(k)) * ROWS
        source = rows(start, ROWS)
        if k != 4:
            direct[k].wait_recv()
            if k in (2, 6):
                direct[8 + k // 6].wait_recv()
            else:
                low = k % 4 == 1
                piece = rows(start if low else start + 64, 64)
                index = k + 1 if low else 7 + (k + 1) // 4
                direct[index] = copy_to(
                    n1_ref.at[piece],
                    n1_ref.at[piece],
                    n1_s.at[index],
                    n1_r.at[index],
                    (d, chip_peer(s, k % 4)),
                )
            forwards[k] = copy_to(
                n1_ref.at[source], n1_ref.at[source], f_s.at[k], f_r.at[k], mate
            )
        forwards[last].wait_recv()
        project(lax.div(chip_peer(s, chip_back(last)), 2))
        last = k
        if k == 3:
            pass_on(cots, cot_place, c_s, c_r)
    forwards[last].wait_recv()
    project(lax.div(chip_peer(s, chip_back(last)), 2))

    k_nat[...] = jnp.transpose(qkv_ref[HD : 2 * HD].astype(F32)).astype(BF16)
    outs = []
    for block in range(LENGTH // QBLOCK):
        begin, end = block * QBLOCK, (block + 1) * QBLOCK
        query = qkv_ref[0:HD, begin:end]
        scores = dot_nn(k_nat[0:end], query)
        low = scores[begin:]
        key = lax.broadcasted_iota(jnp.int32, low.shape, 0)
        pos = lax.broadcasted_iota(jnp.int32, low.shape, 1)
        low = jnp.where(key <= pos, low, NEGATIVE)
        if block:
            scores = jnp.concatenate([scores[:begin], low], 0)
        else:
            scores = low
        top = jnp.max(scores, 0, keepdims=True)
        expo = jnp.exp2((scores - top) * (MULT * LOG2E))
        total = jnp.sum(expo, 0, keepdims=True)
        probs = (expo * (1.0 / total)).astype(BF16)
        lse_ref[:, begin:end] = top * MULT + jnp.log(total)
        o_own[:, begin:end] = dot_nn(qkv_ref[2 * HD :, 0:end], probs).astype(BF16)
    place = rows(s * HD, HD)
    for k in SEQ_ORDER:
        to = seq_peer(s, k)
        outs.append(
            copy_to(
                o_own.at[:, rows(to * ROWS, ROWS)], o_ref.at[place], o_s.at[k], o_r.at[k], (d, to)
            )
        )
    o_ref[place] = o_own[:, mine]
    for k in (2, 6, 4, 3, 7, 5):
        outs_w[k].wait_recv()
    own_w.wait()
    share = copy_to(wouts_ref.at[:, half], wouts_ref.at[:, half], l_s.at[0], l_r.at[0], mate)
    for copy in outs:
        copy.wait_recv()
    share.wait_recv()
    mixed = jnp.transpose(o_ref[...].astype(F32)).astype(BF16)
    h = x + dot_nn(mixed, wouts_ref[...])
    h_ref[...] = h
    r2 = lax.rsqrt(jnp.mean(h * h, -1, keepdims=True) + EPSILON)
    n2 = (h * r2 * packs_ref[1:2, :]).astype(BF16)
    n2_ref[...] = n2
    router = jnp.concatenate(
        [packs_ref[8:24, :], jnp.zeros((ROWS - 16, D), F32)], 0
    ).astype(BF16)
    logits = dot_nt(n2, router)
    label = lax.broadcasted_iota(jnp.int32, (ROWS, ROWS), 0)
    named = jnp.zeros((ROWS, ROWS), F32)
    for j in range(8):
        named = jnp.where(routes_ref[j : j + 1, :] == label, 1.0, named)
    chosen = jnp.transpose(named) > 0.0
    masked = jnp.where(chosen, logits, NEGATIVE)
    expo = jnp.where(chosen, jnp.exp(masked - jnp.max(masked, -1, keepdims=True)), 0.0)
    gates = expo / jnp.sum(expo, -1, keepdims=True)
    gates_ref[...] = gates
    gates_t_ref[...] = jnp.transpose(gates)[0:16]

    for k in (2, 6, 4, 3, 7, 5):
        cots[k].wait_recv()
    own_c.wait()
    for copies in (direct, forwards, outs_w, cots):
        for copy in copies.values():
            copy.wait_send()
    for copy in small + picks + outs:
        copy.wait_send()
    share.wait_send()


def experts_kernel(
    n2_ref, gates_ref, cots_hbm, exp_hbm,
    dn2_ref, dgate_ref, mix_ref, grad_ref,
    cots_ref, exp_ref, n2s, gs, part, dgp, recv_z, recv, recvg, acts, dgus, dys, for_mate, from_mate,
    n_s, n_r, g_s, g_r, z_s, z_r, d_s, d_r, e_s, e_r, m_s, m_r, own_s,
):
    d, s = lax.axis_index("dp"), lax.axis_index("seq")
    core = lax.rem(s, 2)
    mate = (d, sibling(s))
    fetches = [
        pltpu.make_async_copy(exp_hbm, exp_ref, own_s.at[0]),
        pltpu.make_async_copy(cots_hbm, cots_ref, own_s.at[1]),
    ]
    for copy in fetches:
        copy.start()
    greet([(dp_peer(d, k), s) for k in DP_ORDER] + [mate])
    mine = rows(d * ROWS, ROWS)
    other = rows(dp_peer(d, 1) * ROWS, ROWS)
    gathers = {}
    gate_gathers = {}
    for k in DP_ORDER:
        gate_gathers[k] = copy_to(
            gates_ref, gs.at[:, mine], g_s.at[k], g_r.at[k], (dp_peer(d, k), s)
        )
    for k in (1, 2, 6):
        gathers[k] = copy_to(n2_ref, n2s.at[mine], n_s.at[k], n_r.at[k], (dp_peer(d, k), s))
    n2s[mine] = n2_ref[...]
    gs[:, mine] = gates_ref[...]
    gathers[1].wait_recv()
    for k in (3, 7):
        gathers[k] = copy_to(
            n2s.at[other], n2s.at[other], n_s.at[k], n_r.at[k], (dp_peer(d, k - 1), s)
        )
    x = lax.div(d, 2)
    for copy in fetches:
        copy.wait()
    backs = []
    pairs = {}
    sums = {}
    z = lax.rem(d, 2)

    def onward(turn):
        pairs[turn].wait_recv()
        block = rows(dp_peer(d, 2 * turn) * ROWS, ROWS)
        part[block] = (part[block].astype(F32) + recv_z[turn].astype(F32)).astype(BF16)
        if turn:
            sums[turn] = copy_to(
                part.at[block],
                recv.at[turn],
                d_s.at[turn],
                d_r.at[turn],
                (dp_peer(d, 2 * turn), s),
            )

    for step, turn in enumerate((0, 1, 3, 2)):
        if step == 1:
            for k in (2, 6, 3, 7):
                gathers[k].wait_recv()
                start = dp_peer(d, dp_back(k)) * ROWS
                low = k < 4
                piece = rows(start if low else start + 64, 64)
                index = k + 2
                gathers[index] = copy_to(
                    n2s.at[piece],
                    n2s.at[piece],
                    n_s.at[index],
                    n_r.at[index],
                    (dp_peer(d, 2 if low else 6), s),
                )
        for z_off in (0, 1):
            k = 2 * turn + z_off
            if k:
                gate_gathers[dp_back(k)].wait_recv()
            if turn == 2:
                gathers[k].wait_recv()
                gathers[k + 4].wait_recv()
        place = rows(lax.rem(x + turn, 4) * 256, 256)
        tokens = n2s[place]
        cot = cots_ref[place].astype(F32)
        gates = jnp.transpose(jnp.concatenate([gs[:, place], jnp.zeros((ROWS - 16, 256), F32)], 0))
        lane = lax.broadcasted_iota(jnp.int32, gates.shape, 1)
        dn2 = jnp.zeros((256, D), F32)
        mix = jnp.zeros((256, D), F32)
        dgate = jnp.zeros(gates.shape, F32)
        for e in range(2):
            up_w = exp_ref[e, :, 0 : 2 * FF]
            down_w = exp_ref[e, :, 2 * FF :]
            here = lane == 2 * d + e
            gate = jnp.sum(jnp.where(here, gates, 0.0), -1, keepdims=True)
            gu = dot_nn(tokens, up_w)
            g, u = gu[:, :FF], gu[:, FF:]
            sigmoid = 1.0 / (1.0 + jnp.exp(-g))
            silu = g * sigmoid
            act = (silu * u).astype(BF16)
            acts[place, e * FF : (e + 1) * FF] = act
            y = dot_nt(act, down_w)
            dgate = jnp.where(here, jnp.sum(cot * y, -1, keepdims=True), dgate)
            mix = mix + gate * y
            dy = (gate * cot).astype(BF16)
            dys[place, e * D : (e + 1) * D] = dy
            dact = dot_nn(dy, down_w)
            dg = dact * u * (sigmoid * (1.0 + g * (1.0 - sigmoid)))
            du = dact * silu
            dgu = jnp.concatenate([dg, du], 1).astype(BF16)
            dgus[place, e * D : (e + 1) * D] = dgu
            dn2 = dn2 + dot_nt(dgu, up_w)
        mix_ref[place] = mix.astype(BF16)
        part[place] = dn2.astype(BF16)
        dgp[:, place] = jnp.transpose(dgate)[0:16]
        away = rows(dp_peer(d, 2 * turn + 1) * ROWS, ROWS)
        pairs[turn] = copy_to(
            part.at[away], recv_z.at[turn], z_s.at[turn], z_r.at[turn], (dp_peer(d, 1), s)
        )
        for z_off in (0, 1):
            k = 2 * turn + z_off
            if k:
                to = dp_peer(d, k)
                block = rows(to * ROWS, ROWS)
                backs.append(
                    copy_to(dgp.at[:, block], recvg.at[k], e_s.at[k], e_r.at[k], (to, s))
                )
        if step:
            onward((0, 1, 3, 2)[step - 1])

    def grads(e):
        wide = rows(e * D, D)
        return (
            dot_tn(n2s[...], dgus[:, wide]),
            dot_tn(dys[:, wide], acts[:, rows(e * FF, FF)]),
        )

    first, second = grads(1 - core)
    for_mate[:, 0 : 2 * FF] = first.astype(BF16)
    for_mate[:, 2 * FF :] = second.astype(BF16)
    swap = copy_to(for_mate, from_mate, m_s.at[0], m_r.at[0], mate)
    onward(2)
    first, second = grads(core)
    swap.wait_recv()
    grad_ref[:, 0 : 2 * FF] = (first + from_mate[:, 0 : 2 * FF].astype(F32)).astype(BF16)
    grad_ref[:, 2 * FF :] = (second + from_mate[:, 2 * FF :].astype(F32)).astype(BF16)
    for copy in list(sums.values()) + backs:
        copy.wait_recv()
    total = part[mine].astype(F32)
    for k in range(1, 4):
        total = total + recv[k].astype(F32)
    totalg = dgp[:, mine]
    for k in range(1, 8):
        totalg = totalg + recvg[k]
    dn2_ref[...] = total
    dgate_ref[...] = jnp.transpose(
        jnp.concatenate([totalg, jnp.zeros((ROWS - 16, ROWS), F32)], 0)
    )
    for copies in (gathers, gate_gathers, pairs, sums):
        for copy in copies.values():
            copy.wait_send()
    for copy in backs:
        copy.wait_send()
    swap.wait_send()


def back_kernel(
    dn2_ref, dgate_ref, gates_ref, mix_ref, x_ref, h_ref, n2_ref, cot_ref, packs_ref, wouts_ref, perm_ref,
    n1_hbm, qkv_ref, lse_ref, o_ref, cos_ref, sin_ref, ge_ref,
    out_ref, gx_ref, gout_ref, fin_ref, full_ref,
    n1_ref, mix_own, mix_far, perms_ref, half_e, whole_e, stage_e, recv_z, part_e, sum_e, recv_m, gop, recv_g, zout, zin, gosum, gopart, gomate, dot_own, dot_all, k_nat, v_nat, dq_acc, dk_acc, dv_acc, kv_own, kv_mate,
    dp_own, dp_tok, finp, recv_f,
    w_s, w_r, l_s, l_r, b_s, b_r, c_s, c_r, z_s, z_r, ag_s, ag_r, fs_s, fs_r,
    m_s, m_r, go_s, go_r, zz_s, zz_r, own_s, gp_s, gp_r, gm_s, gm_r, gq_s, gq_r, do_s, do_r, kv_s, kv_r, dp_s, dp_r, f_s, f_r, t_s, t_r, u_s, u_r,
):
    d, s = lax.axis_index("dp"), lax.axis_index("seq")
    core = lax.rem(s, 2)
    greet(
        [(dp_peer(d, k), s) for k in DP_ORDER] + [(d, seq_peer(s, k)) for k in SEQ_ORDER]
    )
    here = rows(d * ROWS, ROWS)
    mine = rows(s * ROWS, ROWS)
    head = rows(s * HD, HD)
    mate = (d, sibling(s))

    def slab(k):
        return rows(lax.div(chip_peer(s, k), 2) * ROWS, ROWS)

    lanes = rows(d * ROWS, ROWS)
    side = rows(core * 1024, 1024)

    halves = {}
    wholes_e = {}

    def begin_scatter():
        for base in (4, 0):
            far = lax.div(chip_peer(s, base + 2), 2) * ROWS
            for low in (True, False):
                k = base + (1 if low else 3)
                piece = rows(far if low else far + 64, 64)
                halves[k] = copy_to(
                    ge_ref.at[piece],
                    half_e.at[k],
                    b_s.at[k],
                    b_r.at[k],
                    (d, chip_peer(s, k % 4)),
                )

    def mid_scatter(base):
        for low in (True, False):
            k = base + (1 if low else 3)
            halves[k].wait_recv()
            start = lax.div(chip_peer(s, k), 2) * ROWS
            first, second = rows(start, 64), rows(start + 64, 64)
            added = half_e[k].astype(F32)
            if low:
                stage_e[k, 0:64] = (ge_ref[first].astype(F32) + added).astype(BF16)
                stage_e[k, 64:128] = ge_ref[second]
            else:
                stage_e[k, 0:64] = ge_ref[first]
                stage_e[k, 64:128] = (ge_ref[second].astype(F32) + added).astype(BF16)
            wholes_e[k] = copy_to(
                stage_e.at[k], whole_e.at[k], c_s.at[k], c_r.at[k], (d, chip_peer(s, k % 4))
            )

    def end_scatter(base):
        wholes_e[base + 1].wait_recv()
        wholes_e[base + 3].wait_recv()
        return (
            ge_ref[slab(base)].astype(F32)
            + whole_e[base + 1].astype(F32)
            + whole_e[base + 3].astype(F32)
        )

    fetch_n1 = pltpu.make_async_copy(n1_hbm, n1_ref, own_s.at[0])
    fetch_mix = pltpu.make_async_copy(mix_ref.at[here], mix_own, own_s.at[1])
    fetch_far = pltpu.make_async_copy(
        mix_ref.at[rows(dp_peer(d, 1) * ROWS, ROWS)], mix_far, own_s.at[2]
    )
    fetch_n1.start()
    fetch_far.start()
    fetch_mix.start()

    def along_x(source, landing, send, recv):
        copies = {}
        for k in (3, 7, 5, 2, 6, 4):
            block = rows(dp_peer(d, k) * ROWS, ROWS)
            copies[k] = copy_to(
                source.at[block],
                landing.at[k],
                send.at[k],
                recv.at[k],
                (dp_peer(d, k - k % 2), s),
            )
        return copies

    def partner_sum(copies, own, landing, index):
        for k in (3, 7, 5):
            copies[k].wait_recv()
        total = own.astype(F32)
        for k in (3, 7, 5):
            total = total + landing[k].astype(F32)
        zout[index] = total.astype(BF16)
        return copy_to(
            zout.at[index],
            zin.at[index],
            zz_s.at[index],
            zz_r.at[index],
            (dp_peer(d, 1), s),
        )

    def full_sum(copies, beside, own, landing, index):
        for k in (2, 6, 4):
            copies[k].wait_recv()
        total = own.astype(F32)
        for k in (2, 6, 4):
            total = total + landing[k].astype(F32)
        beside.wait_recv()
        return total + zin[index].astype(F32)

    apart = rows(dp_peer(d, 1) * ROWS, ROWS)
    begin_scatter()
    gates = gates_ref[...]
    dgate = dgate_ref[...]
    inner = jnp.sum(gates * dgate, -1, keepdims=True)
    dlogits = (gates * (dgate - inner)).astype(BF16)
    router = jnp.concatenate(
        [packs_ref[8:24, :], jnp.zeros((ROWS - 16, D), F32)], 0
    ).astype(BF16)
    dn2 = dn2_ref[...] + dot_nn(dlogits, router)
    h = h_ref[...]
    r2 = lax.rsqrt(jnp.mean(h * h, -1, keepdims=True) + EPSILON)
    c = dn2 * packs_ref[1:2, :]
    dh = cot_ref[...].astype(F32) + r2 * c - h * (
        r2 * r2 * r2 * jnp.mean(c * h, -1, keepdims=True)
    )
    da = dh.astype(BF16)
    dot_own[...] = dot_nt(wouts_ref[...], da).astype(BF16)
    moves = []
    for k in SEQ_ORDER:
        to = seq_peer(s, k)
        moves.append(
            copy_to(
                dot_own.at[rows(to * HD, HD)], dot_all.at[:, mine], do_s.at[k], do_r.at[k], (d, to)
            )
        )
    dot_all[:, mine] = dot_own[head]

    sides = {}
    for k in (1, 2, 6, 4):
        sides[k] = copy_to(
            perm_ref.at[side],
            perms_ref.at[side, lanes],
            w_s.at[k],
            w_r.at[k],
            (dp_peer(d, k), s),
        )
    perms_ref[side, lanes] = perm_ref[side]
    gop[...] = dot_nn(o_ref[...], da).astype(BF16)
    router_grad = dot_tn(dlogits, n2_ref[...])[0:16].astype(BF16)
    gain_two = jnp.sum(dn2 * h * r2, 0, keepdims=True)
    k_nat[...] = jnp.transpose(qkv_ref[HD : 2 * HD].astype(F32)).astype(BF16)
    v_nat[...] = jnp.transpose(qkv_ref[2 * HD :].astype(F32)).astype(BF16)
    mid_scatter(4)
    for copy in moves:
        copy.wait_recv()
    blocks = LENGTH // QBLOCK
    for block in reversed(range(blocks)):
        begin, end = block * QBLOCK, (block + 1) * QBLOCK
        query = qkv_ref[0:HD, begin:end]
        grad = dot_all[:, begin:end]
        scores = dot_nn(k_nat[0:end], query)
        probs = jnp.exp2(scores * (MULT * LOG2E) - lse_ref[:, begin:end] * LOG2E)
        low = probs[begin:]
        key = lax.broadcasted_iota(jnp.int32, low.shape, 0)
        pos = lax.broadcasted_iota(jnp.int32, low.shape, 1)
        low = jnp.where(key <= pos, low, 0.0)
        if block:
            probs = jnp.concatenate([probs[:begin], low], 0)
        else:
            probs = low
        pgrad = dot_nn(v_nat[0:end], grad)
        inner = jnp.sum(probs * pgrad, 0, keepdims=True)
        ds = (probs * (pgrad - inner)).astype(BF16)
        dv = dot_nt(grad, probs.astype(BF16))
        dk = dot_nt(query, ds)
        if block == blocks - 1:
            dv_acc[...] = dv
            dk_acc[...] = dk
        else:
            dv_acc[:, 0:end] += dv
            dk_acc[:, 0:end] += dk
        dq_acc[:, begin:end] = dot_nn(qkv_ref[HD : 2 * HD, 0:end], ds)
        if block == 3:
            mid_scatter(0)
            sides[1].wait_recv()
            next_to = perms_ref.at[side, rows(dp_peer(d, 1) * ROWS, ROWS)]
            for k in (3, 7, 5):
                sides[k] = copy_to(
                    next_to, next_to, w_s.at[k], w_r.at[k], (dp_peer(d, k - 1), s)
                )
            gos = along_x(gop, recv_g, go_s, go_r)
    kv_own[0:HD] = (dk_acc[...] * MULT).astype(BF16)
    kv_own[HD:] = dv_acc[...].astype(BF16)
    swap = copy_to(kv_own, kv_mate, kv_s.at[0], kv_r.at[0], mate)
    part_e[...] = end_scatter(4).astype(BF16)
    beside = copy_to(part_e, recv_z, z_s.at[0], z_r.at[0], (d, chip_peer(s, 4)))
    cosine = cos_ref[...]
    sine = sin_ref[...]

    def unturn(v):
        a, b = v[:HALF], v[HALF:]
        return jnp.concatenate([a * cosine + b * sine, b * cosine - a * sine], 0)

    dp_own[0:HD] = unturn((dq_acc[...] * MULT).astype(BF16).astype(F32)).astype(BF16)
    swap.wait_recv()
    both = kv_own[...].astype(F32) + kv_mate[...].astype(F32)
    dp_own[HD:] = jnp.where(core == 0, unturn(both[:HD]), both[HD:]).astype(BF16)
    shares = []
    slot = rows(s * ROWS, ROWS)
    for k in SEQ_ORDER:
        to = seq_peer(s, k)
        shares.append(
            copy_to(
                dp_own.at[:, rows(to * ROWS, ROWS)],
                dp_tok.at[slot],
                dp_s.at[k],
                dp_r.at[k],
                (d, to),
            )
        )
    dp_tok[slot] = dp_own[:, mine]
    fetch_n1.wait()
    finp[0:128, :] = dot_nn(dp_own[...], n1_ref[...]).astype(BF16)

    total = end_scatter(0)
    beside.wait_recv()
    sum_e[...] = (total + recv_z[...].astype(F32)).astype(BF16)
    gather = {}
    spare = {}
    own_e = full_ref.at[core, slab(0)]
    keep = pltpu.make_async_copy(sum_e, own_e, fs_s.at[8])
    keep.start()
    for k in (4, 1, 3):
        gather[k] = copy_to(sum_e, own_e, ag_s.at[k], ag_r.at[k], (d, chip_peer(s, k)))
    spare[0] = copy_to(sum_e, own_e, fs_s.at[0], fs_r.at[0], mate)

    def arrived(k):
        gather[k].wait_recv()
        if k in (2, 6):
            gather[8 + k // 6].wait_recv()
        at = full_ref.at[core, slab(chip_back(k))]
        spare[k] = copy_to(at, at, fs_s.at[k], fs_r.at[k], mate)
        if k % 2:
            low = k % 4 == 1
            start = lax.div(chip_peer(s, chip_back(k)), 2) * ROWS
            piece = full_ref.at[core, rows(start if low else start + 64, 64)]
            index = k + 1 if low else 7 + (k + 1) // 4
            gather[index] = copy_to(
                piece, piece, ag_s.at[index], ag_r.at[index], (d, chip_peer(s, k % 4))
            )
        return at

    for copy in shares:
        copy.wait_recv()
    for k in (2, 6, 4, 3, 7, 5):
        sides[k].wait_recv()
    share = copy_to(perms_ref.at[side], perms_ref.at[side], l_s.at[0], l_r.at[0], mate)
    share.wait_recv()
    dn1 = dot_tn(dp_tok[...], perms_ref[...])
    x = x_ref[...].astype(F32)
    r1 = lax.rsqrt(jnp.mean(x * x, -1, keepdims=True) + EPSILON)
    c = dn1 * packs_ref[0:1, :]
    gx_ref[...] = dh + r1 * c - x * (r1 * r1 * r1 * jnp.mean(c * x, -1, keepdims=True))
    gain_one = jnp.sum(dn1 * x * r1, 0, keepdims=True)
    finp[128:144, :] = router_grad
    finp[144:160, :] = jnp.concatenate([gain_two, gain_one, jnp.zeros((14, D), F32)], 0).astype(
        BF16
    )
    finals = []
    for k in DP_ORDER:
        to = dp_peer(d, k)
        finals.append(
            copy_to(
                finp.at[:, rows(to * ROWS, ROWS)], recv_f.at[k], f_s.at[k], f_r.at[k], (to, s)
            )
        )
    mixes = along_x(mix_ref, recv_m, m_s, m_r)
    partner = arrived(4)
    for k in (5, 7):
        gather[k] = copy_to(partner, partner, ag_s.at[k], ag_r.at[k], (d, chip_peer(s, k - 4)))
    for k in (1, 3):
        arrived(k)
    go_z = partner_sum(gos, gop[apart], recv_g, 0)
    gosum[...] = full_sum(gos, go_z, gop[here], recv_g, 0).astype(BF16)
    pieces = []
    for k in CHIP_ORDER:
        pieces.append(
            copy_to(
                gosum.at[:, slab(k)], gopart.at[k], gp_s.at[k], gp_r.at[k], (d, chip_peer(s, k))
            )
        )
    for copy in finals:
        copy.wait_recv()
    total = finp[:, here].astype(F32)
    for k in range(1, 8):
        total = total + recv_f[k].astype(F32)
    fin_ref[s] = total.astype(BF16)
    tails = {}
    for k in CHIP_ORDER:
        tails[k] = copy_to(
            fin_ref.at[s], fin_ref.at[s], t_s.at[k], t_r.at[k], (d, chip_peer(s, k))
        )
    passed = [copy_to(fin_ref.at[s], fin_ref.at[s], u_s.at[0], u_r.at[0], mate)]
    for k in (5, 7):
        arrived(k)
    for copy in pieces:
        copy.wait_recv()
    total = gosum[:, slab(0)].astype(F32)
    for k in range(1, 8):
        total = total + gopart[k].astype(F32)
    gomate[0] = total
    pair = copy_to(gomate.at[0], gomate.at[1], gm_s.at[0], gm_r.at[0], mate)
    pair.wait_recv()
    gout_ref[:, slab(0)] = (total + gomate[1]).astype(BF16)
    wholes = []
    for k in CHIP_ORDER:
        wholes.append(
            copy_to(
                gout_ref.at[:, slab(0)],
                gout_ref.at[:, slab(0)],
                gq_s.at[k],
                gq_r.at[k],
                (d, chip_peer(s, k)),
            )
        )
    fetch_mix.wait()
    fetch_far.wait()
    mix_z = partner_sum(mixes, mix_far[...], recv_m, 1)
    for k in CHIP_ORDER:
        tails[k].wait_recv()
        at = fin_ref.at[chip_peer(s, chip_back(k))]
        passed.append(copy_to(at, at, u_s.at[k], u_r.at[k], mate))
    for k in (2, 6):
        arrived(k)
    total = h + full_sum(mixes, mix_z, mix_own[...], recv_m, 1)
    out_ref[...] = total.astype(BF16)
    keep.wait()
    for copy in wholes + passed:
        copy.wait_recv()
    for copy in spare.values():
        copy.wait_recv()
    share.wait_send()
    beside.wait_send()
    go_z.wait_send()
    mix_z.wait_send()
    for copies in (gos, mixes, sides, halves, wholes_e, gather, spare, tails):
        for copy in copies.values():
            copy.wait_send()
    for copy in moves + [swap, pair] + shares + pieces + finals + wholes + passed:
        copy.wait_send()


def widen_kernel(narrow_ref, wide_ref):
    wide_ref[...] = narrow_ref[...].astype(F32)


def widen(narrow):
    block = pl.BlockSpec((1, 256, 3 * FF), lambda e, i: (e, i, 0))
    return pl.pallas_call(
        widen_kernel,
        out_shape=sds((2, D, 3 * FF), F32),
        grid=(2, 4),
        in_specs=[block],
        out_specs=block,
        compiler_params=pltpu.CompilerParams(vmem_limit_bytes=32 << 20),
        name="widen",
    )(narrow)


def sems(count):
    return pltpu.SemaphoreType.DMA((count,))


def params(identity):
    return pltpu.CompilerParams(
        collective_id=identity, has_side_effects=True, vmem_limit_bytes=60 << 20
    )


def angle_tables():
    freqs = np.float32(THETA) ** (
        -(np.arange(HALF, dtype=np.float32) * np.float32(2.0) / np.float32(HD))
    )
    angles = freqs.astype(np.float32)[:, None] * np.arange(LENGTH, dtype=np.float32)[None, :]
    angles = angles.astype(np.float64)
    return np.cos(angles).astype(np.float32), np.sin(angles).astype(np.float32)


def sds(shape, dtype):
    return jax.ShapeDtypeStruct(shape, dtype)


def shards(tokens, w_qkv, w_out, w_router, gain_attn, gain_moe, experts, routes, cotangent):
    cosine, sine = angle_tables()
    cosine, sine = jnp.asarray(cosine), jnp.asarray(sine)
    pack = jnp.concatenate(
        [
            gain_attn.astype(F32)[None],
            gain_moe.astype(F32)[None],
            jnp.zeros((6, ROWS), F32),
            w_router.astype(F32).T,
        ],
        0,
    )
    query_w = w_qkv[:, :D].reshape(ROWS, QH, HD)
    keys_w = w_qkv[:, D:].reshape(ROWS, 2, QH // 2, HD).transpose(0, 2, 1, 3).reshape(ROWS, QH, HD)
    perm = jnp.concatenate([query_w, keys_w], -1).reshape(ROWS, 2 * D).T

    n1, qkv, lse, o_tok, h, n2, gates, gates_t, packs, wouts, cots = pl.pallas_call(
        front_kernel,
        out_shape=(
            sds((LENGTH, D), BF16),
            sds((3 * HD, LENGTH), BF16),
            sds((1, LENGTH), F32),
            sds((D, ROWS), BF16),
            sds((ROWS, D), F32),
            sds((ROWS, D), BF16),
            sds((ROWS, ROWS), F32),
            sds((16, ROWS), F32),
            sds((24, D), F32),
            sds((D, D), BF16),
            sds((D, D), BF16),
        ),
        in_specs=[VMEM, VMEM, VMEM, VMEM, VMEM, VMEM, VMEM, VMEM],
        out_specs=(VMEM,) * 10 + (ANY,),
        scratch_shapes=[
            pltpu.VMEM((ROWS, D), BF16),
            pltpu.VMEM((HD, D), BF16),
            pltpu.VMEM((HD, LENGTH), BF16),
            pltpu.VMEM((LENGTH, HD), BF16),
        ]
        + [sems(8)] * 6
        + [sems(10)] * 2
        + [sems(8)] * 6
        + [sems(16)] * 2
        + [sems(2)] * 2
        + [sems(5)],
        compiler_params=params(1),
        name="front",
    )(tokens, pack, perm, w_out, cotangent, routes.T, cosine, sine)

    dn2, dgate, mix, expert_grads = pl.pallas_call(
        experts_kernel,
        out_shape=(
            sds((ROWS, D), F32),
            sds((ROWS, ROWS), F32),
            sds((D, D), BF16),
            sds((D, 3 * FF), BF16),
        ),
        in_specs=[VMEM] * 2 + [ANY] * 2,
        out_specs=(VMEM,) * 4,
        scratch_shapes=[
            pltpu.VMEM((D, D), BF16),
            pltpu.VMEM((2, D, 3 * FF), BF16),
            pltpu.VMEM((D, D), BF16),
            pltpu.VMEM((16, D), F32),
            pltpu.VMEM((D, D), BF16),
            pltpu.VMEM((16, D), F32),
            pltpu.VMEM((4, ROWS, D), BF16),
            pltpu.VMEM((4, ROWS, D), BF16),
            pltpu.VMEM((8, 16, ROWS), F32),
            pltpu.VMEM((D, 2 * FF), BF16),
            pltpu.VMEM((D, 2 * D), BF16),
            pltpu.VMEM((D, 2 * D), BF16),
            pltpu.VMEM((D, 3 * FF), BF16),
            pltpu.VMEM((D, 3 * FF), BF16),
        ]
        + [sems(10)] * 2
        + [sems(8)] * 2
        + [sems(4)] * 4
        + [sems(8)] * 2
        + [sems(1)] * 2
        + [sems(2)],
        compiler_params=params(2),
        name="experts",
    )(n2, gates_t, cots, experts)

    out, grad_x, grad_out, fin, grad_experts = pl.pallas_call(
        back_kernel,
        out_shape=(
            sds((ROWS, D), BF16),
            sds((ROWS, D), F32),
            sds((ROWS, D), BF16),
            sds((N_SEQ, 160, ROWS), BF16),
            sds((2, D, 3 * FF), BF16),
        ),
        in_specs=[VMEM] * 3 + [ANY] + [VMEM] * 7 + [ANY] + [VMEM] * 6,
        out_specs=(VMEM,) * 4 + (ANY,),
        scratch_shapes=[
            pltpu.VMEM((LENGTH, D), BF16),
            pltpu.VMEM((ROWS, D), BF16),
            pltpu.VMEM((ROWS, D), BF16),
            pltpu.VMEM((2 * D, D), BF16),
            pltpu.VMEM((8, 64, 3 * FF), BF16),
            pltpu.VMEM((8, ROWS, 3 * FF), BF16),
            pltpu.VMEM((8, ROWS, 3 * FF), BF16),
            pltpu.VMEM((ROWS, 3 * FF), BF16),
            pltpu.VMEM((ROWS, 3 * FF), BF16),
            pltpu.VMEM((ROWS, 3 * FF), BF16),
            pltpu.VMEM((8, ROWS, D), BF16),
            pltpu.VMEM((D, D), BF16),
            pltpu.VMEM((8, ROWS, D), BF16),
            pltpu.VMEM((2, ROWS, D), BF16),
            pltpu.VMEM((2, ROWS, D), BF16),
            pltpu.VMEM((ROWS, D), BF16),
            pltpu.VMEM((8, ROWS, ROWS), BF16),
            pltpu.VMEM((2, ROWS, ROWS), F32),
            pltpu.VMEM((D, ROWS), BF16),
            pltpu.VMEM((HD, LENGTH), BF16),
            pltpu.VMEM((LENGTH, HD), BF16),
            pltpu.VMEM((LENGTH, HD), BF16),
            pltpu.VMEM((HD, LENGTH), F32),
            pltpu.VMEM((HD, LENGTH), F32),
            pltpu.VMEM((HD, LENGTH), F32),
            pltpu.VMEM((ROWS, LENGTH), BF16),
            pltpu.VMEM((ROWS, LENGTH), BF16),
            pltpu.VMEM((ROWS, LENGTH), BF16),
            pltpu.VMEM((2 * D, ROWS), BF16),
            pltpu.VMEM((160, D), BF16),
            pltpu.VMEM((8, 160, ROWS), BF16),
        ]
        + [sems(8)] * 2
        + [sems(1)] * 2
        + [sems(8)] * 4
        + [sems(1)] * 2
        + [sems(10)] * 2
        + [sems(9)] * 2
        + [sems(8)] * 4
        + [sems(2)] * 2
        + [sems(3)]
        + [sems(8)] * 2
        + [sems(1)] * 2
        + [sems(8)] * 2
        + [sems(16)] * 2
        + [sems(1)] * 2
        + [sems(16)] * 2
        + [sems(8)] * 6,
        compiler_params=params(3),
        name="back",
    )(
        dn2, dgate, gates, mix, tokens, h, n2, cotangent, packs, wouts, perm,
        n1, qkv, lse, o_tok, cosine, sine, expert_grads,
    )

    grads = fin[:, :128].astype(F32)
    query_g = grads[:, :HD].reshape(D, ROWS).T
    keys_g = (
        grads[:, HD:].reshape(QH // 2, 2, HD, ROWS).transpose(3, 1, 0, 2).reshape(ROWS, D)
    )
    grad_qkv = jnp.concatenate([query_g, keys_g], -1)
    small = jnp.sum(fin[:, 128:].astype(F32), 0)
    return (
        out,
        grad_x,
        grad_qkv,
        grad_out.astype(F32),
        small[:16].T,
        small[17],
        small[16],
        widen(grad_experts),
    )


def solution(mesh):
    placed = (
        P(("dp", "seq"), None),
        P("dp", None),
        P("dp", None),
        P("dp", None),
        P("dp"),
        P("dp"),
        P("dp", None, None),
        P(("dp", "seq"), None),
        P(("dp", "seq"), None),
    )
    return jax.shard_map(
        shards,
        mesh=mesh,
        in_specs=placed,
        out_specs=(
            P(("dp", "seq"), None),
            P(("dp", "seq"), None),
            P("dp", None),
            P("dp", None),
            P("dp", None),
            P("dp"),
            P("dp"),
            P("dp", None, None),
        ),
        check_vma=False,
    )
```
